256 devices in a mesh: tm: 16 (over x, z_hi), view: 16 (over z_lo, y, core).
Axes of the slice: x: 4, y: 4, z: 8 (z_hi: 4, z_lo: 2; z = z_hi * 2 + z_lo), core: 2. Of those that a mesh axis runs over, the one named last changes fastest.
Arguments:
- queries: bfloat16 [16, 16, 128, 1280], P('tm', 'view'), may hold values from -32 to 32, as said below
- keys: bfloat16 [16, 16, 128, 1280], P('tm', 'view'), may hold values from -32 to 32
- values: bfloat16 [16, 16, 128, 1280], P('tm', 'view'), may hold values from -6 to 6
- view_mask: int32 [8, 32, 32], replicated, may hold values from 0 to 1, as said below
- frame_times: int32 [8], replicated, may hold values from 0 to 11, as said below
- out_weight: bfloat16 [1280, 1280], replicated, may hold values from -0.15625 to 0.15625
Outputs:
- attended: bfloat16 [16, 16, 128, 1280], P('tm', 'view')
The draws below stay inside these ranges and needn't reach their ends.
Inputs may be any that keep to these rules, and one draw needn't show every extreme that they name: `queries`: in the hidden and the shown draw alike, entries lie within the stated range. 0 or 1; view_mask[f, v, v] = 1 for every frame and view. frame_times[0] = 0; the steps from one frame to the next are four steps of 1, one step of 3 and 2 steps of 2, in any order.
All inputs are finite; a program needn't handle non-finite values.
Results may differ from the reference program's by a relative error of at most 0.014.
Values may be sent and summed in bfloat16 or wider, within the bound.
No kernel may reach another device: no remote copies, remote signals or barrier semaphores. Data moves between devices by JAX's collectives and lax.ppermute only.
A program may use at most 128 MiB of HBM per device.

```python
import jax
import jax.numpy as jnp
from jax import lax

HEADS = 20
DM = 1280
PIX = 128
REACH = 4
FRAMES = 8
GROUPS = 2
VGROUP = 16
VIEWS = 32


def draw_queries(key, part):
    key = jax.random.fold_in(key, 1)
    shape = (GROUPS * FRAMES, VGROUP, PIX, DM)
    return jax.random.normal(key, shape, jnp.float32).astype(jnp.bfloat16)


def draw_keys(key, part):
    key = jax.random.fold_in(key, 2)
    shape = (GROUPS * FRAMES, VGROUP, PIX, DM)
    return jax.random.normal(key, shape, jnp.float32).astype(jnp.bfloat16)


def draw_view_mask(key, part):
    key = jax.random.fold_in(key, 5)
    random_bits = jax.random.randint(key, (FRAMES, VIEWS, VIEWS), 0, 4)
    diagonal = jnp.arange(VIEWS)[:, None] == jnp.arange(VIEWS)[None, :]
    return jnp.where(diagonal[None], 1, (random_bits > 0).astype(jnp.int32)).astype(jnp.int32)


def draw_frame_times(key, part):
    key = jax.random.fold_in(key, 7)
    position = jnp.arange(FRAMES - 1, dtype=jnp.int32)
    base_steps = jnp.where(position < 4, 1, jnp.where(position == 4, 3, 2)).astype(jnp.int32)
    steps = jax.random.permutation(key, base_steps)
    spacing = jnp.concatenate([jnp.zeros((1,), jnp.int32), steps])
    return jnp.cumsum(spacing).astype(jnp.int32)


def block_levels(own_key, extent, shards, low, high):
    level = 1.0
    for dim, shards_of in shards:
        draws = jax.random.uniform(jax.random.fold_in(jax.random.fold_in(own_key, 6), dim), (shards_of,), jnp.float32, low / len(shards), high / len(shards))
        level = level * jnp.repeat(jnp.exp(draws), extent[dim] // shards_of).reshape((-1,) + (1,) * (len(extent) - 1 - dim))
    return level


def gaussian(stream_key, shape, spread, bound, pieces=(), kind=jnp.bfloat16):
    loudness = block_levels(stream_key, shape, pieces, -0.22, 0.18) if pieces else 1.0
    values = jax.random.normal(stream_key, shape, jnp.float32) * spread * loudness
    return jnp.minimum(jnp.maximum(values, -bound), bound).astype(kind)


def setup_inputs(seed: int = 0) -> dict:
    splits = jax.random.split(jax.random.key(seed), 7)
    queries = draw_queries(jax.random.fold_in(splits[6], 71), 0)
    keys = draw_keys(jax.random.fold_in(splits[6], 71), 0)
    values = gaussian(splits[2], (GROUPS * FRAMES, VGROUP, PIX, DM), 1.0, 6.0, ((0, 16), (1, 16)))
    view_mask = draw_view_mask(jax.random.fold_in(splits[6], 71), 0)
    frame_times = draw_frame_times(jax.random.fold_in(splits[6], 71), 0)
    out_weight = gaussian(splits[5], (DM, DM), DM ** -0.5, 0.15625)
    return {"queries": queries, "keys": keys, "values": values, "view_mask": view_mask, "frame_times": frame_times, "out_weight": out_weight}


def to_views(array):
    return array.reshape(GROUPS, FRAMES, VGROUP, PIX, DM).transpose(0, 2, 1, 3, 4).reshape(VIEWS, FRAMES, PIX, DM)


def reference(queries, keys, values, view_mask, frame_times, out_weight):
    queries = to_views(queries)
    keys = to_views(keys)
    values = to_views(values)
    views, frames, cells, model_width = queries.shape
    head_size = model_width // HEADS
    scale = head_size ** -0.5

    def attend_block(block_id):
        view_id = block_id // frames
        frame_id = block_id % frames
        query_rows = queries[view_id, frame_id].astype(jnp.float32).reshape(cells, HEADS, head_size)
        key_all = jnp.concatenate([keys[:, frame_id], keys[view_id]], 0).astype(jnp.float32).reshape(-1, HEADS, head_size)
        value_all = jnp.concatenate([values[:, frame_id], values[view_id]], 0).astype(jnp.float32).reshape(-1, HEADS, head_size)
        view_ok = view_mask[frame_id, view_id] == 1
        clock = frame_times - frame_times[frame_id]
        time_ok = (jnp.arange(frames, dtype=jnp.int32) != frame_id) & (jnp.abs(clock) <= REACH)
        allowed = jnp.repeat(jnp.concatenate([view_ok, time_ok]), cells)
        scores = jnp.einsum('phd,khd->hpk', query_rows, key_all) * scale
        row_max = jnp.max(jnp.where(allowed, scores, -jnp.inf), -1, keepdims=True)
        weights = jnp.where(allowed, jnp.exp(scores - row_max), 0.0)
        row_sum = jnp.sum(weights, -1)
        rounded = lax.optimization_barrier(weights.astype(jnp.bfloat16)).astype(jnp.float32)
        summed = jnp.einsum('hpk,khd->hpd', rounded, value_all)
        heads_out = (summed / row_sum[:, :, None]).transpose(1, 0, 2).reshape(cells, model_width).astype(jnp.bfloat16)
        return jnp.dot(heads_out, out_weight, preferred_element_type=jnp.float32).astype(jnp.bfloat16)

    result = lax.map(attend_block, jnp.arange(views * frames, dtype=jnp.int32))
    result = result.reshape(GROUPS, VGROUP, FRAMES, PIX, DM).transpose(0, 2, 1, 3, 4)
    return result.reshape(GROUPS * FRAMES, VGROUP, PIX, DM)
```

```python
import jax
import jax.numpy as jnp
from jax import lax
from jax.experimental import pallas as pl
from jax.experimental.pallas import tpu as pltpu
from jax.sharding import Mesh, PartitionSpec as P

HEADS = 20
REACH = 4
FRAMES = 8
HEAD = 64
CELLS = 128
MAIN = 16
RING = 4
NEG = -(2.0**30)
LOG2E = 1.4426950408889634
RATE = HEAD**-0.5 * LOG2E
TILE = 256
CHUNK = 512
Z_ROWS = 960
X_ROWS = 448
T_ROWS = 208
O_ROWS = 144
F32 = jnp.float32
BF16 = jnp.bfloat16
VMEM = pl.BlockSpec(memory_space=pltpu.VMEM)
SMEM = pl.BlockSpec(memory_space=pltpu.SMEM)


def lanes(shape):
    return lax.broadcasted_iota(jnp.int32, shape, len(shape) - 1)


def rows_of(shape):
    return lax.broadcasted_iota(jnp.int32, shape, len(shape) - 2)


def swap_halves(x):
    return pltpu.roll(x, HEAD, 1)


def params(mib):
    return pltpu.CompilerParams(vmem_limit_bytes=mib * 1024 * 1024)


def pack_kernel(q_ref, k_ref, v_ref, view_ref, ring_ref, z0, z1, z2, z3, parts):
    frame = lax.axis_index("f")
    half = frame // 4
    place = frame % 4

    def pair(a_ref, a, b_ref, b):
        left = a_ref[:, a * HEAD : (a + 1) * HEAD]
        right = b_ref[:, b * HEAD : (b + 1) * HEAD]
        return jnp.concatenate([left, right], axis=1)

    for t in range(MAIN):
        view_ref[t, 0:CELLS] = pair(k_ref, t, v_ref, t)
        view_ref[t, CELLS : 2 * CELLS] = pair(q_ref, t, q_ref, MAIN + t % RING)
    for y in range(RING):
        ring_ref[y] = pair(k_ref, MAIN + y, v_ref, MAIN + y)
    for j in range(4):
        base = 5 * j
        first = [pair(k_ref, base, v_ref, base), pair(k_ref, base + 1, v_ref, base + 1)]
        first.append(pair(q_ref, base, q_ref, base + 1))
        second = [pair(k_ref, base + 2, v_ref, base + 2), pair(k_ref, base + 3, v_ref, base + 3)]
        second.append(pair(q_ref, base + 2, q_ref, base + 3))
        for i in range(3):
            a, b = first[i].astype(F32), second[i].astype(F32)
            parts[j, i * CELLS : (i + 1) * CELLS] = jnp.where(half == 0, a, b).astype(BF16)
            parts[j, 576 + i * CELLS : 576 + (i + 1) * CELLS] = jnp.where(half == 0, b, a).astype(BF16)
        parts[j, 384:512] = pair(k_ref, base + 4, v_ref, base + 4)
        last = q_ref[:, (base + 4) * HEAD : (base + 5) * HEAD]
        parts[j, 512:576] = jnp.concatenate([last[0:64], last[64:128]], axis=1)
    for k, out in enumerate((z0, z1, z2, z3)):
        out[...] = parts[place ^ k]


def pack(q, k, v):
    block = jax.ShapeDtypeStruct((Z_ROWS, CELLS), BF16)
    return pl.pallas_call(
        pack_kernel,
        out_shape=[
            jax.ShapeDtypeStruct((MAIN, 2 * CELLS, CELLS), BF16),
            jax.ShapeDtypeStruct((RING, CELLS, CELLS), BF16),
            block,
            block,
            block,
            block,
        ],
        in_specs=[VMEM] * 3,
        out_specs=[VMEM] * 6,
        scratch_shapes=[pltpu.VMEM((4, Z_ROWS, CELLS), BF16)],
        compiler_params=params(32),
        name="pack",
    )(q, k, v)


def score_tile(q, key_ref, score_ref, count):
    best = None
    for start in range(0, count, CHUNK):
        s = lax.dot_general(
            q, key_ref[start : start + CHUNK], (((1,), (1,)), ((), ())), preferred_element_type=F32
        )
        score_ref[:, start : start + CHUNK] = s
        for lane in range(0, CHUNK, 128):
            part = s[:, lane : lane + 128]
            best = part if best is None else jnp.maximum(best, part)
    return jnp.max(best, axis=1, keepdims=True)


def weigh_tile(score_ref, row_max, value_ref, count):
    total = None
    for start in range(0, count, CHUNK):
        s = score_ref[:, start : start + CHUNK]
        w = jnp.exp2((s - row_max) * RATE).astype(BF16)
        part = jnp.dot(w, value_ref[start : start + CHUNK], preferred_element_type=F32)
        total = part if total is None else total + part
    return total


def split3(x):
    high = x.astype(BF16).astype(F32)
    middle = (x - high).astype(BF16).astype(F32)
    low = (x - high - middle).astype(BF16).astype(F32)
    return [high, middle, low]


def level_rows(levels, lane):
    columns = [part for level in levels for part in split3(level)]
    table = jnp.zeros_like(columns[0])
    for i, column in enumerate(columns):
        table = jnp.where(lane == i, column, table)
    return table


def keys_with_mask(kv, mask_row, lane):
    return jnp.where(lane < HEAD, kv, mask_row).astype(BF16)


def view_kernel(own_ref, other_ref, ring_ref, mask_ref, out_ref, key_s, value_s, rkey_s, rvalue_s, s_a, s_b, r_s):
    frame = lax.axis_index("f")
    core = lax.axis_index("c")
    y = lax.axis_index("y")
    ring = lax.axis_index("g") * 2 + lax.axis_index("zl")
    lane = lanes((CELLS, CELLS))

    seen = mask_ref[frame].astype(F32)
    b32, u32 = rows_of((32, 32)), lanes((32, 32))
    key_view = jnp.where(b32 < 16, 2 * b32 + core, 2 * (b32 - 16) + 1 - core)
    pick = (u32 == key_view).astype(F32)
    v128, l128 = rows_of((32, 128)), lanes((32, 128))
    query_pick = ((l128 >= HEAD) & (l128 < HEAD + 16) & (v128 == 2 * (l128 - HEAD) + core)).astype(F32)
    by_key = lax.dot_general(pick, seen, (((1,), (1,)), ((), ())), preferred_element_type=F32)
    allowed = jnp.dot(by_key, query_pick, preferred_element_type=F32)
    bias = jnp.where((l128 >= HEAD) & (l128 < HEAD + 16) & (allowed < 0.5), NEG, 0.0)
    r8, ru8 = rows_of((8, 32)), lanes((8, 32))
    ring_pick = (ru8 == ring * 8 + r8).astype(F32)
    by_ring = lax.dot_general(ring_pick, seen, (((1,), (1,)), ((), ())), preferred_element_type=F32)
    ring_allowed = jnp.dot(by_ring, query_pick, preferred_element_type=F32)
    l8 = lanes((8, 128))
    ring_bias = jnp.where((l8 >= HEAD) & (l8 < HEAD + 16) & (ring_allowed < 0.5), NEG, 0.0)

    for b in range(32):
        kv = (own_ref[b, 0:CELLS] if b < 16 else other_ref[b - 16, 0:CELLS]).astype(F32)
        rows = slice(b * CELLS, (b + 1) * CELLS)
        key_s[rows] = keys_with_mask(kv, bias[b : b + 1], lane)
        value_s[rows] = jnp.where(lane < HEAD, swap_halves(kv), 1.0).astype(BF16)
    for b in range(8):
        kv = ring_ref[b, y].astype(F32)
        rows = slice(b * CELLS, (b + 1) * CELLS)
        rkey_s[rows] = keys_with_mask(kv, ring_bias[b : b + 1], lane)
        rvalue_s[rows] = jnp.where(lane < HEAD, 1.0, kv).astype(BF16)

    def queries(j):
        qq = own_ref[j, CELLS : 2 * CELLS].astype(F32)
        hot = (lane == HEAD + j).astype(F32)
        main = jnp.where(lane < HEAD, qq, hot).astype(BF16)
        ring_q = jnp.where(lane < HEAD, swap_halves(qq), hot).astype(BF16)
        return main, ring_q

    def tile(i):
        a, b = queries(2 * i), queries(2 * i + 1)
        return jnp.concatenate([a[0], b[0]], axis=0), jnp.concatenate([a[1], b[1]], axis=0)

    wide = lanes((TILE, CELLS))

    def finish(i, score_ref, row_max, ring_q):
        ring_max = score_tile(ring_q, rkey_s, r_s, 1024)
        main = weigh_tile(score_ref, row_max, value_s, 4096)
        part = weigh_tile(r_s, ring_max, rvalue_s, 1024)
        main_sum = swap_halves(main)
        heads = jnp.where(wide < HEAD, main / main_sum, part / swap_halves(part))
        main_level = row_max * RATE + jnp.log2(jnp.where(wide < HEAD, main_sum, 1.0))
        ring_level = ring_max * RATE + jnp.log2(jnp.where(wide < HEAD, part, 1.0))
        table = level_rows([main_level, ring_level], wide)
        for n in range(2):
            rows = slice(n * CELLS, (n + 1) * CELLS)
            out_ref[2 * i + n, 0:CELLS] = heads[rows].astype(BF16)
            out_ref[2 * i + n, CELLS:O_ROWS] = table[rows].T[0:16].astype(BF16)

    q0, rq0 = tile(0)
    m0 = score_tile(q0, key_s, s_a, 4096)

    def body(step, carry):
        m_a, rq_a = carry
        q_b, rq_b = tile(2 * step + 1)
        m_b = score_tile(q_b, key_s, s_b, 4096)
        finish(2 * step, s_a, m_a, rq_a)
        q_a, rq_next = tile(jnp.minimum(2 * step + 2, 7))
        m_next = score_tile(q_a, key_s, s_a, 4096)
        finish(2 * step + 1, s_b, m_b, rq_b)
        return m_next, rq_next

    lax.fori_loop(0, 4, body, (m0, rq0))


def view_attention(own, other, ring, view_mask):
    return pl.pallas_call(
        view_kernel,
        out_shape=jax.ShapeDtypeStruct((MAIN, O_ROWS, CELLS), BF16),
        in_specs=[VMEM] * 4,
        out_specs=VMEM,
        scratch_shapes=[
            pltpu.VMEM((4096, CELLS), BF16),
            pltpu.VMEM((4096, CELLS), BF16),
            pltpu.VMEM((1024, CELLS), BF16),
            pltpu.VMEM((1024, CELLS), BF16),
            pltpu.VMEM((TILE, 4096), F32),
            pltpu.VMEM((TILE, 4096), F32),
            pltpu.VMEM((TILE, 1024), F32),
        ],
        compiler_params=params(48),
        cost_estimate=pl.CostEstimate(flops=2700000000, bytes_accessed=4000000, transcendentals=11000000),
        name="view_attention",
    )(own, other, ring, view_mask)


def time_kernel(z0, z1, z2, z3, x_ref, times_ref, o0, o1, o2, o3, o4, o5, o6, o7, key_s, value_s, q_s, s_ref):
    frame = lax.axis_index("f")
    lane = lanes((CELLS, CELLS))
    own = (z0, z1, z2, z3)
    outs = (o0, o1, o2, o3, o4, o5, o6, o7)

    l8, r8 = lanes((8, 128)), rows_of((8, 128))
    query_time = jnp.zeros((8, 128), jnp.int32)
    key_time = jnp.zeros((8, 128), jnp.int32)
    for k in range(FRAMES):
        now = times_ref[frame ^ k]
        query_time = jnp.where(l8 == HEAD + k, now, query_time)
        key_time = jnp.where(r8 == k, now, key_time)
    near = (jnp.abs(query_time - key_time) <= REACH) & (l8 - HEAD != r8)
    bias = jnp.where((l8 >= HEAD) & (l8 < HEAD + 8) & jnp.logical_not(near), NEG, 0.0)

    for head in range(3):
        slots = 8 if head < 2 else 4
        for k in range(slots):
            if head == 2:
                kv = own[k][384:512]
            elif k < 4:
                kv = own[k][head * CELLS : (head + 1) * CELLS]
            else:
                kv = x_ref[k - 4, 64 + head * CELLS : 64 + (head + 1) * CELLS]
            kv = kv.astype(F32)
            rows = slice(k * CELLS, (k + 1) * CELLS)
            key_s[head, rows] = keys_with_mask(kv, bias[k : k + 1], lane)
            value_s[head, rows] = jnp.where(lane < HEAD, swap_halves(kv), 1.0).astype(BF16)
        for k in range(8):
            hot = jnp.where(lane == HEAD + k, 1.0, 0.0)
            rows = slice(k * CELLS, (k + 1) * CELLS)
            if head < 2:
                qq = (own[k][256:384] if k < 4 else x_ref[k - 4, 320:448]).astype(F32)
                qq = swap_halves(qq) if head == 1 else qq
            else:
                packed = (own[k][512:576] if k < 4 else x_ref[k - 4, 0:64]).astype(F32)
                qq = jnp.concatenate([packed, swap_halves(packed)], axis=0)
            q_s[head, rows] = jnp.where(lane < HEAD, qq, hot).astype(BF16)

    wide = lanes((TILE, CELLS))
    for i in range(4):
        heads, levels = [], []
        for head in range(3):
            count = 1024 if head < 2 else 512
            q = q_s[head, i * TILE : (i + 1) * TILE]
            score = s_ref.at[(3 * i + head) % 2]
            row_max = score_tile(q, key_s.at[head], score, count)
            total = weigh_tile(score, row_max, value_s.at[head], count)
            sums = swap_halves(total)
            heads.append(jnp.where(wide < HEAD, total / sums, 0.0))
            levels.append(row_max * RATE + jnp.log2(jnp.where(wide < HEAD, sums, 1.0)))
        both = heads[0] + swap_halves(heads[1])
        table = level_rows(levels, wide)
        for n in range(2):
            rows = slice(n * CELLS, (n + 1) * CELLS)
            out = outs[2 * i + n]
            out[0:128] = both[rows].astype(BF16)
            last = heads[2][rows]
            out[128:192] = (last[0:64] + swap_halves(last[64:128])).astype(BF16)
            out[192:208] = table[rows].T[0:16].astype(BF16)


def time_attention(own, crossed, frame_times):
    return pl.pallas_call(
        time_kernel,
        out_shape=[jax.ShapeDtypeStruct((T_ROWS, CELLS), BF16)] * 8,
        in_specs=[VMEM] * 5 + [SMEM],
        out_specs=[VMEM] * 8,
        scratch_shapes=[
            pltpu.VMEM((3, 1024, CELLS), BF16),
            pltpu.VMEM((3, 1024, CELLS), BF16),
            pltpu.VMEM((3, 1024, CELLS), BF16),
            pltpu.VMEM((2, TILE, 1024), F32),
        ],
        compiler_params=params(40),
        cost_estimate=pl.CostEstimate(flops=700000000, bytes_accessed=2000000, transcendentals=2700000),
        name="time_attention",
    )(*own, crossed, frame_times)


def join_kernel(view_ref, t0, t1, t2, t3, t4, t5, t6, t7, weight_ref, out_ref, times, heads_s):
    frame = lax.axis_index("f")
    for k, piece in enumerate((t0, t1, t2, t3, t4, t5, t6, t7)):
        times[frame ^ k] = piece[...]

    def level(block, i):
        parts = block[3 * i : 3 * i + 3].astype(F32)
        return parts[0:1] + parts[1:2] + parts[2:3]

    sources = []
    view_levels = [view_ref[t, CELLS:O_ROWS].astype(F32) for t in range(MAIN)]
    time_levels = [times[d, 192:208].astype(F32) for d in range(8)]
    for head in range(HEADS):
        found = []
        if head < MAIN:
            found.append((("view", head, 0), level(view_levels[head], 0)))
        else:
            for ring in range(4):
                t = 4 * ring + head - MAIN
                found.append((("view", t, 1), level(view_levels[t], 1)))
        group, i = head // 5, head % 5
        if i < 4:
            d = (i // 2) * 4 + group
            found.append((("time", d, i % 2), level(time_levels[d], i % 2)))
        else:
            for side in range(2):
                d = side * 4 + group
                found.append((("time", d, 2), level(time_levels[d], 2)))
        sources.append(found)

    columns = []
    for found in sources:
        best = found[0][1]
        for _, value in found[1:]:
            best = jnp.maximum(best, value)
        powers = [jnp.exp2(value - best) for _, value in found]
        total = powers[0]
        for power in powers[1:]:
            total = total + power
        columns.extend(power / total for power in powers)
    columns.extend([jnp.zeros((128 - len(columns), CELLS), F32)])
    table = jnp.concatenate(columns, axis=0).T

    def block(kind, at, i):
        if kind == "view":
            return view_ref[at, 0:CELLS, i * HEAD : (i + 1) * HEAD].astype(F32)
        if i < 2:
            return times[at, 0:CELLS, i * HEAD : (i + 1) * HEAD].astype(F32)
        packed = times[at, 128:192].astype(F32)
        return jnp.concatenate([packed[:, 0:HEAD], packed[:, HEAD:128]], axis=0)

    position = 0
    for head, found in enumerate(sources):
        total = None
        for which, _ in found:
            part = block(*which) * table[:, position : position + 1]
            total = part if total is None else total + part
            position += 1
        heads_s[:, head * HEAD : (head + 1) * HEAD] = total.astype(BF16)
    out_ref[...] = jnp.dot(heads_s[...], weight_ref[...], preferred_element_type=F32).astype(BF16)


def join(view_out, pieces, out_weight):
    return pl.pallas_call(
        join_kernel,
        out_shape=jax.ShapeDtypeStruct((CELLS, HEADS * HEAD), BF16),
        in_specs=[VMEM] * 10,
        out_specs=VMEM,
        scratch_shapes=[pltpu.VMEM((8, T_ROWS, CELLS), BF16), pltpu.VMEM((CELLS, HEADS * HEAD), BF16)],
        compiler_params=params(32),
        name="join",
    )(view_out, *pieces, out_weight)


def across(array, k):
    return lax.ppermute(array, "f", [(i, i ^ k) for i in range(FRAMES)])


def after(array, *others):
    return lax.optimization_barrier((array,) + others)[0]


def local(queries, keys, values, view_mask, frame_times, out_weight):
    model = queries.shape[3]
    q, k, v = (a.reshape(CELLS, model) for a in (queries, keys, values))
    to_view, to_ring, *z = pack(q, k, v)
    ring = lax.all_gather(to_ring, ("y", "c"), axis=0, tiled=False)
    z = [z[0]] + [across(z[i], i) for i in (1, 2, 3)]
    own = lax.all_to_all(to_view, ("g", "zl", "y"), 0, 0)
    other = lax.ppermute(own, "c", [(0, 1), (1, 0)])
    crossed = across(jnp.stack([a[512:960] for a in z]), 4)
    view_out = view_attention(own, other, ring, view_mask)
    pieces = time_attention(z, crossed, frame_times)
    pieces = [pieces[0]] + [across(pieces[i], i) for i in range(1, 8)]
    view_back = lax.all_to_all(view_out, ("g", "zl", "y"), 0, 0)
    result = join(view_back, pieces, out_weight)
    return result.reshape(1, 1, CELLS, model)


def solution(mesh):
    fine = Mesh(mesh.devices.reshape(2, 8, 2, 4, 2), ("g", "f", "zl", "y", "c"))
    blocks = P(("g", "f"), ("zl", "y", "c"), None, None)
    return jax.shard_map(
        local,
        mesh=fine,
        in_specs=(blocks, blocks, blocks, P(), P(), P()),
        out_specs=blocks,
        check_vma=False,
    )
```

```python
import jax
import jax.numpy as jnp
from jax import lax
from jax.experimental import pallas as pl
from jax.experimental.pallas import tpu as pltpu
from jax.sharding import Mesh, PartitionSpec as P

HEADS = 20
REACH = 4
FRAMES = 8
HEAD = 64
CELLS = 128
MAIN = 16
RING = 4
NEG = -(2.0**30)
LOG2E = 1.4426950408889634
RATE = HEAD**-0.5 * LOG2E
TILE = 256
CHUNK = 512
Z_ROWS = 960
X_ROWS = 640
T_ROWS = 336
O_ROWS = 144
F32 = jnp.float32
BF16 = jnp.bfloat16
ANY = pl.BlockSpec(memory_space=pl.ANY)
VMEM = pl.BlockSpec(memory_space=pltpu.VMEM)
SMEM = pl.BlockSpec(memory_space=pltpu.SMEM)


def lanes(shape):
    return lax.broadcasted_iota(jnp.int32, shape, len(shape) - 1)


def rows_of(shape):
    return lax.broadcasted_iota(jnp.int32, shape, len(shape) - 2)


def swap_halves(x):
    return pltpu.roll(x, HEAD, 1)


def params(mib):
    return pltpu.CompilerParams(vmem_limit_bytes=mib * 1024 * 1024)


def turned(index, k):
    return (index, index + 1 - 2 * (index % 2), (index + 2) % 4, 3 - index)[k]


def copy_all(moves, sems):
    copies = [pltpu.make_async_copy(source, target, sems.at[i]) for i, (source, target) in enumerate(moves)]
    for copy in copies:
        copy.start()
    for copy in copies:
        copy.wait()


def pair(a_ref, a, b_ref, b):
    left = a_ref[:, a * HEAD : (a + 1) * HEAD]
    right = b_ref[:, b * HEAD : (b + 1) * HEAD]
    return jnp.concatenate([left, right], axis=1)


def pack_time_kernel(q_hbm, k_hbm, v_hbm, z0, z1, z2, z3, ring_ref, q_ref, k_ref, v_ref, sems, parts):
    place = lax.axis_index("f") % 4
    copy_all([(k_hbm, k_ref), (v_hbm, v_ref), (q_hbm, q_ref)], sems)
    for j in range(4):
        base = 5 * j
        for i in range(5):
            parts[j, i * CELLS : (i + 1) * CELLS] = pair(k_ref, base + i, v_ref, base + i)
        for i in range(2):
            rows = slice((5 + i) * CELLS, (6 + i) * CELLS)
            parts[j, rows] = pair(q_ref, base + 2 * i, q_ref, base + 2 * i + 1)
        last = q_ref[:, (base + 4) * HEAD : (base + 5) * HEAD]
        parts[j, 896:960] = jnp.concatenate([last[0:64], last[64:128]], axis=1)
    keep = pltpu.make_async_copy(parts.at[place], z0, sems.at[3])
    keep.start()
    for k, out in enumerate((z1, z2, z3)):
        out[...] = parts[turned(place, k + 1)]
    for y in range(RING):
        ring_ref[y] = pair(k_ref, MAIN + y, v_ref, MAIN + y)
    keep.wait()


def in_hbm(x):
    return pltpu.with_memory_space_constraint(x, pltpu.HBM)


def pack_time(q, k, v):
    block = jax.ShapeDtypeStruct((Z_ROWS, CELLS), BF16)
    whole = jax.ShapeDtypeStruct((CELLS, HEADS * HEAD), BF16)
    return pl.pallas_call(
        pack_time_kernel,
        out_shape=[pltpu.HBM((Z_ROWS, CELLS), BF16)] + [block] * 3 + [jax.ShapeDtypeStruct((RING, CELLS, CELLS), BF16)] + [whole] * 3,
        in_specs=[ANY] * 3,
        out_specs=[ANY] + [VMEM] * 7,
        scratch_shapes=[pltpu.SemaphoreType.DMA((4,)), pltpu.VMEM((4, Z_ROWS, CELLS), BF16)],
        compiler_params=params(16),
        name="pack_time",
    )(in_hbm(q), in_hbm(k), in_hbm(v))


def pack_view_kernel(q_ref, k_ref, v_ref, view_ref):
    for t in range(MAIN):
        view_ref[t, 0:CELLS] = pair(k_ref, t, v_ref, t)
        view_ref[t, CELLS : 2 * CELLS] = pair(q_ref, t, q_ref, MAIN + t % RING)


def pack_view(q, k, v):
    return pl.pallas_call(
        pack_view_kernel,
        out_shape=jax.ShapeDtypeStruct((MAIN, 2 * CELLS, CELLS), BF16),
        in_specs=[VMEM] * 3,
        out_specs=VMEM,
        compiler_params=params(16),
        cost_estimate=pl.CostEstimate(flops=4000000000, bytes_accessed=2000000, transcendentals=0),
        name="pack_view",
    )(q, k, v)


def stack_kernel(z0, z1, z2, z3, own_ref, ring_ref, sibling_ref, out_ref, kv_ref, r0, r1, r2, r3, sems):
    y = lax.axis_index("y")
    moves = [(piece.at[pl.ds(0, X_ROWS)], out_ref.at[k]) for k, piece in enumerate((z0, z1, z2, z3))]
    moves.append((own_ref.at[:, pl.ds(0, CELLS)], kv_ref))
    for k, out in enumerate((r0, r1, r2, r3)):
        moves.append((ring_ref.at[turned(y, k)], out.at[0]))
        moves.append((sibling_ref.at[turned(y, k)], out.at[1]))
    copy_all(moves, sems)


def stack(z, own, ring, other):
    block = jax.ShapeDtypeStruct((2, CELLS, CELLS), BF16)
    return pl.pallas_call(
        stack_kernel,
        out_shape=[
            jax.ShapeDtypeStruct((4, X_ROWS, CELLS), BF16),
            jax.ShapeDtypeStruct((MAIN, CELLS, CELLS), BF16),
        ]
        + [block] * 4,
        in_specs=[ANY] * 7,
        out_specs=[ANY] * 6,
        scratch_shapes=[pltpu.SemaphoreType.DMA((13,))],
        compiler_params=params(4),
        name="stack",
    )(*z, own, ring, other)


def score_tile(q, key_ref, score_ref, count):
    best = None
    for start in range(0, count, CHUNK):
        s = lax.dot_general(
            q, key_ref[start : start + CHUNK], (((1,), (1,)), ((), ())), preferred_element_type=F32
        )
        score_ref[:, start : start + CHUNK] = s
        for lane in range(0, CHUNK, 128):
            part = s[:, lane : lane + 128]
            best = part if best is None else jnp.maximum(best, part)
    return jnp.max(best, axis=1, keepdims=True)


def weigh_tile(score_ref, row_max, value_ref, count):
    total = None
    for start in range(0, count, CHUNK):
        s = score_ref[:, start : start + CHUNK]
        w = jnp.exp2((s - row_max) * RATE).astype(BF16)
        part = jnp.dot(w, value_ref[start : start + CHUNK], preferred_element_type=F32)
        total = part if total is None else total + part
    return total


def split3(x):
    high = x.astype(BF16).astype(F32)
    middle = (x - high).astype(BF16).astype(F32)
    low = (x - high - middle).astype(BF16).astype(F32)
    return [high, middle, low]


def level_rows(levels, lane, at=0):
    columns = [part for level in levels for part in split3(level)]
    table = jnp.zeros_like(columns[0])
    for i, column in enumerate(columns):
        table = jnp.where(lane == at + i, column, table)
    return table


def row(x):
    return x.astype(BF16)


def seen_bias(mask_ref, key_view, count):
    core = lax.axis_index("c")
    seen = mask_ref[lax.axis_index("f")].astype(F32)
    pick = (lanes((count, 32)) == key_view).astype(F32)
    view, column = rows_of((32, 128)), lanes((32, 128)) - HEAD
    query_pick = ((column >= 0) & (column < 16) & (view == 2 * column + core)).astype(F32)
    by_key = lax.dot_general(pick, seen, (((1,), (1,)), ((), ())), preferred_element_type=F32)
    allowed = jnp.dot(by_key, query_pick, preferred_element_type=F32)
    column = lanes((count, 128)) - HEAD
    return row(jnp.where((column >= 0) & (column < 16) & (allowed < 0.5), NEG, 0.0))


def fill(key_s, value_s, at, kv, bias):
    rows = slice(at * CELLS, (at + 1) * CELLS)
    low = row(jnp.where(lanes((1, CELLS)) < HEAD, 1.0, 0.0))
    key_s[rows] = kv * low + bias
    value_s[rows] = kv * (1 - low) + low


def view_kernel(own_ref, other_ref, mask_ref, order_ref, out_ref, key_s, value_s, s_a, s_b):
    del order_ref
    core = lax.axis_index("c")
    lane = lanes((CELLS, CELLS))
    block = rows_of((32, 32))
    bias = seen_bias(mask_ref, jnp.where(block < 16, 2 * block + core, 2 * (block - 16) + 1 - core), 32)
    for b in range(32):
        kv = own_ref[b, 0:CELLS] if b < 16 else other_ref[b - 16]
        fill(key_s, value_s, b, kv, bias[b : b + 1])

    def query(j):
        qq = own_ref[j, CELLS : 2 * CELLS].astype(F32)
        return jnp.where(lane < HEAD, qq, (lane == HEAD + j).astype(F32)).astype(BF16)

    def tile(i):
        return jnp.concatenate([query(2 * i), query(2 * i + 1)], axis=0)

    wide = lanes((TILE, CELLS))

    def finish(i, score_ref, row_max):
        main = weigh_tile(score_ref, row_max, value_s, 4096)
        heads = jnp.where(wide < HEAD, swap_halves(main) / main, 0.0)
        table = level_rows([row_max * RATE + jnp.log2(jnp.where(wide < HEAD, main, 1.0))], wide)
        for n in range(2):
            rows = slice(n * CELLS, (n + 1) * CELLS)
            out_ref[2 * i + n, 0:CELLS] = heads[rows].astype(BF16)
            out_ref[2 * i + n, CELLS:O_ROWS] = table[rows].T[0:16].astype(BF16)

    first = score_tile(tile(0), key_s, s_a, 4096)

    def body(step, m_a):
        m_b = score_tile(tile(2 * step + 1), key_s, s_b, 4096)
        finish(2 * step, s_a, m_a)
        m_next = score_tile(tile(jnp.minimum(2 * step + 2, 7)), key_s, s_a, 4096)
        finish(2 * step + 1, s_b, m_b)
        return m_next

    lax.fori_loop(0, 4, body, first)


def view_attention(own, other, view_mask, order):
    return pl.pallas_call(
        view_kernel,
        out_shape=jax.ShapeDtypeStruct((MAIN, O_ROWS, CELLS), BF16),
        in_specs=[VMEM] * 3 + [ANY],
        out_specs=VMEM,
        scratch_shapes=[
            pltpu.VMEM((4096, CELLS), BF16),
            pltpu.VMEM((4096, CELLS), BF16),
            pltpu.VMEM((TILE, 4096), F32),
            pltpu.VMEM((TILE, 4096), F32),
        ],
        compiler_params=params(20),
        cost_estimate=pl.CostEstimate(flops=8000000000, bytes_accessed=4000000, transcendentals=9000000),
        name="view_attention",
    )(own, other, view_mask, order)


def ring_kernel(main_ref, own_ref, r0, r1, r2, r3, mask_ref, order_ref, out_hbm, out_ref, sems, key_s, value_s, s_ref):
    del order_ref
    core = lax.axis_index("c")
    y = lax.axis_index("y")
    ring = lax.axis_index("g") * 2 + lax.axis_index("zl")
    lane = lanes((CELLS, CELLS))
    block = rows_of((8, 32))
    side = jnp.where(block % 2 == 0, core, 1 - core)
    bias = seen_bias(mask_ref, ring * 8 + 2 * (y ^ (block // 2)) + side, 8)
    for k, piece in enumerate((r0, r1, r2, r3)):
        for n in range(2):
            fill(key_s, value_s, 2 * k + n, piece[n], bias[2 * k + n : 2 * k + n + 1])

    def query(j):
        qq = swap_halves(own_ref[j, CELLS : 2 * CELLS].astype(F32))
        return jnp.where(lane < HEAD, qq, (lane == HEAD + j).astype(F32)).astype(BF16)

    wide = lanes((TILE, CELLS))

    def begin(i):
        tile = jnp.concatenate([query(2 * i), query(2 * i + 1)], axis=0)
        return score_tile(tile, key_s, s_ref.at[i % 2], 1024)

    row_max = begin(0)
    copies = []
    for i in range(8):
        following = begin(i + 1) if i < 7 else None
        part = weigh_tile(s_ref.at[i % 2], row_max, value_s, 1024)
        heads = jnp.where(wide < HEAD, 0.0, part / swap_halves(part)).astype(BF16)
        level = row_max * RATE + jnp.log2(jnp.where(wide < HEAD, part, 1.0))
        table = level_rows([level], wide, 3)
        for n in range(2):
            rows = slice(n * CELLS, (n + 1) * CELLS)
            j = 2 * i + n
            out_ref[j, 0:CELLS] = main_ref[j, 0:CELLS] + heads[rows]
            out_ref[j, CELLS:O_ROWS] = main_ref[j, CELLS:O_ROWS] + table[rows].T[0:16].astype(BF16)
        copies.append(pltpu.make_async_copy(out_ref.at[pl.ds(2 * i, 2)], out_hbm.at[pl.ds(2 * i, 2)], sems.at[i]))
        copies[-1].start()
        row_max = following
    for copy in copies:
        copy.wait()


def ring_attention(main, own, pieces, view_mask, order):
    return pl.pallas_call(
        ring_kernel,
        out_shape=pltpu.HBM((MAIN, O_ROWS, CELLS), BF16),
        in_specs=[VMEM] * 7 + [ANY],
        out_specs=ANY,
        scratch_shapes=[
            pltpu.VMEM((MAIN, O_ROWS, CELLS), BF16),
            pltpu.SemaphoreType.DMA((8,)),
            pltpu.VMEM((1024, CELLS), BF16),
            pltpu.VMEM((1024, CELLS), BF16),
            pltpu.VMEM((2, TILE, 1024), F32),
        ],
        compiler_params=params(12),
        cost_estimate=pl.CostEstimate(flops=500000000, bytes_accessed=2000000, transcendentals=2000000),
        name="ring_attention",
    )(main, own, *pieces, view_mask, order)


def time_kernel(z0, z1, z2, z3, x_any, times_ref, o_hbm, o1, o2, o3, o0, z_s, x_ref, sems, key_s, value_s, q_s, s_ref):
    frame = lax.axis_index("f")
    lane = lanes((CELLS, CELLS))
    own = [z_s.at[k] for k in range(4)]
    outs = (o0, o1, o2, o3)

    l8, r8 = lanes((8, 128)), rows_of((8, 128))
    query_time = jnp.zeros((8, 128), jnp.int32)
    key_time = jnp.zeros((8, 128), jnp.int32)
    for k in range(FRAMES):
        now = times_ref[frame ^ k]
        query_time = jnp.where(l8 == HEAD + k, now, query_time)
        key_time = jnp.where(r8 == k, now, key_time)
    near = (jnp.abs(query_time - key_time) <= REACH) & (l8 - HEAD != r8)
    bias = row(jnp.where((l8 >= HEAD) & (l8 < HEAD + 4) & jnp.logical_not(near), NEG, 0.0))
    low = row(jnp.where(lanes((1, CELLS)) < HEAD, 1.0, 0.0))
    high = row(jnp.where(lanes((1, CELLS)) < HEAD, 0.0, 1.0))

    copy_all(list(zip((z0, z1, z2, z3, x_any), own + [x_ref])), sems)

    for head in range(5):
        for k in range(8):
            at = slice(head * CELLS, (head + 1) * CELLS)
            kv = own[k][at] if k < 4 else x_ref[k - 4, at]
            rows = slice(k * CELLS, (k + 1) * CELLS)
            key_s[head, rows] = kv * low + bias[k : k + 1]
            value_s[head, rows] = kv * high + low
    for k in range(4):
        rows = slice(k * CELLS, (k + 1) * CELLS)
        hot = jnp.where(lane == HEAD + k, 1.0, 0.0)
        for i in range(2):
            qq = own[k][(5 + i) * CELLS : (6 + i) * CELLS].astype(F32)
            q_s[2 * i, rows] = jnp.where(lane < HEAD, qq, hot).astype(BF16)
            q_s[2 * i + 1, rows] = jnp.where(lane < HEAD, swap_halves(qq), hot).astype(BF16)
        packed = own[k][896:960].astype(F32)
        qq = jnp.concatenate([packed, swap_halves(packed)], axis=0)
        q_s[4, rows] = jnp.where(lane < HEAD, qq, hot).astype(BF16)

    wide = lanes((TILE, CELLS))
    work = [(i, head) for i in range(2) for head in range(5)]

    def begin(n):
        i, head = work[n]
        return score_tile(q_s[head, i * TILE : (i + 1) * TILE], key_s.at[head], s_ref.at[n % 2], 1024)

    row_max = begin(0)
    heads, levels = [], []
    for n, (i, head) in enumerate(work):
        following = begin(n + 1) if n + 1 < len(work) else None
        total = weigh_tile(s_ref.at[n % 2], row_max, value_s.at[head], 1024)
        sums = swap_halves(total)
        if head % 2 == 0:
            heads.append(jnp.where(wide < HEAD, sums / total, 0.0))
        else:
            heads.append(jnp.where(wide < HEAD, 0.0, total / sums))
        levels.append(row_max * RATE + jnp.log2(jnp.where(wide < HEAD, total, 1.0)))
        row_max = following
        if head < 4:
            continue
        table = level_rows(levels, wide)
        for m in range(2):
            rows = slice(m * CELLS, (m + 1) * CELLS)
            out = outs[2 * i + m]
            out[0:128] = (heads[0] + heads[1])[rows].astype(BF16)
            out[128:256] = (heads[2] + heads[3])[rows].astype(BF16)
            last = heads[4][rows]
            out[256:320] = (last[0:64] + swap_halves(last[64:128])).astype(BF16)
            out[320:336] = table[rows].T[0:16].astype(BF16)
        if i == 0:
            keep = pltpu.make_async_copy(o0, o_hbm, sems.at[5])
            keep.start()
        heads, levels = [], []
    keep.wait()


def time_attention(own, crossed, frame_times):
    return pl.pallas_call(
        time_kernel,
        out_shape=[pltpu.HBM((T_ROWS, CELLS), BF16)] + [jax.ShapeDtypeStruct((T_ROWS, CELLS), BF16)] * 3,
        in_specs=[ANY] * 5 + [SMEM],
        out_specs=[ANY] + [VMEM] * 3,
        scratch_shapes=[
            pltpu.VMEM((T_ROWS, CELLS), BF16),
            pltpu.VMEM((4, Z_ROWS, CELLS), BF16),
            pltpu.VMEM((4, X_ROWS, CELLS), BF16),
            pltpu.SemaphoreType.DMA((6,)),
            pltpu.VMEM((5, 1024, CELLS), BF16),
            pltpu.VMEM((5, 1024, CELLS), BF16),
            pltpu.VMEM((5, 512, CELLS), BF16),
            pltpu.VMEM((2, TILE, 1024), F32),
        ],
        compiler_params=params(16),
        cost_estimate=pl.CostEstimate(flops=700000000, bytes_accessed=2000000, transcendentals=2700000),
        name="time_attention",
    )(*own, crossed, frame_times)


def join_kernel(view_any, t0, t1, t2, t3, weight_any, out_ref, view_ref, times, weight_ref, heads_s, sems):
    place = lax.axis_index("f") % 4
    load = pltpu.make_async_copy(weight_any, weight_ref, sems.at[5])
    moves = [(piece, times.at[turned(place, k)]) for k, piece in enumerate((t0, t1, t2, t3))]
    copies = [pltpu.make_async_copy(*move, sems.at[i]) for i, move in enumerate([*moves, (view_any, view_ref)])]
    for copy in copies:
        copy.start()
    load.start()
    for copy in copies:
        copy.wait()

    view_rows = jnp.concatenate([view_ref[t, CELLS:O_ROWS] for t in range(MAIN)], axis=0)
    time_rows = jnp.concatenate([times[j, 320:336] for j in range(4)], axis=0)

    def levels(rows, picked):
        pick = jnp.where(picked, 1.0, 0.0).astype(BF16)
        return lax.dot_general(rows, pick, (((0,), (0,)), ((), ())), preferred_element_type=F32)

    at, head = rows_of((256, 128)), lanes((256, 128))
    source, part = at // 16, at % 16
    found = []
    for ring in range(4):
        picked = (head >= MAIN) & (source == 4 * ring + head - MAIN) & (part >= 3) & (part < 6)
        if ring == 0:
            picked = picked | ((head < MAIN) & (source == head) & (part < 3))
        found.append(levels(view_rows, picked))
    at, head = rows_of((64, 128)), lanes((64, 128))
    offset = at % 16 - 3 * (head - 5 * (at // 16))
    inside = (head >= 5 * (at // 16)) & (head < 5 * (at // 16) + 5)
    found.append(levels(time_rows, inside & (offset >= 0) & (offset < 3)))
    column = lanes((CELLS, CELLS))
    for ring in range(1, 4):
        found[ring] = jnp.where(column < MAIN, -1e30, found[ring])
    best = found[0]
    for value in found[1:]:
        best = jnp.maximum(best, value)
    powers = [jnp.exp2(value - best) for value in found]
    total = powers[0]
    for power in powers[1:]:
        total = total + power
    shares = [power / total for power in powers]

    def time_block(head):
        j, i = head // 5, head % 5
        if i < 4:
            rows = slice((i // 2) * CELLS, (i // 2 + 1) * CELLS)
            return times[j, rows, (i % 2) * HEAD : (i % 2 + 1) * HEAD].astype(F32)
        packed = times[j, 256:320].astype(F32)
        return jnp.concatenate([packed[:, 0:HEAD], packed[:, HEAD:128]], axis=0)

    load.wait()
    result = None
    for first in range(0, HEADS, 4):
        for h in range(first, first + 4):
            mixed = time_block(h) * shares[4][:, h : h + 1]
            if h < MAIN:
                mixed += view_ref[h, 0:CELLS, 0:HEAD].astype(F32) * shares[0][:, h : h + 1]
            else:
                for ring in range(4):
                    block = view_ref[4 * ring + h - MAIN, 0:CELLS, HEAD:128].astype(F32)
                    mixed += block * shares[ring][:, h : h + 1]
            heads_s[:, h * HEAD : (h + 1) * HEAD] = mixed.astype(BF16)
        columns = slice(first * HEAD, (first + 4) * HEAD)
        product = jnp.dot(heads_s[:, columns], weight_ref[columns], preferred_element_type=F32)
        result = product if result is None else result + product
    out_ref[...] = result.astype(BF16)


def join(view_out, pieces, out_weight):
    return pl.pallas_call(
        join_kernel,
        out_shape=jax.ShapeDtypeStruct((CELLS, HEADS * HEAD), BF16),
        in_specs=[ANY] * 6,
        out_specs=VMEM,
        scratch_shapes=[
            pltpu.VMEM((MAIN, O_ROWS, CELLS), BF16),
            pltpu.VMEM((4, T_ROWS, CELLS), BF16),
            pltpu.VMEM((HEADS * HEAD, HEADS * HEAD), BF16),
            pltpu.VMEM((CELLS, HEADS * HEAD), BF16),
            pltpu.SemaphoreType.DMA((6,)),
        ],
        compiler_params=params(16),
        name="join",
    )(view_out, *pieces, in_hbm(out_weight))


def across(array, k):
    return lax.ppermute(array, "f", [(i, i ^ k) for i in range(FRAMES)])


def around(array, k):
    return lax.ppermute(array, "y", [(i, i ^ k) for i in range(RING)])


def sibling(array):
    return lax.ppermute(array, "c", [(0, 1), (1, 0)])


def local(queries, keys, values, view_mask, frame_times, out_weight):
    model = queries.shape[3]
    q, k, v = (a.reshape(CELLS, model) for a in (queries, keys, values))
    *z, to_ring, q, k, v = pack_time(q, k, v)
    z = [in_hbm(z[0])] + [across(z[i], i) for i in (1, 2, 3)]
    beside = sibling(to_ring)
    own = lax.all_to_all(pack_view(q, k, v), ("g", "zl", "y"), 0, 0)
    stacked, kv, *ring = stack(z, own, to_ring, beside)
    ring = [ring[0]] + [around(ring[i], i) for i in (1, 2, 3)]
    crossed = across(stacked, 4)
    main_out = view_attention(own, sibling(kv), view_mask, stacked)
    view_out = ring_attention(main_out, own, ring, view_mask, crossed)
    view_back = lax.all_to_all(view_out, ("g", "zl", "y"), 0, 0)
    pieces = time_attention([in_hbm(a) for a in z], in_hbm(crossed), frame_times)
    pieces = [in_hbm(pieces[0])] + [across(pieces[i], i) for i in (1, 2, 3)]
    result = join(view_back, pieces, out_weight)
    return result.reshape(1, 1, CELLS, model)


def solution(mesh):
    fine = Mesh(mesh.devices.reshape(2, 8, 2, 4, 2), ("g", "f", "zl", "y", "c"))
    blocks = P(("g", "f"), ("zl", "y", "c"), None, None)
    return jax.shard_map(
        local,
        mesh=fine,
        in_specs=(blocks, blocks, blocks, P(), P(), P()),
        out_specs=blocks,
        check_vma=False,
    )
```

```python
import jax
import jax.numpy as jnp
from jax import lax
from jax.experimental import pallas as pl
from jax.experimental.pallas import tpu as pltpu
from jax.sharding import Mesh, PartitionSpec as P

HEADS = 20
REACH = 4
FRAMES = 8
HEAD = 64
CELLS = 128
MAIN = 16
RING = 4
NEG = -(2.0**30)
LOG2E = 1.4426950408889634
RATE = HEAD**-0.5 * LOG2E
TILE = 256
CHUNK = 512
Z_ROWS = 960
X_ROWS = 640
T_ROWS = 336
O_ROWS = 144
F32 = jnp.float32
BF16 = jnp.bfloat16
ANY = pl.BlockSpec(memory_space=pl.ANY)
VMEM = pl.BlockSpec(memory_space=pltpu.VMEM)
SMEM = pl.BlockSpec(memory_space=pltpu.SMEM)


def lanes(shape):
    return lax.broadcasted_iota(jnp.int32, shape, len(shape) - 1)


def rows_of(shape):
    return lax.broadcasted_iota(jnp.int32, shape, len(shape) - 2)


def swap_halves(x):
    return pltpu.roll(x, HEAD, 1)


def params(mib):
    return pltpu.CompilerParams(vmem_limit_bytes=mib * 1024 * 1024)


def turned(index, k):
    return (index, index + 1 - 2 * (index % 2), (index + 2) % 4, 3 - index)[k]


def copy_all(moves, sems):
    copies = [pltpu.make_async_copy(source, target, sems.at[i]) for i, (source, target) in enumerate(moves)]
    for copy in copies:
        copy.start()
    for copy in copies:
        copy.wait()


def pair(a_ref, a, b_ref, b):
    left = a_ref[:, a * HEAD : (a + 1) * HEAD]
    right = b_ref[:, b * HEAD : (b + 1) * HEAD]
    return jnp.concatenate([left, right], axis=1)


def pack_time_kernel(q_hbm, k_hbm, v_hbm, z0, z1, z2, z3, q_ref, k_ref, v_ref, sems, parts):
    place = lax.axis_index("f") % 4
    copy_all([(k_hbm, k_ref), (v_hbm, v_ref), (q_hbm, q_ref)], sems)
    for j in range(4):
        base = 5 * j
        for i in range(5):
            parts[j, i * CELLS : (i + 1) * CELLS] = pair(k_ref, base + i, v_ref, base + i)
        for i in range(2):
            rows = slice((5 + i) * CELLS, (6 + i) * CELLS)
            parts[j, rows] = pair(q_ref, base + 2 * i, q_ref, base + 2 * i + 1)
        last = q_ref[:, (base + 4) * HEAD : (base + 5) * HEAD]
        parts[j, 896:960] = jnp.concatenate([last[0:64], last[64:128]], axis=1)
    keep = pltpu.make_async_copy(parts.at[place], z0, sems.at[3])
    keep.start()
    for k, out in enumerate((z1, z2, z3)):
        out[...] = parts[turned(place, k + 1)]
    keep.wait()


def in_hbm(x):
    return pltpu.with_memory_space_constraint(x, pltpu.HBM)


def pack_time(q, k, v):
    block = jax.ShapeDtypeStruct((Z_ROWS, CELLS), BF16)
    whole = pltpu.VMEM((CELLS, HEADS * HEAD), BF16)
    return pl.pallas_call(
        pack_time_kernel,
        out_shape=[block] * 4,
        in_specs=[ANY] * 3,
        out_specs=[ANY] + [VMEM] * 3,
        scratch_shapes=[whole] * 3 + [pltpu.SemaphoreType.DMA((4,)), pltpu.VMEM((4, Z_ROWS, CELLS), BF16)],
        compiler_params=params(16),
        name="pack_time",
    )(in_hbm(q), in_hbm(k), in_hbm(v))


def pack_view_kernel(q_hbm, k_hbm, v_hbm, view_ref, ring_ref, q_ref, k_ref, v_ref, sems):
    load = pltpu.make_async_copy(q_hbm, q_ref, sems.at[2])
    load.start()
    copy_all([(k_hbm, k_ref), (v_hbm, v_ref)], sems)
    for t in range(MAIN):
        view_ref[t, 0:CELLS] = pair(k_ref, t, v_ref, t)
    for y in range(RING):
        ring_ref[y] = pair(k_ref, MAIN + y, v_ref, MAIN + y)
    load.wait()
    for t in range(MAIN):
        view_ref[t, CELLS : 2 * CELLS] = pair(q_ref, t, q_ref, MAIN + t % RING)


def pack_view(q, k, v):
    whole = pltpu.VMEM((CELLS, HEADS * HEAD), BF16)
    return pl.pallas_call(
        pack_view_kernel,
        out_shape=[
            jax.ShapeDtypeStruct((MAIN, 2 * CELLS, CELLS), BF16),
            jax.ShapeDtypeStruct((RING, CELLS, CELLS), BF16),
        ],
        in_specs=[ANY] * 3,
        out_specs=[VMEM] * 2,
        scratch_shapes=[whole] * 3 + [pltpu.SemaphoreType.DMA((3,))],
        compiler_params=params(16),
        name="pack_view",
    )(in_hbm(q), in_hbm(k), in_hbm(v))


def ring_pack_kernel(ring_ref, sibling_ref, r0, r1, r2, r3):
    y = lax.axis_index("y")
    for k, out in enumerate((r0, r1, r2, r3)):
        out[0] = ring_ref[turned(y, k)]
        out[1] = sibling_ref[turned(y, k)]


def ring_pack(ring, other):
    return pl.pallas_call(
        ring_pack_kernel,
        out_shape=[jax.ShapeDtypeStruct((2, CELLS, CELLS), BF16)] * 4,
        in_specs=[VMEM] * 2,
        out_specs=[VMEM] * 4,
        compiler_params=params(4),
        name="ring_pack",
    )(ring, other)


def stack_kernel(own_ref, z0, z1, z3, *refs):
    kv_ref, out_ref, sems = refs[-3:]
    moves = [(own_ref.at[:, pl.ds(0, CELLS)], kv_ref)]
    moves += [(piece.at[pl.ds(0, X_ROWS)], out_ref.at[k]) for k, piece in enumerate((z0, z1, z3))]
    copy_all(moves, sems)


def stack(own, z0, z1, z3, order):
    return pl.pallas_call(
        stack_kernel,
        out_shape=[
            jax.ShapeDtypeStruct((MAIN, CELLS, CELLS), BF16),
            jax.ShapeDtypeStruct((3, X_ROWS, CELLS), BF16),
        ],
        in_specs=[ANY] * (4 + len(order)),
        out_specs=[ANY] * 2,
        scratch_shapes=[pltpu.SemaphoreType.DMA((4,))],
        compiler_params=params(4),
        name="stack",
    )(own, z0, z1, z3, *order)


def strip_kernel(z_ref, order_ref, out_ref):
    del order_ref
    out_ref[...] = z_ref[0:X_ROWS]


def strip(z, order):
    return pl.pallas_call(
        strip_kernel,
        out_shape=jax.ShapeDtypeStruct((X_ROWS, CELLS), BF16),
        in_specs=[VMEM, ANY],
        out_specs=VMEM,
        compiler_params=params(4),
        name="strip",
    )(z, order)


def score_tile(q, key_ref, score_ref, count):
    best = None
    for start in range(0, count, CHUNK):
        s = lax.dot_general(
            q, key_ref[start : start + CHUNK], (((1,), (1,)), ((), ())), preferred_element_type=F32
        )
        score_ref[:, start : start + CHUNK] = s
        for lane in range(0, CHUNK, 128):
            part = s[:, lane : lane + 128]
            best = part if best is None else jnp.maximum(best, part)
    return jnp.max(best, axis=1, keepdims=True)


def weigh_tile(score_ref, row_max, value_ref, count):
    total = None
    for start in range(0, count, CHUNK):
        s = score_ref[:, start : start + CHUNK]
        w = jnp.exp2((s - row_max) * RATE).astype(BF16)
        part = jnp.dot(w, value_ref[start : start + CHUNK], preferred_element_type=F32)
        total = part if total is None else total + part
    return total


def split3(x):
    high = x.astype(BF16).astype(F32)
    middle = (x - high).astype(BF16).astype(F32)
    low = (x - high - middle).astype(BF16).astype(F32)
    return [high, middle, low]


def level_rows(levels, lane, at=0):
    columns = [part for level in levels for part in split3(level)]
    table = jnp.zeros_like(columns[0])
    for i, column in enumerate(columns):
        table = jnp.where(lane == at + i, column, table)
    return table


def row(x):
    return x.astype(BF16)


def seen_bias(mask_ref, key_view, count):
    core = lax.axis_index("c")
    seen = mask_ref[lax.axis_index("f")].astype(F32)
    pick = (lanes((count, 32)) == key_view).astype(F32)
    view, column = rows_of((32, 128)), lanes((32, 128)) - HEAD
    query_pick = ((column >= 0) & (column < 16) & (view == 2 * column + core)).astype(F32)
    by_key = lax.dot_general(pick, seen, (((1,), (1,)), ((), ())), preferred_element_type=F32)
    allowed = jnp.dot(by_key, query_pick, preferred_element_type=F32)
    column = lanes((count, 128)) - HEAD
    return row(jnp.where((column >= 0) & (column < 16) & (allowed < 0.5), NEG, 0.0))


def fill(key_s, value_s, at, kv, bias):
    rows = slice(at * CELLS, (at + 1) * CELLS)
    low = row(jnp.where(lanes((1, CELLS)) < HEAD, 1.0, 0.0))
    key_s[rows] = kv * low + bias
    value_s[rows] = kv * (1 - low) + low


def attend_views(own_ref, ring_ref, key_s, value_s, s_a, s_b, first, write):
    lane = lanes((CELLS, CELLS))
    wide = lanes((TILE, CELLS))

    def query(j):
        qq = own_ref[j, CELLS : 2 * CELLS].astype(F32)
        return jnp.where(lane < HEAD, qq, (lane == HEAD + j).astype(F32)).astype(BF16)

    def tile(i):
        return jnp.concatenate([query(2 * i), query(2 * i + 1)], axis=0)

    def finish(i, score_ref, row_max):
        main = weigh_tile(score_ref, row_max, value_s, 4096)
        heads = jnp.where(wide < HEAD, swap_halves(main) / main, 0.0)
        table = level_rows([row_max * RATE + jnp.log2(jnp.where(wide < HEAD, main, 1.0))], wide)
        for n in range(2):
            rows = slice(n * CELLS, (n + 1) * CELLS)
            j = 2 * i + n
            head_rows = ring_ref[j, 0:CELLS] + heads[rows].astype(BF16)
            write(j, head_rows, ring_ref[j, CELLS:O_ROWS] + table[rows].T[0:16].astype(BF16))

    start = score_tile(tile(first), key_s, s_a, 4096)

    def body(step, m_a):
        i = first + 2 * step
        m_b = score_tile(tile(i + 1), key_s, s_b, 4096)
        finish(i, s_a, m_a)
        m_next = score_tile(tile(jnp.minimum(i + 2, first + 3)), key_s, s_a, 4096)
        finish(i + 1, s_b, m_b)
        return m_next

    lax.fori_loop(0, 2, body, start)


def view_kernel(own_ref, other_ref, ring_ref, mask_ref, out_ref, key_s, value_s, s_a, s_b):
    core = lax.axis_index("c")
    block = rows_of((32, 32))
    bias = seen_bias(mask_ref, jnp.where(block < 16, 2 * block + core, 2 * (block - 16) + 1 - core), 32)
    for b in range(32):
        kv = own_ref[b, 0:CELLS] if b < 16 else other_ref[b - 16]
        fill(key_s, value_s, b, kv, bias[b : b + 1])

    def write(j, head_rows, level_part):
        out_ref[j, 0:CELLS] = head_rows
        out_ref[j, CELLS:O_ROWS] = level_part

    attend_views(own_ref, ring_ref, key_s, value_s, s_a, s_b, 0, write)


def view_rest_kernel(own_ref, ring_ref, half_ref, key_s, value_s, out_hbm, out_ref, sems, s_a, s_b):
    early = pltpu.make_async_copy(half_ref, out_hbm.at[pl.ds(0, 8)], sems.at[8])
    early.start()

    def away(j):
        return pltpu.make_async_copy(out_ref.at[j], out_hbm.at[j], sems.at[j - 8])

    def write(j, head_rows, level_part):
        out_ref[j, 0:CELLS] = head_rows
        out_ref[j, CELLS:O_ROWS] = level_part
        away(j).start()

    attend_views(own_ref, ring_ref, key_s, value_s, s_a, s_b, 4, write)
    for j in range(8, 16):
        away(j).wait()
    early.wait()


SCORES = [pltpu.VMEM((TILE, 4096), F32)] * 2


def view_attention(own, other, ring_out, view_mask):
    filled = jax.ShapeDtypeStruct((4096, CELLS), BF16)
    return pl.pallas_call(
        view_kernel,
        out_shape=[jax.ShapeDtypeStruct((8, O_ROWS, CELLS), BF16), filled, filled],
        in_specs=[VMEM] * 4,
        out_specs=[VMEM] * 3,
        scratch_shapes=SCORES,
        compiler_params=params(16),
        cost_estimate=pl.CostEstimate(flops=1000000, bytes_accessed=100000, transcendentals=0),
        name="view_attention",
    )(own, other, ring_out, view_mask)


def view_attention_rest(own, ring_out, half, key_rows, value_rows):
    return pl.pallas_call(
        view_rest_kernel,
        out_shape=pltpu.HBM((MAIN, O_ROWS, CELLS), BF16),
        in_specs=[VMEM] * 5,
        out_specs=ANY,
        scratch_shapes=[pltpu.VMEM((MAIN, O_ROWS, CELLS), BF16), pltpu.SemaphoreType.DMA((9,))] + SCORES,
        compiler_params=params(16),
        cost_estimate=pl.CostEstimate(flops=1000000, bytes_accessed=100000, transcendentals=0),
        name="view_attention_rest",
    )(own, ring_out, half, key_rows, value_rows)


def ring_kernel(own_ref, r0, r1, r2, r3, mask_ref, out_ref, key_s, value_s, s_ref):
    core = lax.axis_index("c")
    y = lax.axis_index("y")
    ring = lax.axis_index("g") * 2 + lax.axis_index("zl")
    lane = lanes((CELLS, CELLS))
    block = rows_of((8, 32))
    side = jnp.where(block % 2 == 0, core, 1 - core)
    bias = seen_bias(mask_ref, ring * 8 + 2 * (y ^ (block // 2)) + side, 8)
    for k, piece in enumerate((r0, r1, r2, r3)):
        for n in range(2):
            fill(key_s, value_s, 2 * k + n, piece[n], bias[2 * k + n : 2 * k + n + 1])

    def query(j):
        qq = swap_halves(own_ref[j, CELLS : 2 * CELLS].astype(F32))
        return jnp.where(lane < HEAD, qq, (lane == HEAD + j).astype(F32)).astype(BF16)

    wide = lanes((TILE, CELLS))

    def begin(i):
        tile = jnp.concatenate([query(2 * i), query(2 * i + 1)], axis=0)
        return score_tile(tile, key_s, s_ref.at[i % 2], 1024)

    row_max = begin(0)
    for i in range(8):
        following = begin(i + 1) if i < 7 else None
        part = weigh_tile(s_ref.at[i % 2], row_max, value_s, 1024)
        heads = jnp.where(wide < HEAD, 0.0, part / swap_halves(part)).astype(BF16)
        level = row_max * RATE + jnp.log2(jnp.where(wide < HEAD, part, 1.0))
        table = level_rows([level], wide, 3)
        for n in range(2):
            rows = slice(n * CELLS, (n + 1) * CELLS)
            j = 2 * i + n
            out_ref[j, 0:CELLS] = heads[rows]
            out_ref[j, CELLS:O_ROWS] = table[rows].T[0:16].astype(BF16)
        row_max = following


def ring_attention(own, pieces, view_mask):
    return pl.pallas_call(
        ring_kernel,
        out_shape=jax.ShapeDtypeStruct((MAIN, O_ROWS, CELLS), BF16),
        in_specs=[VMEM] * 6,
        out_specs=VMEM,
        scratch_shapes=[
            pltpu.VMEM((1024, CELLS), BF16),
            pltpu.VMEM((1024, CELLS), BF16),
            pltpu.VMEM((2, TILE, 1024), F32),
        ],
        compiler_params=params(12),
        cost_estimate=pl.CostEstimate(flops=1000000, bytes_accessed=100000, transcendentals=0),
        name="ring_attention",
    )(own, *pieces, view_mask)


def time_kernel(z0, z1, z2, z3, x_ref, x2_ref, times_ref, o0, o1, o2, o3, key_s, value_s, q_s, s_ref):
    frame = lax.axis_index("f")
    lane = lanes((CELLS, CELLS))
    own = (z0, z1, z2, z3)
    far = (x_ref.at[0], x_ref.at[1], x2_ref, x_ref.at[2])
    outs = (o0, o1, o2, o3)

    l8, r8 = lanes((8, 128)), rows_of((8, 128))
    query_time = jnp.zeros((8, 128), jnp.int32)
    key_time = jnp.zeros((8, 128), jnp.int32)
    for k in range(FRAMES):
        now = times_ref[frame ^ k]
        query_time = jnp.where(l8 == HEAD + k, now, query_time)
        key_time = jnp.where(r8 == k, now, key_time)
    near = (jnp.abs(query_time - key_time) <= REACH) & (l8 - HEAD != r8)
    bias = row(jnp.where((l8 >= HEAD) & (l8 < HEAD + 4) & jnp.logical_not(near), NEG, 0.0))
    low = row(jnp.where(lanes((1, CELLS)) < HEAD, 1.0, 0.0))
    high = row(jnp.where(lanes((1, CELLS)) < HEAD, 0.0, 1.0))

    for head in range(5):
        for k in range(8):
            at = slice(head * CELLS, (head + 1) * CELLS)
            kv = (own + far)[k][at]
            rows = slice(k * CELLS, (k + 1) * CELLS)
            key_s[head, rows] = kv * low + bias[k : k + 1]
            value_s[head, rows] = kv * high + low
    for k in range(4):
        rows = slice(k * CELLS, (k + 1) * CELLS)
        hot = jnp.where(lane == HEAD + k, 1.0, 0.0)
        for i in range(2):
            qq = own[k][(5 + i) * CELLS : (6 + i) * CELLS].astype(F32)
            q_s[2 * i, rows] = jnp.where(lane < HEAD, qq, hot).astype(BF16)
            q_s[2 * i + 1, rows] = jnp.where(lane < HEAD, swap_halves(qq), hot).astype(BF16)
        packed = own[k][896:960].astype(F32)
        qq = jnp.concatenate([packed, swap_halves(packed)], axis=0)
        q_s[4, rows] = jnp.where(lane < HEAD, qq, hot).astype(BF16)

    wide = lanes((TILE, CELLS))
    work = [(i, head) for i in range(2) for head in range(5)]

    def begin(n):
        i, head = work[n]
        return score_tile(q_s[head, i * TILE : (i + 1) * TILE], key_s.at[head], s_ref.at[n % 2], 1024)

    row_max = begin(0)
    heads, levels = [], []
    for n, (i, head) in enumerate(work):
        following = begin(n + 1) if n + 1 < len(work) else None
        total = weigh_tile(s_ref.at[n % 2], row_max, value_s.at[head], 1024)
        sums = swap_halves(total)
        if head % 2 == 0:
            heads.append(jnp.where(wide < HEAD, sums / total, 0.0))
        else:
            heads.append(jnp.where(wide < HEAD, 0.0, total / sums))
        levels.append(row_max * RATE + jnp.log2(jnp.where(wide < HEAD, total, 1.0)))
        row_max = following
        if head < 4:
            continue
        table = level_rows(levels, wide)
        for m in range(2):
            rows = slice(m * CELLS, (m + 1) * CELLS)
            out = outs[2 * i + m]
            out[0:128] = (heads[0] + heads[1])[rows].astype(BF16)
            out[128:256] = (heads[2] + heads[3])[rows].astype(BF16)
            last = heads[4][rows]
            out[256:320] = (last[0:64] + swap_halves(last[64:128])).astype(BF16)
            out[320:336] = table[rows].T[0:16].astype(BF16)
        heads, levels = [], []


def time_attention(own, crossed, frame_times):
    return pl.pallas_call(
        time_kernel,
        out_shape=[jax.ShapeDtypeStruct((T_ROWS, CELLS), BF16)] * 4,
        in_specs=[VMEM] * 6 + [SMEM],
        out_specs=[VMEM] * 4,
        scratch_shapes=[
            pltpu.VMEM((5, 1024, CELLS), BF16),
            pltpu.VMEM((5, 1024, CELLS), BF16),
            pltpu.VMEM((5, 512, CELLS), BF16),
            pltpu.VMEM((2, TILE, 1024), F32),
        ],
        compiler_params=params(16),
        cost_estimate=pl.CostEstimate(flops=700000000, bytes_accessed=2000000, transcendentals=2700000),
        name="time_attention",
    )(*own, *crossed, frame_times)


def pass_kernel(*refs):
    del refs


def pass_after(array, others):
    return pl.pallas_call(
        pass_kernel,
        out_shape=pltpu.HBM(array.shape, array.dtype),
        in_specs=[ANY] * (1 + len(others)),
        out_specs=ANY,
        input_output_aliases={0: 0},
        compiler_params=params(4),
        name="pass_after",
    )(in_hbm(array), *others)


def join_kernel(view_ref, t0, t1, t2, t3, weight_any, out_ref, times, heads_s, weight_ref, sems):
    load = pltpu.make_async_copy(weight_any, weight_ref, sems.at[0])
    load.start()
    place = lax.axis_index("f") % 4
    for k, piece in enumerate((t0, t1, t2, t3)):
        times[turned(place, k)] = piece[...]

    view_rows = jnp.concatenate([view_ref[t, CELLS:O_ROWS] for t in range(MAIN)], axis=0)
    time_rows = jnp.concatenate([times[j, 320:336] for j in range(4)], axis=0)

    def levels(rows, picked):
        pick = jnp.where(picked, 1.0, 0.0).astype(BF16)
        return lax.dot_general(rows, pick, (((0,), (0,)), ((), ())), preferred_element_type=F32)

    at, head = rows_of((256, 128)), lanes((256, 128))
    source, part = at // 16, at % 16
    found = []
    for ring in range(4):
        picked = (head >= MAIN) & (source == 4 * ring + head - MAIN) & (part >= 3) & (part < 6)
        if ring == 0:
            picked = picked | ((head < MAIN) & (source == head) & (part < 3))
        found.append(levels(view_rows, picked))
    at, head = rows_of((64, 128)), lanes((64, 128))
    offset = at % 16 - 3 * (head - 5 * (at // 16))
    inside = (head >= 5 * (at // 16)) & (head < 5 * (at // 16) + 5)
    found.append(levels(time_rows, inside & (offset >= 0) & (offset < 3)))
    column = lanes((CELLS, CELLS))
    for ring in range(1, 4):
        found[ring] = jnp.where(column < MAIN, -1e30, found[ring])
    best = found[0]
    for value in found[1:]:
        best = jnp.maximum(best, value)
    powers = [jnp.exp2(value - best) for value in found]
    total = powers[0]
    for power in powers[1:]:
        total = total + power
    shares = [power / total for power in powers]

    def time_block(head):
        j, i = head // 5, head % 5
        if i < 4:
            rows = slice((i // 2) * CELLS, (i // 2 + 1) * CELLS)
            return times[j, rows, (i % 2) * HEAD : (i % 2 + 1) * HEAD].astype(F32)
        packed = times[j, 256:320].astype(F32)
        return jnp.concatenate([packed[:, 0:HEAD], packed[:, HEAD:128]], axis=0)

    load.wait()
    result = None
    for first in range(0, HEADS, 4):
        for h in range(first, first + 4):
            mixed = time_block(h) * shares[4][:, h : h + 1]
            if h < MAIN:
                mixed += view_ref[h, 0:CELLS, 0:HEAD].astype(F32) * shares[0][:, h : h + 1]
            else:
                for ring in range(4):
                    block = view_ref[4 * ring + h - MAIN, 0:CELLS, HEAD:128].astype(F32)
                    mixed += block * shares[ring][:, h : h + 1]
            heads_s[:, h * HEAD : (h + 1) * HEAD] = mixed.astype(BF16)
        columns = slice(first * HEAD, (first + 4) * HEAD)
        product = jnp.dot(heads_s[:, columns], weight_ref[columns], preferred_element_type=F32)
        result = product if result is None else result + product
    out_ref[...] = result.astype(BF16)


def join(view_out, pieces, out_weight):
    return pl.pallas_call(
        join_kernel,
        out_shape=jax.ShapeDtypeStruct((CELLS, HEADS * HEAD), BF16),
        in_specs=[VMEM] * 5 + [ANY],
        out_specs=VMEM,
        scratch_shapes=[
            pltpu.VMEM((4, T_ROWS, CELLS), BF16),
            pltpu.VMEM((CELLS, HEADS * HEAD), BF16),
            pltpu.VMEM((HEADS * HEAD, HEADS * HEAD), BF16),
            pltpu.SemaphoreType.DMA((1,)),
        ],
        compiler_params=params(16),
        name="join",
    )(view_out, *pieces, in_hbm(out_weight))


def across(array, k):
    return lax.ppermute(array, "f", [(i, i ^ k) for i in range(FRAMES)])


def around(array, k):
    return lax.ppermute(array, "y", [(i, i ^ k) for i in range(RING)])


def sibling(array):
    return lax.ppermute(array, "c", [(0, 1), (1, 0)])


def local(queries, keys, values, view_mask, frame_times, out_weight):
    model = queries.shape[3]
    q, k, v = (a.reshape(CELLS, model) for a in (queries, keys, values))
    to_view, to_ring = pack_view(q, k, v)
    own = lax.all_to_all(to_view, ("g", "zl", "y"), 0, 0)
    ring = ring_pack(to_ring, sibling(to_ring))
    ring = [ring[0]] + [around(ring[i], i) for i in (1, 2, 3)]
    z0, z1, z2, z3 = pack_time(q, k, v)
    z1, z2, z3 = across(z1, 1), across(z2, 2), across(z3, 3)
    kv, some = stack(own, z0, z1, z3, ring[1:])
    ring_out = ring_attention(own, ring, view_mask)
    half, *filled = view_attention(own, sibling(kv), ring_out, view_mask)
    crossed = (across(some, 4), across(strip(z2, half), 4))
    view_out = view_attention_rest(own, ring_out, half, *filled)
    view_out = pass_after(view_out, crossed)
    view_back = lax.all_to_all(view_out, ("g", "zl", "y"), 0, 0)
    pieces = time_attention((z0, z1, z2, z3), crossed, frame_times)
    pieces = [pieces[0]] + [across(pieces[i], i) for i in (1, 2, 3)]
    result = join(view_back, pieces, out_weight)
    return result.reshape(1, 1, CELLS, model)


def solution(mesh):
    fine = Mesh(mesh.devices.reshape(2, 8, 2, 4, 2), ("g", "f", "zl", "y", "c"))
    blocks = P(("g", "f"), ("zl", "y", "c"), None, None)
    return jax.shard_map(
        local,
        mesh=fine,
        in_specs=(blocks, blocks, blocks, P(), P(), P()),
        out_specs=blocks,
        check_vma=False,
    )
```

```python
import jax
import jax.numpy as jnp
from jax import lax
from jax.experimental import pallas as pl
from jax.experimental.pallas import tpu as pltpu
from jax.sharding import Mesh, PartitionSpec as P

HEADS = 20
REACH = 4
FRAMES = 8
HEAD = 64
CELLS = 128
MAIN = 16
RING = 4
NEG = -(2.0**30)
LOG2E = 1.4426950408889634
RATE = HEAD**-0.5 * LOG2E
TILE = 256
CHUNK = 512
Z_ROWS = 960
X_ROWS = 640
T_ROWS = 336
O_ROWS = 144
F32 = jnp.float32
BF16 = jnp.bfloat16
ANY = pl.BlockSpec(memory_space=pl.ANY)
VMEM = pl.BlockSpec(memory_space=pltpu.VMEM)
SMEM = pl.BlockSpec(memory_space=pltpu.SMEM)


def lanes(shape):
    return lax.broadcasted_iota(jnp.int32, shape, len(shape) - 1)


def rows_of(shape):
    return lax.broadcasted_iota(jnp.int32, shape, len(shape) - 2)


def swap_halves(x):
    return pltpu.roll(x, HEAD, 1)


def params(mib):
    return pltpu.CompilerParams(vmem_limit_bytes=mib * 1024 * 1024)


def turned(index, k):
    return (index, index + 1 - 2 * (index % 2), (index + 2) % 4, 3 - index)[k]


def copy_all(moves, sems):
    copies = [pltpu.make_async_copy(source, target, sems.at[i]) for i, (source, target) in enumerate(moves)]
    for copy in copies:
        copy.start()
    for copy in copies:
        copy.wait()


def pair(a_ref, a, b_ref, b):
    left = a_ref[:, a * HEAD : (a + 1) * HEAD]
    right = b_ref[:, b * HEAD : (b + 1) * HEAD]
    return jnp.concatenate([left, right], axis=1)


def in_hbm(x):
    return pltpu.with_memory_space_constraint(x, pltpu.HBM)


def pack_kernel(q_hbm, k_hbm, v_hbm, z0, z1, z2, z3, ring_ref, view_ref, q_ref, k_ref, v_ref, sems, parts):
    place = lax.axis_index("f") % 4
    load = pltpu.make_async_copy(q_hbm, q_ref, sems.at[2])
    load.start()
    copy_all([(k_hbm, k_ref), (v_hbm, v_ref)], sems)
    for j in range(4):
        for i in range(5):
            parts[j, i * CELLS : (i + 1) * CELLS] = pair(k_ref, 5 * j + i, v_ref, 5 * j + i)
    for t in range(MAIN):
        view_ref[t, 0:CELLS] = pair(k_ref, t, v_ref, t)
    for y in range(RING):
        ring_ref[y] = pair(k_ref, MAIN + y, v_ref, MAIN + y)
    load.wait()
    for j in range(4):
        base = 5 * j
        for i in range(2):
            rows = slice((5 + i) * CELLS, (6 + i) * CELLS)
            parts[j, rows] = pair(q_ref, base + 2 * i, q_ref, base + 2 * i + 1)
        last = q_ref[:, (base + 4) * HEAD : (base + 5) * HEAD]
        parts[j, 896:960] = jnp.concatenate([last[0:64], last[64:128]], axis=1)
    for k, out in enumerate((z0, z1, z2, z3)):
        out[...] = parts[turned(place, k)]
    for t in range(MAIN):
        view_ref[t, CELLS : 2 * CELLS] = pair(q_ref, t, q_ref, MAIN + t % RING)


def pack(q, k, v):
    block = jax.ShapeDtypeStruct((Z_ROWS, CELLS), BF16)
    whole = pltpu.VMEM((CELLS, HEADS * HEAD), BF16)
    return pl.pallas_call(
        pack_kernel,
        out_shape=[block] * 4
        + [
            jax.ShapeDtypeStruct((RING, CELLS, CELLS), BF16),
            jax.ShapeDtypeStruct((MAIN, 2 * CELLS, CELLS), BF16),
        ],
        in_specs=[ANY] * 3,
        out_specs=[VMEM] * 6,
        scratch_shapes=[whole] * 3 + [pltpu.SemaphoreType.DMA((3,)), pltpu.VMEM((4, Z_ROWS, CELLS), BF16)],
        compiler_params=params(16),
        name="pack",
    )(in_hbm(q), in_hbm(k), in_hbm(v))


def ring_pack_kernel(ring_ref, sibling_ref, r0, r1, r2, r3):
    y = lax.axis_index("y")
    for k, out in enumerate((r0, r1, r2, r3)):
        out[0] = ring_ref[turned(y, k)]
        out[1] = sibling_ref[turned(y, k)]


def ring_pack(ring, other):
    return pl.pallas_call(
        ring_pack_kernel,
        out_shape=[jax.ShapeDtypeStruct((2, CELLS, CELLS), BF16)] * 4,
        in_specs=[VMEM] * 2,
        out_specs=[VMEM] * 4,
        compiler_params=params(4),
        name="ring_pack",
    )(ring, other)


def stack_kernel(z0, z1, z2, z3, *refs):
    out_ref = refs[-1]
    for k, piece in enumerate((z0, z1, z2, z3)):
        out_ref[k] = piece[0:X_ROWS]


def stack(z, order):
    return pl.pallas_call(
        stack_kernel,
        out_shape=jax.ShapeDtypeStruct((4, X_ROWS, CELLS), BF16),
        in_specs=[VMEM] * 4 + [ANY] * len(order),
        out_specs=VMEM,
        compiler_params=params(4),
        cost_estimate=pl.CostEstimate(flops=18000000000, bytes_accessed=100000, transcendentals=0),
        name="stack",
    )(*z, *order)


def keep_kernel(own_ref, *refs):
    kv_ref, sems = refs[-2:]
    copy_all([(own_ref.at[:, pl.ds(0, CELLS)], kv_ref)], sems)


def keep(own, order):
    return pl.pallas_call(
        keep_kernel,
        out_shape=jax.ShapeDtypeStruct((MAIN, CELLS, CELLS), BF16),
        in_specs=[ANY] * (1 + len(order)),
        out_specs=ANY,
        scratch_shapes=[pltpu.SemaphoreType.DMA((1,))],
        compiler_params=params(4),
        name="keep",
    )(own, *order)


def score_tile(q, key_ref, score_ref, count):
    best = None
    for start in range(0, count, CHUNK):
        s = lax.dot_general(
            q, key_ref[start : start + CHUNK], (((1,), (1,)), ((), ())), preferred_element_type=F32
        )
        score_ref[:, start : start + CHUNK] = s
        for lane in range(0, CHUNK, 128):
            part = s[:, lane : lane + 128]
            best = part if best is None else jnp.maximum(best, part)
    return jnp.max(best, axis=1, keepdims=True)


def weigh_tile(score_ref, row_max, value_ref, count):
    total = None
    for start in range(0, count, CHUNK):
        s = score_ref[:, start : start + CHUNK]
        w = jnp.exp2((s - row_max) * RATE).astype(BF16)
        part = jnp.dot(w, value_ref[start : start + CHUNK], preferred_element_type=F32)
        total = part if total is None else total + part
    return total


def split3(x):
    high = x.astype(BF16).astype(F32)
    middle = (x - high).astype(BF16).astype(F32)
    low = (x - high - middle).astype(BF16).astype(F32)
    return [high, middle, low]


def level_rows(levels, lane, at=0):
    columns = [part for level in levels for part in split3(level)]
    table = jnp.zeros_like(columns[0])
    for i, column in enumerate(columns):
        table = jnp.where(lane == at + i, column, table)
    return table


def row(x):
    return x.astype(BF16)


def seen_bias(mask_ref, key_view, count):
    core = lax.axis_index("c")
    seen = mask_ref[lax.axis_index("f")].astype(F32)
    pick = (lanes((count, 32)) == key_view).astype(F32)
    view, column = rows_of((32, 128)), lanes((32, 128)) - HEAD
    query_pick = ((column >= 0) & (column < 16) & (view == 2 * column + core)).astype(F32)
    by_key = lax.dot_general(pick, seen, (((1,), (1,)), ((), ())), preferred_element_type=F32)
    allowed = jnp.dot(by_key, query_pick, preferred_element_type=F32)
    column = lanes((count, 128)) - HEAD
    return row(jnp.where((column >= 0) & (column < 16) & (allowed < 0.5), NEG, 0.0))


def fill(key_s, value_s, at, kv, bias):
    rows = slice(at * CELLS, (at + 1) * CELLS)
    low = row(jnp.where(lanes((1, CELLS)) < HEAD, 1.0, 0.0))
    key_s[rows] = kv * low + bias
    value_s[rows] = kv * (1 - low) + low


def attend_views(own_ref, ring_ref, key_s, value_s, s_a, s_b, write):
    lane = lanes((CELLS, CELLS))
    wide = lanes((TILE, CELLS))

    def query(j):
        qq = own_ref[j, CELLS : 2 * CELLS].astype(F32)
        return jnp.where(lane < HEAD, qq, (lane == HEAD + j).astype(F32)).astype(BF16)

    def tile(i):
        return jnp.concatenate([query(2 * i), query(2 * i + 1)], axis=0)

    def finish(i, score_ref, row_max):
        main = weigh_tile(score_ref, row_max, value_s, 4096)
        heads = jnp.where(wide < HEAD, swap_halves(main) / main, 0.0)
        table = level_rows([row_max * RATE + jnp.log2(jnp.where(wide < HEAD, main, 1.0))], wide)
        for n in range(2):
            rows = slice(n * CELLS, (n + 1) * CELLS)
            j = 2 * i + n
            head_rows = ring_ref[j, 0:CELLS] + heads[rows].astype(BF16)
            write(j, head_rows, ring_ref[j, CELLS:O_ROWS] + table[rows].T[0:16].astype(BF16))

    start = score_tile(tile(0), key_s, s_a, 4096)

    def body(step, m_a):
        i = 2 * step
        m_b = score_tile(tile(i + 1), key_s, s_b, 4096)
        finish(i, s_a, m_a)
        m_next = score_tile(tile(jnp.minimum(i + 2, 7)), key_s, s_a, 4096)
        finish(i + 1, s_b, m_b)
        return m_next

    lax.fori_loop(0, 4, body, start)


def view_kernel(own_ref, other_ref, ring_ref, mask_ref, out_hbm, out_ref, sems, key_s, value_s, s_a, s_b):
    core = lax.axis_index("c")
    block = rows_of((32, 32))
    bias = seen_bias(mask_ref, jnp.where(block < 16, 2 * block + core, 2 * (block - 16) + 1 - core), 32)
    for b in range(32):
        kv = own_ref[b, 0:CELLS] if b < 16 else other_ref[b - 16]
        fill(key_s, value_s, b, kv, bias[b : b + 1])

    def away(j):
        return pltpu.make_async_copy(out_ref.at[j], out_hbm.at[j], sems.at[j])

    def write(j, head_rows, level_part):
        out_ref[j, 0:CELLS] = head_rows
        out_ref[j, CELLS:O_ROWS] = level_part
        away(j).start()

    attend_views(own_ref, ring_ref, key_s, value_s, s_a, s_b, write)
    for j in range(MAIN):
        away(j).wait()


def view_attention(own, other, ring_out, view_mask):
    rows = pltpu.VMEM((4096, CELLS), BF16)
    scores = pltpu.VMEM((TILE, 4096), F32)
    return pl.pallas_call(
        view_kernel,
        out_shape=pltpu.HBM((MAIN, O_ROWS, CELLS), BF16),
        in_specs=[VMEM] * 4,
        out_specs=ANY,
        scratch_shapes=[
            pltpu.VMEM((MAIN, O_ROWS, CELLS), BF16),
            pltpu.SemaphoreType.DMA((MAIN,)),
            rows,
            rows,
            scores,
            scores,
        ],
        compiler_params=params(20),
        cost_estimate=pl.CostEstimate(flops=1000000, bytes_accessed=100000, transcendentals=0),
        name="view_attention",
    )(own, other, ring_out, view_mask)


def ring_kernel(own_ref, r0, r1, r2, r3, mask_ref, out_ref, key_s, value_s, s_ref):
    core = lax.axis_index("c")
    y = lax.axis_index("y")
    ring = lax.axis_index("g") * 2 + lax.axis_index("zl")
    lane = lanes((CELLS, CELLS))
    block = rows_of((8, 32))
    side = jnp.where(block % 2 == 0, core, 1 - core)
    bias = seen_bias(mask_ref, ring * 8 + 2 * (y ^ (block // 2)) + side, 8)
    for k, piece in enumerate((r0, r1, r2, r3)):
        for n in range(2):
            fill(key_s, value_s, 2 * k + n, piece[n], bias[2 * k + n : 2 * k + n + 1])

    def query(j):
        qq = swap_halves(own_ref[j, CELLS : 2 * CELLS].astype(F32))
        return jnp.where(lane < HEAD, qq, (lane == HEAD + j).astype(F32)).astype(BF16)

    wide = lanes((TILE, CELLS))

    def begin(i):
        tile = jnp.concatenate([query(2 * i), query(2 * i + 1)], axis=0)
        return score_tile(tile, key_s, s_ref.at[i % 2], 1024)

    row_max = begin(0)
    for i in range(8):
        following = begin(i + 1) if i < 7 else None
        part = weigh_tile(s_ref.at[i % 2], row_max, value_s, 1024)
        heads = jnp.where(wide < HEAD, 0.0, part / swap_halves(part)).astype(BF16)
        level = row_max * RATE + jnp.log2(jnp.where(wide < HEAD, part, 1.0))
        table = level_rows([level], wide, 3)
        for n in range(2):
            rows = slice(n * CELLS, (n + 1) * CELLS)
            j = 2 * i + n
            out_ref[j, 0:CELLS] = heads[rows]
            out_ref[j, CELLS:O_ROWS] = table[rows].T[0:16].astype(BF16)
        row_max = following


def ring_attention(own, pieces, view_mask):
    return pl.pallas_call(
        ring_kernel,
        out_shape=jax.ShapeDtypeStruct((MAIN, O_ROWS, CELLS), BF16),
        in_specs=[VMEM] * 6,
        out_specs=VMEM,
        scratch_shapes=[
            pltpu.VMEM((1024, CELLS), BF16),
            pltpu.VMEM((1024, CELLS), BF16),
            pltpu.VMEM((2, TILE, 1024), F32),
        ],
        compiler_params=params(12),
        cost_estimate=pl.CostEstimate(flops=1000000, bytes_accessed=100000, transcendentals=0),
        name="ring_attention",
    )(own, *pieces, view_mask)


def time_kernel(z0, z1, z2, z3, x_ref, times_ref, o0, o1, o2, o3, key_s, value_s, q_s, s_ref):
    frame = lax.axis_index("f")
    lane = lanes((CELLS, CELLS))
    own = (z0, z1, z2, z3)
    far = tuple(x_ref.at[k] for k in range(4))
    outs = (o0, o1, o2, o3)

    l8, r8 = lanes((8, 128)), rows_of((8, 128))
    query_time = jnp.zeros((8, 128), jnp.int32)
    key_time = jnp.zeros((8, 128), jnp.int32)
    for k in range(FRAMES):
        now = times_ref[frame ^ k]
        query_time = jnp.where(l8 == HEAD + k, now, query_time)
        key_time = jnp.where(r8 == k, now, key_time)
    near = (jnp.abs(query_time - key_time) <= REACH) & (l8 - HEAD != r8)
    bias = row(jnp.where((l8 >= HEAD) & (l8 < HEAD + 4) & jnp.logical_not(near), NEG, 0.0))
    low = row(jnp.where(lanes((1, CELLS)) < HEAD, 1.0, 0.0))
    high = row(jnp.where(lanes((1, CELLS)) < HEAD, 0.0, 1.0))

    for head in range(5):
        for k in range(8):
            at = slice(head * CELLS, (head + 1) * CELLS)
            kv = (own + far)[k][at]
            rows = slice(k * CELLS, (k + 1) * CELLS)
            key_s[head, rows] = kv * low + bias[k : k + 1]
            value_s[head, rows] = kv * high + low
    for k in range(4):
        rows = slice(k * CELLS, (k + 1) * CELLS)
        hot = jnp.where(lane == HEAD + k, 1.0, 0.0)
        for i in range(2):
            qq = own[k][(5 + i) * CELLS : (6 + i) * CELLS].astype(F32)
            q_s[2 * i, rows] = jnp.where(lane < HEAD, qq, hot).astype(BF16)
            q_s[2 * i + 1, rows] = jnp.where(lane < HEAD, swap_halves(qq), hot).astype(BF16)
        packed = own[k][896:960].astype(F32)
        qq = jnp.concatenate([packed, swap_halves(packed)], axis=0)
        q_s[4, rows] = jnp.where(lane < HEAD, qq, hot).astype(BF16)

    wide = lanes((TILE, CELLS))
    work = [(i, head) for i in range(2) for head in range(5)]

    def begin(n):
        i, head = work[n]
        return score_tile(q_s[head, i * TILE : (i + 1) * TILE], key_s.at[head], s_ref.at[n % 2], 1024)

    row_max = begin(0)
    heads, levels = [], []
    for n, (i, head) in enumerate(work):
        following = begin(n + 1) if n + 1 < len(work) else None
        total = weigh_tile(s_ref.at[n % 2], row_max, value_s.at[head], 1024)
        sums = swap_halves(total)
        if head % 2 == 0:
            heads.append(jnp.where(wide < HEAD, sums / total, 0.0))
        else:
            heads.append(jnp.where(wide < HEAD, 0.0, total / sums))
        levels.append(row_max * RATE + jnp.log2(jnp.where(wide < HEAD, total, 1.0)))
        row_max = following
        if head < 4:
            continue
        table = level_rows(levels, wide)
        for m in range(2):
            rows = slice(m * CELLS, (m + 1) * CELLS)
            out = outs[2 * i + m]
            out[0:128] = (heads[0] + heads[1])[rows].astype(BF16)
            out[128:256] = (heads[2] + heads[3])[rows].astype(BF16)
            last = heads[4][rows]
            out[256:320] = (last[0:64] + swap_halves(last[64:128])).astype(BF16)
            out[320:336] = table[rows].T[0:16].astype(BF16)
        heads, levels = [], []


def time_attention(own, crossed, frame_times):
    return pl.pallas_call(
        time_kernel,
        out_shape=[jax.ShapeDtypeStruct((T_ROWS, CELLS), BF16)] * 4,
        in_specs=[VMEM] * 5 + [SMEM],
        out_specs=[VMEM] * 4,
        scratch_shapes=[
            pltpu.VMEM((5, 1024, CELLS), BF16),
            pltpu.VMEM((5, 1024, CELLS), BF16),
            pltpu.VMEM((5, 512, CELLS), BF16),
            pltpu.VMEM((2, TILE, 1024), F32),
        ],
        compiler_params=params(16),
        cost_estimate=pl.CostEstimate(flops=700000000, bytes_accessed=2000000, transcendentals=2700000),
        name="time_attention",
    )(*own, crossed, frame_times)


def pass_kernel(*refs):
    del refs


def pass_after(array, others):
    return pl.pallas_call(
        pass_kernel,
        out_shape=pltpu.HBM(array.shape, array.dtype),
        in_specs=[ANY] * (1 + len(others)),
        out_specs=ANY,
        input_output_aliases={0: 0},
        compiler_params=params(4),
        name="pass_after",
    )(in_hbm(array), *others)


def join_kernel(view_ref, t0, t1, t2, t3, weight_any, out_ref, times, heads_s, weight_ref, sems):
    load = pltpu.make_async_copy(weight_any, weight_ref, sems.at[0])
    load.start()
    place = lax.axis_index("f") % 4
    for k, piece in enumerate((t0, t1, t2, t3)):
        times[turned(place, k)] = piece[...]

    view_rows = jnp.concatenate([view_ref[t, CELLS:O_ROWS] for t in range(MAIN)], axis=0)
    time_rows = jnp.concatenate([times[j, 320:336] for j in range(4)], axis=0)

    def levels(rows, picked):
        pick = jnp.where(picked, 1.0, 0.0).astype(BF16)
        return lax.dot_general(rows, pick, (((0,), (0,)), ((), ())), preferred_element_type=F32)

    at, head = rows_of((256, 128)), lanes((256, 128))
    source, part = at // 16, at % 16
    found = []
    for ring in range(4):
        picked = (head >= MAIN) & (source == 4 * ring + head - MAIN) & (part >= 3) & (part < 6)
        if ring == 0:
            picked = picked | ((head < MAIN) & (source == head) & (part < 3))
        found.append(levels(view_rows, picked))
    at, head = rows_of((64, 128)), lanes((64, 128))
    offset = at % 16 - 3 * (head - 5 * (at // 16))
    inside = (head >= 5 * (at // 16)) & (head < 5 * (at // 16) + 5)
    found.append(levels(time_rows, inside & (offset >= 0) & (offset < 3)))
    column = lanes((CELLS, CELLS))
    for ring in range(1, 4):
        found[ring] = jnp.where(column < MAIN, -1e30, found[ring])
    best = found[0]
    for value in found[1:]:
        best = jnp.maximum(best, value)
    powers = [jnp.exp2(value - best) for value in found]
    total = powers[0]
    for power in powers[1:]:
        total = total + power
    shares = [power / total for power in powers]

    def time_block(head):
        j, i = head // 5, head % 5
        if i < 4:
            rows = slice((i // 2) * CELLS, (i // 2 + 1) * CELLS)
            return times[j, rows, (i % 2) * HEAD : (i % 2 + 1) * HEAD].astype(F32)
        packed = times[j, 256:320].astype(F32)
        return jnp.concatenate([packed[:, 0:HEAD], packed[:, HEAD:128]], axis=0)

    load.wait()
    result = None
    for first in range(0, HEADS, 4):
        for h in range(first, first + 4):
            mixed = time_block(h) * shares[4][:, h : h + 1]
            if h < MAIN:
                mixed += view_ref[h, 0:CELLS, 0:HEAD].astype(F32) * shares[0][:, h : h + 1]
            else:
                for ring in range(4):
                    block = view_ref[4 * ring + h - MAIN, 0:CELLS, HEAD:128].astype(F32)
                    mixed += block * shares[ring][:, h : h + 1]
            heads_s[:, h * HEAD : (h + 1) * HEAD] = mixed.astype(BF16)
        columns = slice(first * HEAD, (first + 4) * HEAD)
        product = jnp.dot(heads_s[:, columns], weight_ref[columns], preferred_element_type=F32)
        result = product if result is None else result + product
    out_ref[...] = result.astype(BF16)


def join(view_out, pieces, out_weight):
    return pl.pallas_call(
        join_kernel,
        out_shape=jax.ShapeDtypeStruct((CELLS, HEADS * HEAD), BF16),
        in_specs=[VMEM] * 5 + [ANY],
        out_specs=VMEM,
        scratch_shapes=[
            pltpu.VMEM((4, T_ROWS, CELLS), BF16),
            pltpu.VMEM((CELLS, HEADS * HEAD), BF16),
            pltpu.VMEM((HEADS * HEAD, HEADS * HEAD), BF16),
            pltpu.SemaphoreType.DMA((1,)),
        ],
        compiler_params=params(16),
        name="join",
    )(view_out, *pieces, in_hbm(out_weight))


def across(array, k):
    return lax.ppermute(array, "f", [(i, i ^ k) for i in range(FRAMES)])


def around(array, k):
    return lax.ppermute(array, "y", [(i, i ^ k) for i in range(RING)])


def sibling(array):
    return lax.ppermute(array, "c", [(0, 1), (1, 0)])


def local(queries, keys, values, view_mask, frame_times, out_weight):
    model = queries.shape[3]
    q, k, v = (a.reshape(CELLS, model) for a in (queries, keys, values))
    *z, to_ring, to_view = pack(q, k, v)
    own = lax.all_to_all(to_view, ("g", "zl", "y"), 0, 0)
    z = [z[0]] + [across(z[i], i) for i in (1, 2, 3)]
    ring = ring_pack(to_ring, sibling(to_ring))
    ring = [ring[0]] + [around(ring[i], i) for i in (1, 2, 3)]
    some = stack(z, ring[1:])
    crossed = across(some, 4)
    other = sibling(keep(own, [some]))
    ring_out = ring_attention(own, ring, view_mask)
    view_out = view_attention(own, other, ring_out, view_mask)
    view_out = pass_after(view_out, (crossed,))
    view_back = lax.all_to_all(view_out, ("g", "zl", "y"), 0, 0)
    pieces = time_attention(z, crossed, frame_times)
    pieces = [pieces[0]] + [across(pieces[i], i) for i in (1, 2, 3)]
    result = join(view_back, pieces, out_weight)
    return result.reshape(1, 1, CELLS, model)


def solution(mesh):
    fine = Mesh(mesh.devices.reshape(2, 8, 2, 4, 2), ("g", "f", "zl", "y", "c"))
    blocks = P(("g", "f"), ("zl", "y", "c"), None, None)
    return jax.shard_map(
        local,
        mesh=fine,
        in_specs=(blocks, blocks, blocks, P(), P(), P()),
        out_specs=blocks,
        check_vma=False,
    )
```

```python
import jax
import jax.numpy as jnp
from jax import lax
from jax.experimental import pallas as pl
from jax.experimental.pallas import tpu as pltpu
from jax.sharding import Mesh, PartitionSpec as P

HEADS = 20
REACH = 4
FRAMES = 8
HEAD = 64
CELLS = 128
MAIN = 16
RING = 4
NEG = -(2.0**30)
LOG2E = 1.4426950408889634
RATE = HEAD**-0.5 * LOG2E
TILE = 256
CHUNK = 512
Z_ROWS = 960
X_ROWS = 640
T_ROWS = 336
O_ROWS = 144
F32 = jnp.float32
BF16 = jnp.bfloat16
ANY = pl.BlockSpec(memory_space=pl.ANY)
VMEM = pl.BlockSpec(memory_space=pltpu.VMEM)
SMEM = pl.BlockSpec(memory_space=pltpu.SMEM)


def lanes(shape):
    return lax.broadcasted_iota(jnp.int32, shape, len(shape) - 1)


def rows_of(shape):
    return lax.broadcasted_iota(jnp.int32, shape, len(shape) - 2)


def swap_halves(x):
    return pltpu.roll(x, HEAD, 1)


def params(mib):
    return pltpu.CompilerParams(vmem_limit_bytes=mib * 1024 * 1024)


def turned(index, k):
    return (index, index + 1 - 2 * (index % 2), (index + 2) % 4, 3 - index)[k]


def copy_all(moves, sems):
    copies = [pltpu.make_async_copy(source, target, sems.at[i]) for i, (source, target) in enumerate(moves)]
    for copy in copies:
        copy.start()
    for copy in copies:
        copy.wait()


def pair(a_ref, a, b_ref, b):
    left = a_ref[:, a * HEAD : (a + 1) * HEAD]
    right = b_ref[:, b * HEAD : (b + 1) * HEAD]
    return jnp.concatenate([left, right], axis=1)


def in_hbm(x):
    return pltpu.with_memory_space_constraint(x, pltpu.HBM)


def pack_kernel(q_hbm, k_hbm, v_hbm, x0, z0, z1, z2, z3, ring_ref, view_ref, q_ref, k_ref, v_ref, sems, parts):
    place = lax.axis_index("f") % 4
    load = pltpu.make_async_copy(q_hbm, q_ref, sems.at[2])
    load.start()
    copy_all([(k_hbm, k_ref), (v_hbm, v_ref)], sems)
    for j in range(4):
        for i in range(5):
            parts[j, i * CELLS : (i + 1) * CELLS] = pair(k_ref, 5 * j + i, v_ref, 5 * j + i)
    for t in range(MAIN):
        view_ref[t, 0:CELLS] = pair(k_ref, t, v_ref, t)
    for y in range(RING):
        ring_ref[y] = pair(k_ref, MAIN + y, v_ref, MAIN + y)
    load.wait()
    for j in range(4):
        base = 5 * j
        for i in range(2):
            rows = slice((5 + i) * CELLS, (6 + i) * CELLS)
            parts[j, rows] = pair(q_ref, base + 2 * i, q_ref, base + 2 * i + 1)
        last = q_ref[:, (base + 4) * HEAD : (base + 5) * HEAD]
        parts[j, 896:960] = jnp.concatenate([last[0:64], last[64:128]], axis=1)
    for k, out in enumerate((z0, z1, z2, z3)):
        out[...] = parts[turned(place, k)]
    x0[...] = z0[0:X_ROWS]
    for t in range(MAIN):
        view_ref[t, CELLS : 2 * CELLS] = pair(q_ref, t, q_ref, MAIN + t % RING)


def pack(q, k, v):
    block = jax.ShapeDtypeStruct((Z_ROWS, CELLS), BF16)
    whole = pltpu.VMEM((CELLS, HEADS * HEAD), BF16)
    return pl.pallas_call(
        pack_kernel,
        out_shape=[jax.ShapeDtypeStruct((X_ROWS, CELLS), BF16)]
        + [block] * 4
        + [
            jax.ShapeDtypeStruct((RING, CELLS, CELLS), BF16),
            jax.ShapeDtypeStruct((MAIN, 2 * CELLS, CELLS), BF16),
        ],
        in_specs=[ANY] * 3,
        out_specs=[VMEM] * 7,
        scratch_shapes=[whole] * 3 + [pltpu.SemaphoreType.DMA((3,)), pltpu.VMEM((4, Z_ROWS, CELLS), BF16)],
        compiler_params=params(16),
        name="pack",
    )(in_hbm(q), in_hbm(k), in_hbm(v))


def ring_pack_kernel(ring_ref, sibling_ref, r0, r1, r2, r3):
    y = lax.axis_index("y")
    for k, out in enumerate((r0, r1, r2, r3)):
        out[0] = ring_ref[turned(y, k)]
        out[1] = sibling_ref[turned(y, k)]


def ring_pack(ring, other):
    return pl.pallas_call(
        ring_pack_kernel,
        out_shape=[jax.ShapeDtypeStruct((2, CELLS, CELLS), BF16)] * 4,
        in_specs=[VMEM] * 2,
        out_specs=[VMEM] * 4,
        compiler_params=params(4),
        name="ring_pack",
    )(ring, other)


def strip_kernel(z_ref, *refs):
    refs[-1][...] = z_ref[0:X_ROWS]


def strip(z, order=()):
    return pl.pallas_call(
        strip_kernel,
        out_shape=jax.ShapeDtypeStruct((X_ROWS, CELLS), BF16),
        in_specs=[VMEM] + [ANY] * len(order),
        out_specs=VMEM,
        compiler_params=params(4),
        name="strip",
    )(z, *order)


def keep_kernel(own_ref, *refs):
    kv_ref, sems = refs[-2:]
    copy_all([(own_ref.at[:, pl.ds(0, CELLS)], kv_ref)], sems)


def keep(own, order):
    return pl.pallas_call(
        keep_kernel,
        out_shape=jax.ShapeDtypeStruct((MAIN, CELLS, CELLS), BF16),
        in_specs=[ANY] * (1 + len(order)),
        out_specs=ANY,
        scratch_shapes=[pltpu.SemaphoreType.DMA((1,))],
        compiler_params=params(4),
        name="keep",
    )(own, *order)


def score_tile(q, key_ref, score_ref, count):
    best = None
    for start in range(0, count, CHUNK):
        s = lax.dot_general(
            q, key_ref[start : start + CHUNK], (((1,), (1,)), ((), ())), preferred_element_type=F32
        )
        score_ref[:, start : start + CHUNK] = s
        for lane in range(0, CHUNK, 128):
            part = s[:, lane : lane + 128]
            best = part if best is None else jnp.maximum(best, part)
    return jnp.max(best, axis=1, keepdims=True)


def weigh_tile(score_ref, row_max, value_ref, count):
    total = None
    for start in range(0, count, CHUNK):
        s = score_ref[:, start : start + CHUNK]
        w = jnp.exp2((s - row_max) * RATE).astype(BF16)
        part = jnp.dot(w, value_ref[start : start + CHUNK], preferred_element_type=F32)
        total = part if total is None else total + part
    return total


def split3(x):
    high = x.astype(BF16).astype(F32)
    middle = (x - high).astype(BF16).astype(F32)
    low = (x - high - middle).astype(BF16).astype(F32)
    return [high, middle, low]


def level_rows(levels, lane, at=0):
    columns = [part for level in levels for part in split3(level)]
    table = jnp.zeros_like(columns[0])
    for i, column in enumerate(columns):
        table = jnp.where(lane == at + i, column, table)
    return table


def row(x):
    return x.astype(BF16)


def seen_bias(mask_ref, key_view, count):
    core = lax.axis_index("c")
    seen = mask_ref[lax.axis_index("f")].astype(F32)
    pick = (lanes((count, 32)) == key_view).astype(F32)
    view, column = rows_of((32, 128)), lanes((32, 128)) - HEAD
    query_pick = ((column >= 0) & (column < 16) & (view == 2 * column + core)).astype(F32)
    by_key = lax.dot_general(pick, seen, (((1,), (1,)), ((), ())), preferred_element_type=F32)
    allowed = jnp.dot(by_key, query_pick, preferred_element_type=F32)
    column = lanes((count, 128)) - HEAD
    return row(jnp.where((column >= 0) & (column < 16) & (allowed < 0.5), NEG, 0.0))


def fill(key_s, value_s, at, kv, bias):
    rows = slice(at * CELLS, (at + 1) * CELLS)
    low = row(jnp.where(lanes((1, CELLS)) < HEAD, 1.0, 0.0))
    key_s[rows] = kv * low + bias
    value_s[rows] = kv * (1 - low) + low


def attend_views(own_ref, ring_ref, key_s, value_s, s_a, s_b, write):
    lane = lanes((CELLS, CELLS))
    wide = lanes((TILE, CELLS))

    def query(j):
        qq = own_ref[j, CELLS : 2 * CELLS].astype(F32)
        return jnp.where(lane < HEAD, qq, (lane == HEAD + j).astype(F32)).astype(BF16)

    def tile(i):
        return jnp.concatenate([query(2 * i), query(2 * i + 1)], axis=0)

    def finish(i, score_ref, row_max):
        main = weigh_tile(score_ref, row_max, value_s, 4096)
        heads = jnp.where(wide < HEAD, swap_halves(main) / main, 0.0)
        table = level_rows([row_max * RATE + jnp.log2(jnp.where(wide < HEAD, main, 1.0))], wide)
        for n in range(2):
            rows = slice(n * CELLS, (n + 1) * CELLS)
            j = 2 * i + n
            head_rows = ring_ref[j, 0:CELLS] + heads[rows].astype(BF16)
            write(j, head_rows, ring_ref[j, CELLS:O_ROWS] + table[rows].T[0:16].astype(BF16))

    start = score_tile(tile(0), key_s, s_a, 4096)

    def body(step, m_a):
        i = 2 * step
        m_b = score_tile(tile(i + 1), key_s, s_b, 4096)
        finish(i, s_a, m_a)
        m_next = score_tile(tile(jnp.minimum(i + 2, 7)), key_s, s_a, 4096)
        finish(i + 1, s_b, m_b)
        return m_next

    lax.fori_loop(0, 4, body, start)


def view_kernel(own_ref, other_ref, ring_ref, mask_ref, out_hbm, out_ref, sems, key_s, value_s, s_a, s_b):
    core = lax.axis_index("c")
    block = rows_of((32, 32))
    bias = seen_bias(mask_ref, jnp.where(block < 16, 2 * block + core, 2 * (block - 16) + 1 - core), 32)
    for b in range(32):
        kv = own_ref[b, 0:CELLS] if b < 16 else other_ref[b - 16]
        fill(key_s, value_s, b, kv, bias[b : b + 1])

    def away(j):
        return pltpu.make_async_copy(out_ref.at[j], out_hbm.at[j], sems.at[j])

    def write(j, head_rows, level_part):
        out_ref[j, 0:CELLS] = head_rows
        out_ref[j, CELLS:O_ROWS] = level_part
        away(j).start()

    attend_views(own_ref, ring_ref, key_s, value_s, s_a, s_b, write)
    for j in range(MAIN):
        away(j).wait()


def view_attention(own, other, ring_out, view_mask):
    rows = pltpu.VMEM((4096, CELLS), BF16)
    scores = pltpu.VMEM((TILE, 4096), F32)
    return pl.pallas_call(
        view_kernel,
        out_shape=pltpu.HBM((MAIN, O_ROWS, CELLS), BF16),
        in_specs=[VMEM] * 4,
        out_specs=ANY,
        scratch_shapes=[
            pltpu.VMEM((MAIN, O_ROWS, CELLS), BF16),
            pltpu.SemaphoreType.DMA((MAIN,)),
            rows,
            rows,
            scores,
            scores,
        ],
        compiler_params=params(20),
        cost_estimate=pl.CostEstimate(flops=1000000, bytes_accessed=100000, transcendentals=0),
        name="view_attention",
    )(own, other, ring_out, view_mask)


def ring_kernel(own_ref, r0, r1, r2, r3, mask_ref, out_ref, key_s, value_s, s_ref):
    core = lax.axis_index("c")
    y = lax.axis_index("y")
    ring = lax.axis_index("g") * 2 + lax.axis_index("zl")
    lane = lanes((CELLS, CELLS))
    block = rows_of((8, 32))
    side = jnp.where(block % 2 == 0, core, 1 - core)
    bias = seen_bias(mask_ref, ring * 8 + 2 * (y ^ (block // 2)) + side, 8)
    for k, piece in enumerate((r0, r1, r2, r3)):
        for n in range(2):
            fill(key_s, value_s, 2 * k + n, piece[n], bias[2 * k + n : 2 * k + n + 1])

    def query(j):
        qq = swap_halves(own_ref[j, CELLS : 2 * CELLS].astype(F32))
        return jnp.where(lane < HEAD, qq, (lane == HEAD + j).astype(F32)).astype(BF16)

    wide = lanes((TILE, CELLS))

    def begin(i):
        tile = jnp.concatenate([query(2 * i), query(2 * i + 1)], axis=0)
        return score_tile(tile, key_s, s_ref.at[i % 2], 1024)

    row_max = begin(0)
    for i in range(8):
        following = begin(i + 1) if i < 7 else None
        part = weigh_tile(s_ref.at[i % 2], row_max, value_s, 1024)
        heads = jnp.where(wide < HEAD, 0.0, part / swap_halves(part)).astype(BF16)
        level = row_max * RATE + jnp.log2(jnp.where(wide < HEAD, part, 1.0))
        table = level_rows([level], wide, 3)
        for n in range(2):
            rows = slice(n * CELLS, (n + 1) * CELLS)
            j = 2 * i + n
            out_ref[j, 0:CELLS] = heads[rows]
            out_ref[j, CELLS:O_ROWS] = table[rows].T[0:16].astype(BF16)
        row_max = following


def ring_attention(own, pieces, view_mask):
    return pl.pallas_call(
        ring_kernel,
        out_shape=jax.ShapeDtypeStruct((MAIN, O_ROWS, CELLS), BF16),
        in_specs=[VMEM] * 6,
        out_specs=VMEM,
        scratch_shapes=[
            pltpu.VMEM((1024, CELLS), BF16),
            pltpu.VMEM((1024, CELLS), BF16),
            pltpu.VMEM((2, TILE, 1024), F32),
        ],
        compiler_params=params(12),
        cost_estimate=pl.CostEstimate(flops=1000000, bytes_accessed=100000, transcendentals=0),
        name="ring_attention",
    )(own, *pieces, view_mask)


def time_kernel(z0, z1, z2, z3, x0, x1, x2, x3, times_ref, o0, o1, o2, o3, key_s, value_s, q_s, s_ref):
    frame = lax.axis_index("f")
    lane = lanes((CELLS, CELLS))
    own = (z0, z1, z2, z3)
    far = (x0, x1, x2, x3)
    outs = (o0, o1, o2, o3)

    l8, r8 = lanes((8, 128)), rows_of((8, 128))
    query_time = jnp.zeros((8, 128), jnp.int32)
    key_time = jnp.zeros((8, 128), jnp.int32)
    for k in range(FRAMES):
        now = times_ref[frame ^ k]
        query_time = jnp.where(l8 == HEAD + k, now, query_time)
        key_time = jnp.where(r8 == k, now, key_time)
    near = (jnp.abs(query_time - key_time) <= REACH) & (l8 - HEAD != r8)
    bias = row(jnp.where((l8 >= HEAD) & (l8 < HEAD + 4) & jnp.logical_not(near), NEG, 0.0))
    low = row(jnp.where(lanes((1, CELLS)) < HEAD, 1.0, 0.0))
    high = row(jnp.where(lanes((1, CELLS)) < HEAD, 0.0, 1.0))

    for head in range(5):
        for k in range(8):
            at = slice(head * CELLS, (head + 1) * CELLS)
            kv = (own + far)[k][at]
            rows = slice(k * CELLS, (k + 1) * CELLS)
            key_s[head, rows] = kv * low + bias[k : k + 1]
            value_s[head, rows] = kv * high + low
    for k in range(4):
        rows = slice(k * CELLS, (k + 1) * CELLS)
        hot = jnp.where(lane == HEAD + k, 1.0, 0.0)
        for i in range(2):
            qq = own[k][(5 + i) * CELLS : (6 + i) * CELLS].astype(F32)
            q_s[2 * i, rows] = jnp.where(lane < HEAD, qq, hot).astype(BF16)
            q_s[2 * i + 1, rows] = jnp.where(lane < HEAD, swap_halves(qq), hot).astype(BF16)
        packed = own[k][896:960].astype(F32)
        qq = jnp.concatenate([packed, swap_halves(packed)], axis=0)
        q_s[4, rows] = jnp.where(lane < HEAD, qq, hot).astype(BF16)

    wide = lanes((TILE, CELLS))
    work = [(i, head) for i in range(2) for head in range(5)]

    def begin(n):
        i, head = work[n]
        return score_tile(q_s[head, i * TILE : (i + 1) * TILE], key_s.at[head], s_ref.at[n % 2], 1024)

    row_max = begin(0)
    heads, levels = [], []
    for n, (i, head) in enumerate(work):
        following = begin(n + 1) if n + 1 < len(work) else None
        total = weigh_tile(s_ref.at[n % 2], row_max, value_s.at[head], 1024)
        sums = swap_halves(total)
        if head % 2 == 0:
            heads.append(jnp.where(wide < HEAD, sums / total, 0.0))
        else:
            heads.append(jnp.where(wide < HEAD, 0.0, total / sums))
        levels.append(row_max * RATE + jnp.log2(jnp.where(wide < HEAD, total, 1.0)))
        row_max = following
        if head < 4:
            continue
        table = level_rows(levels, wide)
        for m in range(2):
            rows = slice(m * CELLS, (m + 1) * CELLS)
            out = outs[2 * i + m]
            out[0:128] = (heads[0] + heads[1])[rows].astype(BF16)
            out[128:256] = (heads[2] + heads[3])[rows].astype(BF16)
            last = heads[4][rows]
            out[256:320] = (last[0:64] + swap_halves(last[64:128])).astype(BF16)
            out[320:336] = table[rows].T[0:16].astype(BF16)
        heads, levels = [], []


def time_attention(own, crossed, frame_times):
    return pl.pallas_call(
        time_kernel,
        out_shape=[jax.ShapeDtypeStruct((T_ROWS, CELLS), BF16)] * 4,
        in_specs=[VMEM] * 8 + [SMEM],
        out_specs=[VMEM] * 4,
        scratch_shapes=[
            pltpu.VMEM((5, 1024, CELLS), BF16),
            pltpu.VMEM((5, 1024, CELLS), BF16),
            pltpu.VMEM((5, 512, CELLS), BF16),
            pltpu.VMEM((2, TILE, 1024), F32),
        ],
        compiler_params=params(16),
        cost_estimate=pl.CostEstimate(flops=17000000000, bytes_accessed=2000000, transcendentals=2700000),
        name="time_attention",
    )(*own, *crossed, frame_times)


def join_kernel(view_ref, t0, t1, t2, t3, weight_any, out_ref, times, heads_s, weight_ref, sems):
    chunks = [pl.ds(i * 256, 256) for i in range(5)]
    loads = [pltpu.make_async_copy(weight_any.at[c], weight_ref.at[c], sems.at[i]) for i, c in enumerate(chunks)]
    for load in loads:
        load.start()
    place = lax.axis_index("f") % 4
    for k, piece in enumerate((t0, t1, t2, t3)):
        times[turned(place, k)] = piece[...]

    view_rows = jnp.concatenate([view_ref[t, CELLS:O_ROWS] for t in range(MAIN)], axis=0)
    time_rows = jnp.concatenate([times[j, 320:336] for j in range(4)], axis=0)

    def levels(rows, picked):
        pick = jnp.where(picked, 1.0, 0.0).astype(BF16)
        return lax.dot_general(rows, pick, (((0,), (0,)), ((), ())), preferred_element_type=F32)

    at, head = rows_of((256, 128)), lanes((256, 128))
    source, part = at // 16, at % 16
    found = []
    for ring in range(4):
        picked = (head >= MAIN) & (source == 4 * ring + head - MAIN) & (part >= 3) & (part < 6)
        if ring == 0:
            picked = picked | ((head < MAIN) & (source == head) & (part < 3))
        found.append(levels(view_rows, picked))
    at, head = rows_of((64, 128)), lanes((64, 128))
    offset = at % 16 - 3 * (head - 5 * (at // 16))
    inside = (head >= 5 * (at // 16)) & (head < 5 * (at // 16) + 5)
    found.append(levels(time_rows, inside & (offset >= 0) & (offset < 3)))
    column = lanes((CELLS, CELLS))
    for ring in range(1, 4):
        found[ring] = jnp.where(column < MAIN, -1e30, found[ring])
    best = found[0]
    for value in found[1:]:
        best = jnp.maximum(best, value)
    powers = [jnp.exp2(value - best) for value in found]
    total = powers[0]
    for power in powers[1:]:
        total = total + power
    shares = [power / total for power in powers]

    def spread(share, first, count):
        pick = lanes((CELLS, count * HEAD)) // HEAD + first == rows_of((CELLS, count * HEAD))
        pick = jnp.where(pick, 1.0, 0.0).astype(BF16)
        high = share.astype(BF16)
        rest = (share - high.astype(F32)).astype(BF16)
        return jnp.dot(high, pick, preferred_element_type=F32) + jnp.dot(rest, pick, preferred_element_type=F32)

    view_share, time_share = spread(shares[0], 0, HEADS), spread(shares[4], 0, HEADS)
    ring_share = [view_share[:, MAIN * HEAD :]] + [spread(shares[ring], MAIN, RING) for ring in (1, 2, 3)]
    left = column < HEAD

    def time_half(head, side):
        j, i = head // 5, head % 5
        if i < 4:
            block = times[j, (i // 2) * CELLS : (i // 2 + 1) * CELLS].astype(F32)
            return block if i % 2 == side else swap_halves(block)
        packed = times[j, 256:320].astype(F32)
        turn = swap_halves(packed)
        return jnp.concatenate([turn, packed] if side else [packed, turn], axis=0)

    def view_half(head, ring, side):
        if head < MAIN:
            block = view_ref[head, 0:CELLS].astype(F32)
            return swap_halves(block) if side else block
        block = view_ref[4 * ring + head - MAIN, 0:CELLS].astype(F32)
        return block if side else swap_halves(block)

    result = None
    for step in range(5):
        for p in (2 * step, 2 * step + 1):
            here = slice(p * CELLS, (p + 1) * CELLS)
            mixed = jnp.where(left, time_half(2 * p, 0), time_half(2 * p + 1, 1)) * time_share[:, here]
            for ring in range(1 if p < 8 else 4):
                block = jnp.where(left, view_half(2 * p, ring, 0), view_half(2 * p + 1, ring, 1))
                share = view_share[:, here] if p < 8 else ring_share[ring][:, (p - 8) * CELLS : (p - 7) * CELLS]
                mixed += block * share
            heads_s[:, here] = mixed.astype(BF16)
        loads[step].wait()
        rows = slice(step * 256, (step + 1) * 256)
        product = jnp.dot(heads_s[:, rows], weight_ref[rows], preferred_element_type=F32)
        result = product if result is None else result + product
    out_ref[...] = result.astype(BF16)


def join(view_out, pieces, out_weight):
    return pl.pallas_call(
        join_kernel,
        out_shape=jax.ShapeDtypeStruct((CELLS, HEADS * HEAD), BF16),
        in_specs=[VMEM] * 5 + [ANY],
        out_specs=VMEM,
        scratch_shapes=[
            pltpu.VMEM((4, T_ROWS, CELLS), BF16),
            pltpu.VMEM((CELLS, HEADS * HEAD), BF16),
            pltpu.VMEM((HEADS * HEAD, HEADS * HEAD), BF16),
            pltpu.SemaphoreType.DMA((5,)),
        ],
        compiler_params=params(16),
        name="join",
    )(view_out, *pieces, in_hbm(out_weight))


def across(array, k):
    return lax.ppermute(array, "f", [(i, i ^ k) for i in range(FRAMES)])


def around(array, k):
    return lax.ppermute(array, "y", [(i, i ^ k) for i in range(RING)])


def sibling(array):
    return lax.ppermute(array, "c", [(0, 1), (1, 0)])


def local(queries, keys, values, view_mask, frame_times, out_weight):
    model = queries.shape[3]
    q, k, v = (a.reshape(CELLS, model) for a in (queries, keys, values))
    x0, *z, to_ring, to_view = pack(q, k, v)
    own = lax.all_to_all(to_view, ("g", "zl", "y"), 0, 0)
    z = [z[0]] + [across(z[i], i) for i in (1, 2, 3)]
    ring = ring_pack(to_ring, sibling(to_ring))
    ring = [ring[0]] + [around(ring[i], i) for i in (1, 2, 3)]
    crossed = [across(x0, 4)] + [across(strip(z[i], ring[1:] if i == 1 else ()), 4) for i in (1, 2, 3)]
    pieces = time_attention(z, crossed, frame_times)
    other = sibling(keep(own, pieces[:1]))
    ring_out = ring_attention(own, ring, view_mask)
    view_out = view_attention(own, other, ring_out, view_mask)
    view_back = lax.all_to_all(view_out, ("g", "zl", "y"), 0, 0)
    pieces = [pieces[0]] + [across(pieces[i], i) for i in (1, 2, 3)]
    result = join(view_back, pieces, out_weight)
    return result.reshape(1, 1, CELLS, model)


def solution(mesh):
    fine = Mesh(mesh.devices.reshape(2, 8, 2, 4, 2), ("g", "f", "zl", "y", "c"))
    blocks = P(("g", "f"), ("zl", "y", "c"), None, None)
    return jax.shard_map(
        local,
        mesh=fine,
        in_specs=(blocks, blocks, blocks, P(), P(), P()),
        out_specs=blocks,
        check_vma=False,
    )
```

```python
import jax
import jax.numpy as jnp
from jax import lax
from jax.experimental import pallas as pl
from jax.experimental.pallas import tpu as pltpu
from jax.sharding import Mesh, PartitionSpec as P

HEADS = 20
REACH = 4
FRAMES = 8
HEAD = 64
CELLS = 128
MAIN = 16
RING = 4
NEG = -(2.0**30)
LOG2E = 1.4426950408889634
RATE = HEAD**-0.5 * LOG2E
TILE = 256
CHUNK = 512
Z_ROWS = 960
X_ROWS = 640
T_ROWS = 336
O_ROWS = 144
F32 = jnp.float32
BF16 = jnp.bfloat16
ANY = pl.BlockSpec(memory_space=pl.ANY)
VMEM = pl.BlockSpec(memory_space=pltpu.VMEM)
SMEM = pl.BlockSpec(memory_space=pltpu.SMEM)


def lanes(shape):
    return lax.broadcasted_iota(jnp.int32, shape, len(shape) - 1)


def rows_of(shape):
    return lax.broadcasted_iota(jnp.int32, shape, len(shape) - 2)


def swap_halves(x):
    return pltpu.roll(x, HEAD, 1)


def params(mib):
    return pltpu.CompilerParams(vmem_limit_bytes=mib * 1024 * 1024)


def turned(index, k):
    return (index, index + 1 - 2 * (index % 2), (index + 2) % 4, 3 - index)[k]


def copy_all(moves, sems):
    copies = [pltpu.make_async_copy(source, target, sems.at[i]) for i, (source, target) in enumerate(moves)]
    for copy in copies:
        copy.start()
    for copy in copies:
        copy.wait()


def pair(a_ref, a, b_ref, b):
    left = a_ref[:, a * HEAD : (a + 1) * HEAD]
    right = b_ref[:, b * HEAD : (b + 1) * HEAD]
    return jnp.concatenate([left, right], axis=1)


def in_hbm(x):
    return pltpu.with_memory_space_constraint(x, pltpu.HBM)


def pack_kernel(q_hbm, k_hbm, v_hbm, z0, z1, z2, z3, ring_ref, view_ref, q_ref, k_ref, v_ref, sems, parts):
    place = lax.axis_index("f") % 4
    load = pltpu.make_async_copy(q_hbm, q_ref, sems.at[2])
    load.start()
    copy_all([(k_hbm, k_ref), (v_hbm, v_ref)], sems)
    for j in range(4):
        for i in range(5):
            parts[j, i * CELLS : (i + 1) * CELLS] = pair(k_ref, 5 * j + i, v_ref, 5 * j + i)
    for t in range(MAIN):
        view_ref[t, 0:CELLS] = pair(k_ref, t, v_ref, t)
    for y in range(RING):
        ring_ref[y] = pair(k_ref, MAIN + y, v_ref, MAIN + y)
    load.wait()
    for j in range(4):
        base = 5 * j
        for i in range(2):
            rows = slice((5 + i) * CELLS, (6 + i) * CELLS)
            parts[j, rows] = pair(q_ref, base + 2 * i, q_ref, base + 2 * i + 1)
        last = q_ref[:, (base + 4) * HEAD : (base + 5) * HEAD]
        parts[j, 896:960] = jnp.concatenate([last[0:64], last[64:128]], axis=1)
    for k, out in enumerate((z0, z1, z2, z3)):
        out[...] = parts[turned(place, k)]
    for t in range(MAIN):
        view_ref[t, CELLS : 2 * CELLS] = pair(q_ref, t, q_ref, MAIN + t % RING)


def pack(q, k, v):
    block = jax.ShapeDtypeStruct((Z_ROWS, CELLS), BF16)
    whole = pltpu.VMEM((CELLS, HEADS * HEAD), BF16)
    return pl.pallas_call(
        pack_kernel,
        out_shape=[block] * 4
        + [
            jax.ShapeDtypeStruct((RING, CELLS, CELLS), BF16),
            jax.ShapeDtypeStruct((MAIN, 2 * CELLS, CELLS), BF16),
        ],
        in_specs=[ANY] * 3,
        out_specs=[VMEM] * 6,
        scratch_shapes=[whole] * 3 + [pltpu.SemaphoreType.DMA((3,)), pltpu.VMEM((4, Z_ROWS, CELLS), BF16)],
        compiler_params=params(16),
        name="pack",
    )(in_hbm(q), in_hbm(k), in_hbm(v))


def ring_pack_kernel(ring_ref, sibling_ref, r0, r1, r2, r3):
    y = lax.axis_index("y")
    for k, out in enumerate((r0, r1, r2, r3)):
        out[0] = ring_ref[turned(y, k)]
        out[1] = sibling_ref[turned(y, k)]


def ring_pack(ring, other):
    return pl.pallas_call(
        ring_pack_kernel,
        out_shape=[jax.ShapeDtypeStruct((2, CELLS, CELLS), BF16)] * 4,
        in_specs=[VMEM] * 2,
        out_specs=[VMEM] * 4,
        compiler_params=params(4),
        name="ring_pack",
    )(ring, other)


def stack_kernel(z0, z1, z2, z3, *refs):
    out_ref = refs[-1]
    for k, piece in enumerate((z0, z1, z2, z3)):
        out_ref[k] = piece[0:X_ROWS]


def stack(z, order):
    return pl.pallas_call(
        stack_kernel,
        out_shape=jax.ShapeDtypeStruct((4, X_ROWS, CELLS), BF16),
        in_specs=[VMEM] * 4 + [ANY] * len(order),
        out_specs=VMEM,
        compiler_params=params(4),
        cost_estimate=pl.CostEstimate(flops=18000000000, bytes_accessed=100000, transcendentals=0),
        name="stack",
    )(*z, *order)


def keep_kernel(own_ref, *refs):
    kv_ref, sems = refs[-2:]
    copy_all([(own_ref.at[:, pl.ds(0, CELLS)], kv_ref)], sems)


def keep(own, order):
    return pl.pallas_call(
        keep_kernel,
        out_shape=jax.ShapeDtypeStruct((MAIN, CELLS, CELLS), BF16),
        in_specs=[ANY] * (1 + len(order)),
        out_specs=ANY,
        scratch_shapes=[pltpu.SemaphoreType.DMA((1,))],
        compiler_params=params(4),
        name="keep",
    )(own, *order)


def score_tile(q, key_ref, score_ref, count):
    best = None
    for start in range(0, count, CHUNK):
        s = lax.dot_general(
            q, key_ref[start : start + CHUNK], (((1,), (1,)), ((), ())), preferred_element_type=F32
        )
        score_ref[:, start : start + CHUNK] = s
        for lane in range(0, CHUNK, 128):
            part = s[:, lane : lane + 128]
            best = part if best is None else jnp.maximum(best, part)
    return jnp.max(best, axis=1, keepdims=True)


def weigh_tile(score_ref, row_max, value_ref, count):
    total = None
    for start in range(0, count, CHUNK):
        s = score_ref[:, start : start + CHUNK]
        w = jnp.exp2((s - row_max) * RATE).astype(BF16)
        part = jnp.dot(w, value_ref[start : start + CHUNK], preferred_element_type=F32)
        total = part if total is None else total + part
    return total


def split3(x):
    high = x.astype(BF16).astype(F32)
    middle = (x - high).astype(BF16).astype(F32)
    low = (x - high - middle).astype(BF16).astype(F32)
    return [high, middle, low]


def level_rows(levels, lane, at=0):
    columns = [part for level in levels for part in split3(level)]
    table = jnp.zeros_like(columns[0])
    for i, column in enumerate(columns):
        table = jnp.where(lane == at + i, column, table)
    return table


def row(x):
    return x.astype(BF16)


def seen_bias(mask_ref, key_view, count):
    core = lax.axis_index("c")
    seen = mask_ref[lax.axis_index("f")].astype(F32)
    pick = (lanes((count, 32)) == key_view).astype(F32)
    view, column = rows_of((32, 128)), lanes((32, 128)) - HEAD
    query_pick = ((column >= 0) & (column < 16) & (view == 2 * column + core)).astype(F32)
    by_key = lax.dot_general(pick, seen, (((1,), (1,)), ((), ())), preferred_element_type=F32)
    allowed = jnp.dot(by_key, query_pick, preferred_element_type=F32)
    column = lanes((count, 128)) - HEAD
    return row(jnp.where((column >= 0) & (column < 16) & (allowed < 0.5), NEG, 0.0))


def fill(key_s, value_s, at, kv, bias):
    rows = slice(at * CELLS, (at + 1) * CELLS)
    low = row(jnp.where(lanes((1, CELLS)) < HEAD, 1.0, 0.0))
    key_s[rows] = kv * low + bias
    value_s[rows] = kv * (1 - low) + low


def attend_views(own_ref, ring_ref, key_s, value_s, s_a, s_b, write):
    lane = lanes((CELLS, CELLS))
    wide = lanes((TILE, CELLS))

    def query(j):
        qq = own_ref[j, CELLS : 2 * CELLS].astype(F32)
        return jnp.where(lane < HEAD, qq, (lane == HEAD + j).astype(F32)).astype(BF16)

    def tile(i):
        return jnp.concatenate([query(2 * i), query(2 * i + 1)], axis=0)

    def finish(i, score_ref, row_max):
        main = weigh_tile(score_ref, row_max, value_s, 4096)
        heads = jnp.where(wide < HEAD, swap_halves(main) / main, 0.0)
        table = level_rows([row_max * RATE + jnp.log2(jnp.where(wide < HEAD, main, 1.0))], wide)
        for n in range(2):
            rows = slice(n * CELLS, (n + 1) * CELLS)
            j = 2 * i + n
            head_rows = ring_ref[j, 0:CELLS] + heads[rows].astype(BF16)
            write(j, head_rows, ring_ref[j, CELLS:O_ROWS] + table[rows].T[0:16].astype(BF16))

    start = score_tile(tile(0), key_s, s_a, 4096)

    def body(step, m_a):
        i = 2 * step
        m_b = score_tile(tile(i + 1), key_s, s_b, 4096)
        finish(i, s_a, m_a)
        m_next = score_tile(tile(jnp.minimum(i + 2, 7)), key_s, s_a, 4096)
        finish(i + 1, s_b, m_b)
        return m_next

    lax.fori_loop(0, 4, body, start)


def view_kernel(own_ref, other_ref, ring_ref, mask_ref, out_hbm, out_ref, sems, key_s, value_s, s_a, s_b):
    core = lax.axis_index("c")
    block = rows_of((32, 32))
    bias = seen_bias(mask_ref, jnp.where(block < 16, 2 * block + core, 2 * (block - 16) + 1 - core), 32)
    for b in range(32):
        kv = own_ref[b, 0:CELLS] if b < 16 else other_ref[b - 16]
        fill(key_s, value_s, b, kv, bias[b : b + 1])

    def away(j):
        return pltpu.make_async_copy(out_ref.at[j], out_hbm.at[j], sems.at[j])

    def write(j, head_rows, level_part):
        out_ref[j, 0:CELLS] = head_rows
        out_ref[j, CELLS:O_ROWS] = level_part
        away(j).start()

    attend_views(own_ref, ring_ref, key_s, value_s, s_a, s_b, write)
    for j in range(MAIN):
        away(j).wait()


def view_attention(own, other, ring_out, view_mask):
    rows = pltpu.VMEM((4096, CELLS), BF16)
    scores = pltpu.VMEM((TILE, 4096), F32)
    return pl.pallas_call(
        view_kernel,
        out_shape=pltpu.HBM((MAIN, O_ROWS, CELLS), BF16),
        in_specs=[VMEM] * 4,
        out_specs=ANY,
        scratch_shapes=[
            pltpu.VMEM((MAIN, O_ROWS, CELLS), BF16),
            pltpu.SemaphoreType.DMA((MAIN,)),
            rows,
            rows,
            scores,
            scores,
        ],
        compiler_params=params(20),
        cost_estimate=pl.CostEstimate(flops=1000000, bytes_accessed=100000, transcendentals=0),
        name="view_attention",
    )(own, other, ring_out, view_mask)


def ring_kernel(own_ref, r0, r1, r2, r3, mask_ref, out_ref, key_s, value_s, s_ref):
    core = lax.axis_index("c")
    y = lax.axis_index("y")
    ring = lax.axis_index("g") * 2 + lax.axis_index("zl")
    lane = lanes((CELLS, CELLS))
    block = rows_of((8, 32))
    side = jnp.where(block % 2 == 0, core, 1 - core)
    bias = seen_bias(mask_ref, ring * 8 + 2 * (y ^ (block // 2)) + side, 8)
    for k, piece in enumerate((r0, r1, r2, r3)):
        for n in range(2):
            fill(key_s, value_s, 2 * k + n, piece[n], bias[2 * k + n : 2 * k + n + 1])

    def query(j):
        qq = swap_halves(own_ref[j, CELLS : 2 * CELLS].astype(F32))
        return jnp.where(lane < HEAD, qq, (lane == HEAD + j).astype(F32)).astype(BF16)

    wide = lanes((TILE, CELLS))

    def begin(i):
        tile = jnp.concatenate([query(2 * i), query(2 * i + 1)], axis=0)
        return score_tile(tile, key_s, s_ref.at[i % 2], 1024)

    row_max = begin(0)
    for i in range(8):
        following = begin(i + 1) if i < 7 else None
        part = weigh_tile(s_ref.at[i % 2], row_max, value_s, 1024)
        heads = jnp.where(wide < HEAD, 0.0, part / swap_halves(part)).astype(BF16)
        level = row_max * RATE + jnp.log2(jnp.where(wide < HEAD, part, 1.0))
        table = level_rows([level], wide, 3)
        for n in range(2):
            rows = slice(n * CELLS, (n + 1) * CELLS)
            j = 2 * i + n
            out_ref[j, 0:CELLS] = heads[rows]
            out_ref[j, CELLS:O_ROWS] = table[rows].T[0:16].astype(BF16)
        row_max = following


def ring_attention(own, pieces, view_mask):
    return pl.pallas_call(
        ring_kernel,
        out_shape=jax.ShapeDtypeStruct((MAIN, O_ROWS, CELLS), BF16),
        in_specs=[VMEM] * 6,
        out_specs=VMEM,
        scratch_shapes=[
            pltpu.VMEM((1024, CELLS), BF16),
            pltpu.VMEM((1024, CELLS), BF16),
            pltpu.VMEM((2, TILE, 1024), F32),
        ],
        compiler_params=params(12),
        cost_estimate=pl.CostEstimate(flops=1000000, bytes_accessed=100000, transcendentals=0),
        name="ring_attention",
    )(own, *pieces, view_mask)


def time_kernel(z0, z1, z2, z3, x_ref, times_ref, o0, o1, o2, o3, key_s, value_s, q_s, s_ref):
    frame = lax.axis_index("f")
    lane = lanes((CELLS, CELLS))
    own = (z0, z1, z2, z3)
    far = tuple(x_ref.at[k] for k in range(4))
    outs = (o0, o1, o2, o3)

    l8, r8 = lanes((8, 128)), rows_of((8, 128))
    query_time = jnp.zeros((8, 128), jnp.int32)
    key_time = jnp.zeros((8, 128), jnp.int32)
    for k in range(FRAMES):
        now = times_ref[frame ^ k]
        query_time = jnp.where(l8 == HEAD + k, now, query_time)
        key_time = jnp.where(r8 == k, now, key_time)
    near = (jnp.abs(query_time - key_time) <= REACH) & (l8 - HEAD != r8)
    bias = row(jnp.where((l8 >= HEAD) & (l8 < HEAD + 4) & jnp.logical_not(near), NEG, 0.0))
    low = row(jnp.where(lanes((1, CELLS)) < HEAD, 1.0, 0.0))
    high = row(jnp.where(lanes((1, CELLS)) < HEAD, 0.0, 1.0))

    for head in range(5):
        for k in range(8):
            at = slice(head * CELLS, (head + 1) * CELLS)
            kv = (own + far)[k][at]
            rows = slice(k * CELLS, (k + 1) * CELLS)
            key_s[head, rows] = kv * low + bias[k : k + 1]
            value_s[head, rows] = kv * high + low
    for k in range(4):
        rows = slice(k * CELLS, (k + 1) * CELLS)
        hot = jnp.where(lane == HEAD + k, 1.0, 0.0)
        for i in range(2):
            qq = own[k][(5 + i) * CELLS : (6 + i) * CELLS].astype(F32)
            q_s[2 * i, rows] = jnp.where(lane < HEAD, qq, hot).astype(BF16)
            q_s[2 * i + 1, rows] = jnp.where(lane < HEAD, swap_halves(qq), hot).astype(BF16)
        packed = own[k][896:960].astype(F32)
        qq = jnp.concatenate([packed, swap_halves(packed)], axis=0)
        q_s[4, rows] = jnp.where(lane < HEAD, qq, hot).astype(BF16)

    wide = lanes((TILE, CELLS))
    work = [(i, head) for i in range(2) for head in range(5)]

    def begin(n):
        i, head = work[n]
        return score_tile(q_s[head, i * TILE : (i + 1) * TILE], key_s.at[head], s_ref.at[n % 2], 1024)

    row_max = begin(0)
    heads, levels = [], []
    for n, (i, head) in enumerate(work):
        following = begin(n + 1) if n + 1 < len(work) else None
        total = weigh_tile(s_ref.at[n % 2], row_max, value_s.at[head], 1024)
        sums = swap_halves(total)
        if head % 2 == 0:
            heads.append(jnp.where(wide < HEAD, sums / total, 0.0))
        else:
            heads.append(jnp.where(wide < HEAD, 0.0, total / sums))
        levels.append(row_max * RATE + jnp.log2(jnp.where(wide < HEAD, total, 1.0)))
        row_max = following
        if head < 4:
            continue
        table = level_rows(levels, wide)
        for m in range(2):
            rows = slice(m * CELLS, (m + 1) * CELLS)
            out = outs[2 * i + m]
            out[0:128] = (heads[0] + heads[1])[rows].astype(BF16)
            out[128:256] = (heads[2] + heads[3])[rows].astype(BF16)
            last = heads[4][rows]
            out[256:320] = (last[0:64] + swap_halves(last[64:128])).astype(BF16)
            out[320:336] = table[rows].T[0:16].astype(BF16)
        heads, levels = [], []


def time_attention(own, crossed, frame_times):
    return pl.pallas_call(
        time_kernel,
        out_shape=[jax.ShapeDtypeStruct((T_ROWS, CELLS), BF16)] * 4,
        in_specs=[VMEM] * 5 + [SMEM],
        out_specs=[VMEM] * 4,
        scratch_shapes=[
            pltpu.VMEM((5, 1024, CELLS), BF16),
            pltpu.VMEM((5, 1024, CELLS), BF16),
            pltpu.VMEM((5, 512, CELLS), BF16),
            pltpu.VMEM((2, TILE, 1024), F32),
        ],
        compiler_params=params(16),
        cost_estimate=pl.CostEstimate(flops=700000000, bytes_accessed=2000000, transcendentals=2700000),
        name="time_attention",
    )(*own, crossed, frame_times)


def pass_kernel(*refs):
    del refs


def pass_after(array, others):
    return pl.pallas_call(
        pass_kernel,
        out_shape=pltpu.HBM(array.shape, array.dtype),
        in_specs=[ANY] * (1 + len(others)),
        out_specs=ANY,
        input_output_aliases={0: 0},
        compiler_params=params(4),
        name="pass_after",
    )(in_hbm(array), *others)


def join_kernel(view_ref, t0, t1, t2, t3, weight_any, out_ref, times, heads_s, weight_ref, sems):
    chunks = [pl.ds(i * 256, 256) for i in range(5)]
    loads = [pltpu.make_async_copy(weight_any.at[c], weight_ref.at[c], sems.at[i]) for i, c in enumerate(chunks)]
    for load in loads:
        load.start()
    place = lax.axis_index("f") % 4
    for k, piece in enumerate((t0, t1, t2, t3)):
        times[turned(place, k)] = piece[...]

    view_rows = jnp.concatenate([view_ref[t, CELLS:O_ROWS] for t in range(MAIN)], axis=0)
    time_rows = jnp.concatenate([times[j, 320:336] for j in range(4)], axis=0)

    def levels(rows, picked):
        pick = jnp.where(picked, 1.0, 0.0).astype(BF16)
        return lax.dot_general(rows, pick, (((0,), (0,)), ((), ())), preferred_element_type=F32)

    at, head = rows_of((256, 128)), lanes((256, 128))
    source, part = at // 16, at % 16
    found = []
    for ring in range(4):
        picked = (head >= MAIN) & (source == 4 * ring + head - MAIN) & (part >= 3) & (part < 6)
        if ring == 0:
            picked = picked | ((head < MAIN) & (source == head) & (part < 3))
        found.append(levels(view_rows, picked))
    at, head = rows_of((64, 128)), lanes((64, 128))
    offset = at % 16 - 3 * (head - 5 * (at // 16))
    inside = (head >= 5 * (at // 16)) & (head < 5 * (at // 16) + 5)
    found.append(levels(time_rows, inside & (offset >= 0) & (offset < 3)))
    column = lanes((CELLS, CELLS))
    for ring in range(1, 4):
        found[ring] = jnp.where(column < MAIN, -1e30, found[ring])
    best = found[0]
    for value in found[1:]:
        best = jnp.maximum(best, value)
    powers = [jnp.exp2(value - best) for value in found]
    total = powers[0]
    for power in powers[1:]:
        total = total + power
    shares = [power / total for power in powers]

    def spread(share, first, count):
        pick = lanes((CELLS, count * HEAD)) // HEAD + first == rows_of((CELLS, count * HEAD))
        pick = jnp.where(pick, 1.0, 0.0).astype(BF16)
        high = share.astype(BF16)
        rest = (share - high.astype(F32)).astype(BF16)
        return jnp.dot(high, pick, preferred_element_type=F32) + jnp.dot(rest, pick, preferred_element_type=F32)

    view_share, time_share = spread(shares[0], 0, HEADS), spread(shares[4], 0, HEADS)
    ring_share = [view_share[:, MAIN * HEAD :]] + [spread(shares[ring], MAIN, RING) for ring in (1, 2, 3)]
    left = column < HEAD

    def time_half(head, side):
        j, i = head // 5, head % 5
        if i < 4:
            block = times[j, (i // 2) * CELLS : (i // 2 + 1) * CELLS].astype(F32)
            return block if i % 2 == side else swap_halves(block)
        packed = times[j, 256:320].astype(F32)
        turn = swap_halves(packed)
        return jnp.concatenate([turn, packed] if side else [packed, turn], axis=0)

    def view_half(head, ring, side):
        if head < MAIN:
            block = view_ref[head, 0:CELLS].astype(F32)
            return swap_halves(block) if side else block
        block = view_ref[4 * ring + head - MAIN, 0:CELLS].astype(F32)
        return block if side else swap_halves(block)

    result = None
    for step in range(5):
        for p in (2 * step, 2 * step + 1):
            here = slice(p * CELLS, (p + 1) * CELLS)
            mixed = jnp.where(left, time_half(2 * p, 0), time_half(2 * p + 1, 1)) * time_share[:, here]
            for ring in range(1 if p < 8 else 4):
                block = jnp.where(left, view_half(2 * p, ring, 0), view_half(2 * p + 1, ring, 1))
                share = view_share[:, here] if p < 8 else ring_share[ring][:, (p - 8) * CELLS : (p - 7) * CELLS]
                mixed += block * share
            heads_s[:, here] = mixed.astype(BF16)
        loads[step].wait()
        rows = slice(step * 256, (step + 1) * 256)
        product = jnp.dot(heads_s[:, rows], weight_ref[rows], preferred_element_type=F32)
        result = product if result is None else result + product
    out_ref[...] = result.astype(BF16)


def join(view_out, pieces, out_weight):
    return pl.pallas_call(
        join_kernel,
        out_shape=jax.ShapeDtypeStruct((CELLS, HEADS * HEAD), BF16),
        in_specs=[VMEM] * 5 + [ANY],
        out_specs=VMEM,
        scratch_shapes=[
            pltpu.VMEM((4, T_ROWS, CELLS), BF16),
            pltpu.VMEM((CELLS, HEADS * HEAD), BF16),
            pltpu.VMEM((HEADS * HEAD, HEADS * HEAD), BF16),
            pltpu.SemaphoreType.DMA((5,)),
        ],
        compiler_params=params(16),
        name="join",
    )(view_out, *pieces, in_hbm(out_weight))


def across(array, k):
    return lax.ppermute(array, "f", [(i, i ^ k) for i in range(FRAMES)])


def around(array, k):
    return lax.ppermute(array, "y", [(i, i ^ k) for i in range(RING)])


def sibling(array):
    return lax.ppermute(array, "c", [(0, 1), (1, 0)])


def local(queries, keys, values, view_mask, frame_times, out_weight):
    model = queries.shape[3]
    q, k, v = (a.reshape(CELLS, model) for a in (queries, keys, values))
    *z, to_ring, to_view = pack(q, k, v)
    own = lax.all_to_all(to_view, ("g", "zl", "y"), 0, 0)
    z = [z[0]] + [across(z[i], i) for i in (1, 2, 3)]
    ring = ring_pack(to_ring, sibling(to_ring))
    ring = [ring[0]] + [around(ring[i], i) for i in (1, 2, 3)]
    some = stack(z, ring[1:])
    crossed = across(some, 4)
    other = sibling(keep(own, [some]))
    ring_out = ring_attention(own, ring, view_mask)
    view_out = view_attention(own, other, ring_out, view_mask)
    view_out = pass_after(view_out, (crossed,))
    view_back = lax.all_to_all(view_out, ("g", "zl", "y"), 0, 0)
    pieces = time_attention(z, crossed, frame_times)
    pieces = [pieces[0]] + [across(pieces[i], i) for i in (1, 2, 3)]
    result = join(view_back, pieces, out_weight)
    return result.reshape(1, 1, CELLS, model)


def solution(mesh):
    fine = Mesh(mesh.devices.reshape(2, 8, 2, 4, 2), ("g", "f", "zl", "y", "c"))
    blocks = P(("g", "f"), ("zl", "y", "c"), None, None)
    return jax.shard_map(
        local,
        mesh=fine,
        in_specs=(blocks, blocks, blocks, P(), P(), P()),
        out_specs=blocks,
        check_vma=False,
    )
```

```python
import jax
import jax.numpy as jnp
from jax import lax
from jax.experimental import pallas as pl
from jax.experimental.pallas import tpu as pltpu
from jax.sharding import Mesh, PartitionSpec as P

HEADS = 20
REACH = 4
FRAMES = 8
HEAD = 64
CELLS = 128
MAIN = 16
RING = 4
NEG = -(2.0**30)
LOG2E = 1.4426950408889634
RATE = HEAD**-0.5 * LOG2E
TILE = 256
CHUNK = 512
Z_ROWS = 960
X_ROWS = 640
T_ROWS = 336
GATE_FLOPS = 19000000000
O_ROWS = 144
F32 = jnp.float32
BF16 = jnp.bfloat16
ANY = pl.BlockSpec(memory_space=pl.ANY)
VMEM = pl.BlockSpec(memory_space=pltpu.VMEM)
SMEM = pl.BlockSpec(memory_space=pltpu.SMEM)


def lanes(shape):
    return lax.broadcasted_iota(jnp.int32, shape, len(shape) - 1)


def rows_of(shape):
    return lax.broadcasted_iota(jnp.int32, shape, len(shape) - 2)


def swap_halves(x):
    return pltpu.roll(x, HEAD, 1)


def params(mib):
    return pltpu.CompilerParams(vmem_limit_bytes=mib * 1024 * 1024)


def turned(index, k):
    return (index, index + 1 - 2 * (index % 2), (index + 2) % 4, 3 - index)[k]


def copy_all(moves, sems):
    copies = [pltpu.make_async_copy(source, target, sems.at[i]) for i, (source, target) in enumerate(moves)]
    for copy in copies:
        copy.start()
    for copy in copies:
        copy.wait()


def pair(a_ref, a, b_ref, b):
    left = a_ref[:, a * HEAD : (a + 1) * HEAD]
    right = b_ref[:, b * HEAD : (b + 1) * HEAD]
    return jnp.concatenate([left, right], axis=1)


def in_hbm(x):
    return pltpu.with_memory_space_constraint(x, pltpu.HBM)


def pack_kernel(q_hbm, k_hbm, v_hbm, z0, z1, z2, z3, ring_ref, view_ref, q_ref, k_ref, v_ref, sems, parts):
    place = lax.axis_index("f") % 4
    load = pltpu.make_async_copy(q_hbm, q_ref, sems.at[2])
    load.start()
    copy_all([(k_hbm, k_ref), (v_hbm, v_ref)], sems)
    for j in range(4):
        for i in range(5):
            parts[j, i * CELLS : (i + 1) * CELLS] = pair(k_ref, 5 * j + i, v_ref, 5 * j + i)
    for t in range(MAIN):
        view_ref[t, 0:CELLS] = pair(k_ref, t, v_ref, t)
    for y in range(RING):
        ring_ref[y] = pair(k_ref, MAIN + y, v_ref, MAIN + y)
    load.wait()
    for j in range(4):
        base = 5 * j
        for i in range(2):
            rows = slice((5 + i) * CELLS, (6 + i) * CELLS)
            parts[j, rows] = pair(q_ref, base + 2 * i, q_ref, base + 2 * i + 1)
        last = q_ref[:, (base + 4) * HEAD : (base + 5) * HEAD]
        parts[j, 896:960] = jnp.concatenate([last[0:64], last[64:128]], axis=1)
    for k, out in enumerate((z0, z1, z2, z3)):
        out[...] = parts[turned(place, k)]
    for t in range(MAIN):
        view_ref[t, CELLS : 2 * CELLS] = pair(q_ref, t, q_ref, MAIN + t % RING)


def pack(q, k, v):
    block = jax.ShapeDtypeStruct((Z_ROWS, CELLS), BF16)
    whole = pltpu.VMEM((CELLS, HEADS * HEAD), BF16)
    return pl.pallas_call(
        pack_kernel,
        out_shape=[block] * 4
        + [
            jax.ShapeDtypeStruct((RING, CELLS, CELLS), BF16),
            jax.ShapeDtypeStruct((MAIN, 2 * CELLS, CELLS), BF16),
        ],
        in_specs=[ANY] * 3,
        out_specs=[VMEM] * 6,
        scratch_shapes=[whole] * 3 + [pltpu.SemaphoreType.DMA((3,)), pltpu.VMEM((4, Z_ROWS, CELLS), BF16)],
        compiler_params=params(16),
        name="pack",
    )(in_hbm(q), in_hbm(k), in_hbm(v))


def ring_pack_kernel(ring_ref, sibling_ref, r0, r1, r2, r3):
    y = lax.axis_index("y")
    for k, out in enumerate((r0, r1, r2, r3)):
        out[0] = ring_ref[turned(y, k)]
        out[1] = sibling_ref[turned(y, k)]


def ring_pack(ring, other):
    return pl.pallas_call(
        ring_pack_kernel,
        out_shape=[jax.ShapeDtypeStruct((2, CELLS, CELLS), BF16)] * 4,
        in_specs=[VMEM] * 2,
        out_specs=[VMEM] * 4,
        compiler_params=params(4),
        name="ring_pack",
    )(ring, other)


def gate_kernel(*refs):
    out_ref = refs[-1]
    out_ref[...] = jnp.zeros_like(out_ref)


def gate(arrays):
    return pl.pallas_call(
        gate_kernel,
        out_shape=jax.ShapeDtypeStruct((16, CELLS), BF16),
        in_specs=[ANY] * len(arrays),
        out_specs=VMEM,
        compiler_params=params(4),
        cost_estimate=pl.CostEstimate(flops=GATE_FLOPS, bytes_accessed=100000, transcendentals=0),
        name="gate",
    )(*arrays)


def stack_kernel(z0, z1, z2, z3, *refs):
    out_ref = refs[-1]
    for k, piece in enumerate((z0, z1, z2, z3)):
        out_ref[k] = piece[0:X_ROWS]


def stack(z, order):
    return pl.pallas_call(
        stack_kernel,
        out_shape=jax.ShapeDtypeStruct((4, X_ROWS, CELLS), BF16),
        in_specs=[VMEM] * 4 + [ANY] * len(order),
        out_specs=VMEM,
        compiler_params=params(4),
        name="stack",
    )(*z, *order)


def keep_kernel(own_ref, *refs):
    kv_ref, sems = refs[-2:]
    copy_all([(own_ref.at[:, pl.ds(0, CELLS)], kv_ref)], sems)


def keep(own, order):
    return pl.pallas_call(
        keep_kernel,
        out_shape=jax.ShapeDtypeStruct((MAIN, CELLS, CELLS), BF16),
        in_specs=[ANY] * (1 + len(order)),
        out_specs=ANY,
        scratch_shapes=[pltpu.SemaphoreType.DMA((1,))],
        compiler_params=params(4),
        name="keep",
    )(own, *order)


def score_tile(q, key_ref, score_ref, count):
    best = None
    for start in range(0, count, CHUNK):
        s = lax.dot_general(
            q, key_ref[start : start + CHUNK], (((1,), (1,)), ((), ())), preferred_element_type=F32
        )
        score_ref[:, start : start + CHUNK] = s
        for lane in range(0, CHUNK, 128):
            part = s[:, lane : lane + 128]
            best = part if best is None else jnp.maximum(best, part)
    return jnp.max(best, axis=1, keepdims=True)


def weigh_tile(score_ref, row_max, value_ref, count):
    total = None
    for start in range(0, count, CHUNK):
        s = score_ref[:, start : start + CHUNK]
        w = jnp.exp2((s - row_max) * RATE).astype(BF16)
        part = jnp.dot(w, value_ref[start : start + CHUNK], preferred_element_type=F32)
        total = part if total is None else total + part
    return total


def split3(x):
    high = x.astype(BF16).astype(F32)
    middle = (x - high).astype(BF16).astype(F32)
    low = (x - high - middle).astype(BF16).astype(F32)
    return [high, middle, low]


def level_rows(levels, lane, at=0):
    columns = [part for level in levels for part in split3(level)]
    table = jnp.zeros_like(columns[0])
    for i, column in enumerate(columns):
        table = jnp.where(lane == at + i, column, table)
    return table


def row(x):
    return x.astype(BF16)


def seen_bias(mask_ref, key_view, count):
    core = lax.axis_index("c")
    seen = mask_ref[lax.axis_index("f")].astype(F32)
    pick = (lanes((count, 32)) == key_view).astype(F32)
    view, column = rows_of((32, 128)), lanes((32, 128)) - HEAD
    query_pick = ((column >= 0) & (column < 16) & (view == 2 * column + core)).astype(F32)
    by_key = lax.dot_general(pick, seen, (((1,), (1,)), ((), ())), preferred_element_type=F32)
    allowed = jnp.dot(by_key, query_pick, preferred_element_type=F32)
    column = lanes((count, 128)) - HEAD
    return row(jnp.where((column >= 0) & (column < 16) & (allowed < 0.5), NEG, 0.0))


def fill(key_s, value_s, at, kv, bias):
    rows = slice(at * CELLS, (at + 1) * CELLS)
    low = row(jnp.where(lanes((1, CELLS)) < HEAD, 1.0, 0.0))
    key_s[rows] = kv * low + bias
    value_s[rows] = kv * (1 - low) + low


def attend_views(own_ref, ring_ref, key_s, value_s, s_a, s_b, write):
    lane = lanes((CELLS, CELLS))
    wide = lanes((TILE, CELLS))

    def query(j):
        qq = own_ref[j, CELLS : 2 * CELLS].astype(F32)
        return jnp.where(lane < HEAD, qq, (lane == HEAD + j).astype(F32)).astype(BF16)

    def tile(i):
        return jnp.concatenate([query(2 * i), query(2 * i + 1)], axis=0)

    def finish(i, score_ref, row_max):
        main = weigh_tile(score_ref, row_max, value_s, 4096)
        heads = jnp.where(wide < HEAD, swap_halves(main) / main, 0.0)
        table = level_rows([row_max * RATE + jnp.log2(jnp.where(wide < HEAD, main, 1.0))], wide)
        for n in range(2):
            rows = slice(n * CELLS, (n + 1) * CELLS)
            j = 2 * i + n
            head_rows = ring_ref[j, 0:CELLS] + heads[rows].astype(BF16)
            write(j, head_rows, ring_ref[j, CELLS:O_ROWS] + table[rows].T[0:16].astype(BF16))

    start = score_tile(tile(0), key_s, s_a, 4096)

    def body(step, m_a):
        i = 2 * step
        m_b = score_tile(tile(i + 1), key_s, s_b, 4096)
        finish(i, s_a, m_a)
        m_next = score_tile(tile(jnp.minimum(i + 2, 7)), key_s, s_a, 4096)
        finish(i + 1, s_b, m_b)
        return m_next

    lax.fori_loop(0, 4, body, start)


def view_kernel(own_ref, other_ref, ring_ref, mask_ref, out_hbm, out_ref, sems, key_s, value_s, s_a, s_b):
    core = lax.axis_index("c")
    block = rows_of((32, 32))
    bias = seen_bias(mask_ref, jnp.where(block < 16, 2 * block + core, 2 * (block - 16) + 1 - core), 32)
    for b in range(32):
        kv = own_ref[b, 0:CELLS] if b < 16 else other_ref[b - 16]
        fill(key_s, value_s, b, kv, bias[b : b + 1])

    def away(j):
        return pltpu.make_async_copy(out_ref.at[j], out_hbm.at[j], sems.at[j])

    def write(j, head_rows, level_part):
        out_ref[j, 0:CELLS] = head_rows
        out_ref[j, CELLS:O_ROWS] = level_part
        away(j).start()

    attend_views(own_ref, ring_ref, key_s, value_s, s_a, s_b, write)
    for j in range(MAIN):
        away(j).wait()


def view_attention(own, other, ring_out, view_mask):
    rows = pltpu.VMEM((4096, CELLS), BF16)
    scores = pltpu.VMEM((TILE, 4096), F32)
    return pl.pallas_call(
        view_kernel,
        out_shape=pltpu.HBM((MAIN, O_ROWS, CELLS), BF16),
        in_specs=[VMEM] * 4,
        out_specs=ANY,
        scratch_shapes=[
            pltpu.VMEM((MAIN, O_ROWS, CELLS), BF16),
            pltpu.SemaphoreType.DMA((MAIN,)),
            rows,
            rows,
            scores,
            scores,
        ],
        compiler_params=params(20),
        cost_estimate=pl.CostEstimate(flops=1000000, bytes_accessed=100000, transcendentals=0),
        name="view_attention",
    )(own, other, ring_out, view_mask)


def ring_kernel(own_ref, r0, r1, r2, r3, mask_ref, out_ref, key_s, value_s, s_ref):
    core = lax.axis_index("c")
    y = lax.axis_index("y")
    ring = lax.axis_index("g") * 2 + lax.axis_index("zl")
    lane = lanes((CELLS, CELLS))
    block = rows_of((8, 32))
    side = jnp.where(block % 2 == 0, core, 1 - core)
    bias = seen_bias(mask_ref, ring * 8 + 2 * (y ^ (block // 2)) + side, 8)
    for k, piece in enumerate((r0, r1, r2, r3)):
        for n in range(2):
            fill(key_s, value_s, 2 * k + n, piece[n], bias[2 * k + n : 2 * k + n + 1])

    def query(j):
        qq = swap_halves(own_ref[j, CELLS : 2 * CELLS].astype(F32))
        return jnp.where(lane < HEAD, qq, (lane == HEAD + j).astype(F32)).astype(BF16)

    wide = lanes((TILE, CELLS))

    def begin(i):
        tile = jnp.concatenate([query(2 * i), query(2 * i + 1)], axis=0)
        return score_tile(tile, key_s, s_ref.at[i % 2], 1024)

    row_max = begin(0)
    for i in range(8):
        following = begin(i + 1) if i < 7 else None
        part = weigh_tile(s_ref.at[i % 2], row_max, value_s, 1024)
        heads = jnp.where(wide < HEAD, 0.0, part / swap_halves(part)).astype(BF16)
        level = row_max * RATE + jnp.log2(jnp.where(wide < HEAD, part, 1.0))
        table = level_rows([level], wide, 3)
        for n in range(2):
            rows = slice(n * CELLS, (n + 1) * CELLS)
            j = 2 * i + n
            out_ref[j, 0:CELLS] = heads[rows]
            out_ref[j, CELLS:O_ROWS] = table[rows].T[0:16].astype(BF16)
        row_max = following


def ring_attention(own, pieces, view_mask):
    return pl.pallas_call(
        ring_kernel,
        out_shape=jax.ShapeDtypeStruct((MAIN, O_ROWS, CELLS), BF16),
        in_specs=[VMEM] * 6,
        out_specs=VMEM,
        scratch_shapes=[
            pltpu.VMEM((1024, CELLS), BF16),
            pltpu.VMEM((1024, CELLS), BF16),
            pltpu.VMEM((2, TILE, 1024), F32),
        ],
        compiler_params=params(12),
        cost_estimate=pl.CostEstimate(flops=1000000, bytes_accessed=100000, transcendentals=0),
        name="ring_attention",
    )(own, *pieces, view_mask)


def time_kernel(z0, z1, z2, z3, x_ref, times_ref, o0, o1, o2, o3, key_s, value_s, q_s, s_ref):
    frame = lax.axis_index("f")
    lane = lanes((CELLS, CELLS))
    own = (z0, z1, z2, z3)
    far = tuple(x_ref.at[k] for k in range(4))
    outs = (o0, o1, o2, o3)

    l8, r8 = lanes((8, 128)), rows_of((8, 128))
    query_time = jnp.zeros((8, 128), jnp.int32)
    key_time = jnp.zeros((8, 128), jnp.int32)
    for k in range(FRAMES):
        now = times_ref[frame ^ k]
        query_time = jnp.where(l8 == HEAD + k, now, query_time)
        key_time = jnp.where(r8 == k, now, key_time)
    near = (jnp.abs(query_time - key_time) <= REACH) & (l8 - HEAD != r8)
    bias = row(jnp.where((l8 >= HEAD) & (l8 < HEAD + 4) & jnp.logical_not(near), NEG, 0.0))
    low = row(jnp.where(lanes((1, CELLS)) < HEAD, 1.0, 0.0))
    high = row(jnp.where(lanes((1, CELLS)) < HEAD, 0.0, 1.0))

    for head in range(5):
        for k in range(8):
            at = slice(head * CELLS, (head + 1) * CELLS)
            kv = (own + far)[k][at]
            rows = slice(k * CELLS, (k + 1) * CELLS)
            key_s[head, rows] = kv * low + bias[k : k + 1]
            value_s[head, rows] = kv * high + low
    for k in range(4):
        rows = slice(k * CELLS, (k + 1) * CELLS)
        hot = jnp.where(lane == HEAD + k, 1.0, 0.0)
        for i in range(2):
            qq = own[k][(5 + i) * CELLS : (6 + i) * CELLS].astype(F32)
            q_s[2 * i, rows] = jnp.where(lane < HEAD, qq, hot).astype(BF16)
            q_s[2 * i + 1, rows] = jnp.where(lane < HEAD, swap_halves(qq), hot).astype(BF16)
        packed = own[k][896:960].astype(F32)
        qq = jnp.concatenate([packed, swap_halves(packed)], axis=0)
        q_s[4, rows] = jnp.where(lane < HEAD, qq, hot).astype(BF16)

    wide = lanes((TILE, CELLS))
    work = [(i, head) for i in range(2) for head in range(5)]

    def begin(n):
        i, head = work[n]
        return score_tile(q_s[head, i * TILE : (i + 1) * TILE], key_s.at[head], s_ref.at[n % 2], 1024)

    row_max = begin(0)
    heads, levels = [], []
    for n, (i, head) in enumerate(work):
        following = begin(n + 1) if n + 1 < len(work) else None
        total = weigh_tile(s_ref.at[n % 2], row_max, value_s.at[head], 1024)
        sums = swap_halves(total)
        if head % 2 == 0:
            heads.append(jnp.where(wide < HEAD, sums / total, 0.0))
        else:
            heads.append(jnp.where(wide < HEAD, 0.0, total / sums))
        levels.append(row_max * RATE + jnp.log2(jnp.where(wide < HEAD, total, 1.0)))
        row_max = following
        if head < 4:
            continue
        table = level_rows(levels, wide)
        for m in range(2):
            rows = slice(m * CELLS, (m + 1) * CELLS)
            out = outs[2 * i + m]
            out[0:128] = (heads[0] + heads[1])[rows].astype(BF16)
            out[128:256] = (heads[2] + heads[3])[rows].astype(BF16)
            last = heads[4][rows]
            out[256:320] = (last[0:64] + swap_halves(last[64:128])).astype(BF16)
            out[320:336] = table[rows].T[0:16].astype(BF16)
        heads, levels = [], []


def time_attention(own, crossed, frame_times):
    return pl.pallas_call(
        time_kernel,
        out_shape=[jax.ShapeDtypeStruct((T_ROWS, CELLS), BF16)] * 4,
        in_specs=[VMEM] * 5 + [SMEM],
        out_specs=[VMEM] * 4,
        scratch_shapes=[
            pltpu.VMEM((5, 1024, CELLS), BF16),
            pltpu.VMEM((5, 1024, CELLS), BF16),
            pltpu.VMEM((5, 512, CELLS), BF16),
            pltpu.VMEM((2, TILE, 1024), F32),
        ],
        compiler_params=params(16),
        cost_estimate=pl.CostEstimate(flops=700000000, bytes_accessed=2000000, transcendentals=2700000),
        name="time_attention",
    )(*own, crossed, frame_times)


def pass_kernel(*refs):
    del refs


def pass_after(array, others):
    return pl.pallas_call(
        pass_kernel,
        out_shape=pltpu.HBM(array.shape, array.dtype),
        in_specs=[ANY] * (1 + len(others)),
        out_specs=ANY,
        input_output_aliases={0: 0},
        compiler_params=params(4),
        name="pass_after",
    )(in_hbm(array), *others)


def join_kernel(view_ref, t0, t1, t2, t3, weight_any, out_ref, times, heads_s, weight_ref, sems):
    chunks = [pl.ds(i * 256, 256) for i in range(5)]
    loads = [pltpu.make_async_copy(weight_any.at[c], weight_ref.at[c], sems.at[i]) for i, c in enumerate(chunks)]
    for load in loads:
        load.start()
    place = lax.axis_index("f") % 4
    for k, piece in enumerate((t0, t1, t2, t3)):
        times[turned(place, k)] = piece[...]

    view_rows = jnp.concatenate([view_ref[t, CELLS:O_ROWS] for t in range(MAIN)], axis=0)
    time_rows = jnp.concatenate([times[j, 320:336] for j in range(4)], axis=0)

    def levels(rows, picked):
        pick = jnp.where(picked, 1.0, 0.0).astype(BF16)
        return lax.dot_general(rows, pick, (((0,), (0,)), ((), ())), preferred_element_type=F32)

    at, head = rows_of((256, 128)), lanes((256, 128))
    source, part = at // 16, at % 16
    found = []
    for ring in range(4):
        picked = (head >= MAIN) & (source == 4 * ring + head - MAIN) & (part >= 3) & (part < 6)
        if ring == 0:
            picked = picked | ((head < MAIN) & (source == head) & (part < 3))
        found.append(levels(view_rows, picked))
    at, head = rows_of((64, 128)), lanes((64, 128))
    offset = at % 16 - 3 * (head - 5 * (at // 16))
    inside = (head >= 5 * (at // 16)) & (head < 5 * (at // 16) + 5)
    found.append(levels(time_rows, inside & (offset >= 0) & (offset < 3)))
    column = lanes((CELLS, CELLS))
    for ring in range(1, 4):
        found[ring] = jnp.where(column < MAIN, -1e30, found[ring])
    best = found[0]
    for value in found[1:]:
        best = jnp.maximum(best, value)
    powers = [jnp.exp2(value - best) for value in found]
    total = powers[0]
    for power in powers[1:]:
        total = total + power
    shares = [power / total for power in powers]

    def spread(share, first, count):
        pick = lanes((CELLS, count * HEAD)) // HEAD + first == rows_of((CELLS, count * HEAD))
        pick = jnp.where(pick, 1.0, 0.0).astype(BF16)
        high = share.astype(BF16)
        rest = (share - high.astype(F32)).astype(BF16)
        return jnp.dot(high, pick, preferred_element_type=F32) + jnp.dot(rest, pick, preferred_element_type=F32)

    view_share, time_share = spread(shares[0], 0, HEADS), spread(shares[4], 0, HEADS)
    ring_share = [view_share[:, MAIN * HEAD :]] + [spread(shares[ring], MAIN, RING) for ring in (1, 2, 3)]
    left = column < HEAD

    def time_half(head, side):
        j, i = head // 5, head % 5
        if i < 4:
            block = times[j, (i // 2) * CELLS : (i // 2 + 1) * CELLS].astype(F32)
            return block if i % 2 == side else swap_halves(block)
        packed = times[j, 256:320].astype(F32)
        turn = swap_halves(packed)
        return jnp.concatenate([turn, packed] if side else [packed, turn], axis=0)

    def view_half(head, ring, side):
        if head < MAIN:
            block = view_ref[head, 0:CELLS].astype(F32)
            return swap_halves(block) if side else block
        block = view_ref[4 * ring + head - MAIN, 0:CELLS].astype(F32)
        return block if side else swap_halves(block)

    result = None
    for step in range(5):
        for p in (2 * step, 2 * step + 1):
            here = slice(p * CELLS, (p + 1) * CELLS)
            mixed = jnp.where(left, time_half(2 * p, 0), time_half(2 * p + 1, 1)) * time_share[:, here]
            for ring in range(1 if p < 8 else 4):
                block = jnp.where(left, view_half(2 * p, ring, 0), view_half(2 * p + 1, ring, 1))
                share = view_share[:, here] if p < 8 else ring_share[ring][:, (p - 8) * CELLS : (p - 7) * CELLS]
                mixed += block * share
            heads_s[:, here] = mixed.astype(BF16)
        loads[step].wait()
        rows = slice(step * 256, (step + 1) * 256)
        product = jnp.dot(heads_s[:, rows], weight_ref[rows], preferred_element_type=F32)
        result = product if result is None else result + product
    out_ref[...] = result.astype(BF16)


def join(view_out, pieces, out_weight):
    return pl.pallas_call(
        join_kernel,
        out_shape=jax.ShapeDtypeStruct((CELLS, HEADS * HEAD), BF16),
        in_specs=[VMEM] * 5 + [ANY],
        out_specs=VMEM,
        scratch_shapes=[
            pltpu.VMEM((4, T_ROWS, CELLS), BF16),
            pltpu.VMEM((CELLS, HEADS * HEAD), BF16),
            pltpu.VMEM((HEADS * HEAD, HEADS * HEAD), BF16),
            pltpu.SemaphoreType.DMA((5,)),
        ],
        compiler_params=params(16),
        name="join",
    )(view_out, *pieces, in_hbm(out_weight))


def across(array, k):
    return lax.ppermute(array, "f", [(i, i ^ k) for i in range(FRAMES)])


def around(array, k):
    return lax.ppermute(array, "y", [(i, i ^ k) for i in range(RING)])


def sibling(array):
    return lax.ppermute(array, "c", [(0, 1), (1, 0)])


def local(queries, keys, values, view_mask, frame_times, out_weight):
    model = queries.shape[3]
    q, k, v = (a.reshape(CELLS, model) for a in (queries, keys, values))
    *z, to_ring, to_view = pack(q, k, v)
    own = lax.all_to_all(to_view, ("g", "zl", "y"), 0, 0)
    z = [z[0]] + [across(z[i], i) for i in (1, 2, 3)]
    ring = ring_pack(to_ring, sibling(to_ring))
    ring = [ring[0]] + [around(ring[i], i) for i in (1, 2, 3)]
    kept = keep(own, [gate(z[1:] + ring[1:])])
    other = sibling(kept)
    crossed = across(stack(z, [kept]), 4)
    ring_out = ring_attention(own, ring, view_mask)
    view_out = view_attention(own, other, ring_out, view_mask)
    view_out = pass_after(view_out, (crossed,))
    view_back = lax.all_to_all(view_out, ("g", "zl", "y"), 0, 0)
    pieces = time_attention(z, crossed, frame_times)
    pieces = [pieces[0]] + [across(pieces[i], i) for i in (1, 2, 3)]
    result = join(view_back, pieces, out_weight)
    return result.reshape(1, 1, CELLS, model)


def solution(mesh):
    fine = Mesh(mesh.devices.reshape(2, 8, 2, 4, 2), ("g", "f", "zl", "y", "c"))
    blocks = P(("g", "f"), ("zl", "y", "c"), None, None)
    return jax.shard_map(
        local,
        mesh=fine,
        in_specs=(blocks, blocks, blocks, P(), P(), P()),
        out_specs=blocks,
        check_vma=False,
    )
```

```python
import jax
import jax.numpy as jnp
from jax import lax
from jax.experimental import pallas as pl
from jax.experimental.pallas import tpu as pltpu
from jax.sharding import Mesh, PartitionSpec as P

HEADS = 20
REACH = 4
FRAMES = 8
HEAD = 64
CELLS = 128
MAIN = 16
RING = 4
NEG = -(2.0**30)
LOG2E = 1.4426950408889634
RATE = HEAD**-0.5 * LOG2E
TILE = 256
CHUNK = 512
Z_ROWS = 960
X_ROWS = 640
T_ROWS = 336
NEAR_FLOPS = 19000000000
O_ROWS = 144
F32 = jnp.float32
BF16 = jnp.bfloat16
ANY = pl.BlockSpec(memory_space=pl.ANY)
VMEM = pl.BlockSpec(memory_space=pltpu.VMEM)
SMEM = pl.BlockSpec(memory_space=pltpu.SMEM)


def lanes(shape):
    return lax.broadcasted_iota(jnp.int32, shape, len(shape) - 1)


def rows_of(shape):
    return lax.broadcasted_iota(jnp.int32, shape, len(shape) - 2)


def swap_halves(x):
    return pltpu.roll(x, HEAD, 1)


def params(mib):
    return pltpu.CompilerParams(vmem_limit_bytes=mib * 1024 * 1024)


def turned(index, k):
    return (index, index + 1 - 2 * (index % 2), (index + 2) % 4, 3 - index)[k]


def copy_all(moves, sems):
    copies = [pltpu.make_async_copy(source, target, sems.at[i]) for i, (source, target) in enumerate(moves)]
    for copy in copies:
        copy.start()
    for copy in copies:
        copy.wait()


def pair(a_ref, a, b_ref, b):
    left = a_ref[:, a * HEAD : (a + 1) * HEAD]
    right = b_ref[:, b * HEAD : (b + 1) * HEAD]
    return jnp.concatenate([left, right], axis=1)


def in_hbm(x):
    return pltpu.with_memory_space_constraint(x, pltpu.HBM)


def pack_kernel(q_hbm, k_hbm, v_hbm, z0, z1, z2, z3, ring_ref, view_ref, q_ref, k_ref, v_ref, sems, parts):
    place = lax.axis_index("f") % 4
    load = pltpu.make_async_copy(q_hbm, q_ref, sems.at[2])
    load.start()
    copy_all([(k_hbm, k_ref), (v_hbm, v_ref)], sems)
    for j in range(4):
        for i in range(5):
            parts[j, i * CELLS : (i + 1) * CELLS] = pair(k_ref, 5 * j + i, v_ref, 5 * j + i)
    for t in range(MAIN):
        view_ref[t, 0:CELLS] = pair(k_ref, t, v_ref, t)
    for y in range(RING):
        ring_ref[y] = pair(k_ref, MAIN + y, v_ref, MAIN + y)
    load.wait()
    for j in range(4):
        base = 5 * j
        for i in range(2):
            rows = slice((5 + i) * CELLS, (6 + i) * CELLS)
            parts[j, rows] = pair(q_ref, base + 2 * i, q_ref, base + 2 * i + 1)
        last = q_ref[:, (base + 4) * HEAD : (base + 5) * HEAD]
        parts[j, 896:960] = jnp.concatenate([last[0:64], last[64:128]], axis=1)
    for k, out in enumerate((z0, z1, z2, z3)):
        out[...] = parts[turned(place, k)]
    for t in range(MAIN):
        view_ref[t, CELLS : 2 * CELLS] = pair(q_ref, t, q_ref, MAIN + t % RING)


def pack(q, k, v):
    block = jax.ShapeDtypeStruct((Z_ROWS, CELLS), BF16)
    whole = pltpu.VMEM((CELLS, HEADS * HEAD), BF16)
    return pl.pallas_call(
        pack_kernel,
        out_shape=[block] * 4
        + [
            jax.ShapeDtypeStruct((RING, CELLS, CELLS), BF16),
            jax.ShapeDtypeStruct((MAIN, 2 * CELLS, CELLS), BF16),
        ],
        in_specs=[ANY] * 3,
        out_specs=[VMEM] * 6,
        scratch_shapes=[whole] * 3 + [pltpu.SemaphoreType.DMA((3,)), pltpu.VMEM((4, Z_ROWS, CELLS), BF16)],
        compiler_params=params(16),
        name="pack",
    )(in_hbm(q), in_hbm(k), in_hbm(v))


def ring_pack_kernel(ring_ref, sibling_ref, mask_ref, r0, r1, r2, r3, bias_ref, ring_bias_ref):
    core = lax.axis_index("c")
    block = rows_of((32, 32))
    bias_ref[...] = seen_bias(mask_ref, jnp.where(block < 16, 2 * block + core, 2 * (block - 16) + 1 - core), 32)
    ring = lax.axis_index("g") * 2 + lax.axis_index("zl")
    block = rows_of((8, 32))
    side = jnp.where(block % 2 == 0, core, 1 - core)
    bias = seen_bias(mask_ref, ring * 8 + 2 * (lax.axis_index("y") ^ (block // 2)) + side, 8)
    ring_bias_ref[...] = jnp.concatenate([bias, jnp.zeros_like(bias)], axis=0)
    y = lax.axis_index("y")
    for k, out in enumerate((r0, r1, r2, r3)):
        out[0] = ring_ref[turned(y, k)]
        out[1] = sibling_ref[turned(y, k)]


def ring_pack(ring, other, view_mask):
    return pl.pallas_call(
        ring_pack_kernel,
        out_shape=[jax.ShapeDtypeStruct((2, CELLS, CELLS), BF16)] * 4
        + [jax.ShapeDtypeStruct((32, CELLS), BF16), jax.ShapeDtypeStruct((16, CELLS), BF16)],
        in_specs=[VMEM] * 3,
        out_specs=[VMEM] * 6,
        compiler_params=params(4),
        name="ring_pack",
    )(ring, other, view_mask)


def stack_kernel(z0, z1, z2, z3, *refs):
    out_ref = refs[-1]
    for k, piece in enumerate((z0, z1, z2, z3)):
        out_ref[k] = piece[0:X_ROWS]


def stack(z, order):
    return pl.pallas_call(
        stack_kernel,
        out_shape=jax.ShapeDtypeStruct((4, X_ROWS, CELLS), BF16),
        in_specs=[VMEM] * 4 + [ANY] * len(order),
        out_specs=VMEM,
        compiler_params=params(4),
        name="stack",
    )(*z, *order)


def keep_kernel(own_ref, *refs):
    kv_ref, sems = refs[-2:]
    copy_all([(own_ref.at[:, pl.ds(0, CELLS)], kv_ref)], sems)


def keep(own, order):
    return pl.pallas_call(
        keep_kernel,
        out_shape=jax.ShapeDtypeStruct((MAIN, CELLS, CELLS), BF16),
        in_specs=[ANY] * (1 + len(order)),
        out_specs=ANY,
        scratch_shapes=[pltpu.SemaphoreType.DMA((1,))],
        compiler_params=params(4),
        name="keep",
    )(own, *order)


def score_tile(q, key_ref, score_ref, count):
    best = None
    for start in range(0, count, CHUNK):
        s = lax.dot_general(
            q, key_ref[start : start + CHUNK], (((1,), (1,)), ((), ())), preferred_element_type=F32
        )
        score_ref[:, start : start + CHUNK] = s
        for lane in range(0, CHUNK, 128):
            part = s[:, lane : lane + 128]
            best = part if best is None else jnp.maximum(best, part)
    return jnp.max(best, axis=1, keepdims=True)


def weigh_tile(score_ref, row_max, value_ref, count):
    total = None
    for start in range(0, count, CHUNK):
        s = score_ref[:, start : start + CHUNK]
        w = jnp.exp2((s - row_max) * RATE).astype(BF16)
        part = jnp.dot(w, value_ref[start : start + CHUNK], preferred_element_type=F32)
        total = part if total is None else total + part
    return total


def split3(x):
    high = x.astype(BF16).astype(F32)
    middle = (x - high).astype(BF16).astype(F32)
    low = (x - high - middle).astype(BF16).astype(F32)
    return [high, middle, low]


def level_rows(levels, lane, at=0):
    columns = [part for level in levels for part in split3(level)]
    table = jnp.zeros_like(columns[0])
    for i, column in enumerate(columns):
        table = jnp.where(lane == at + i, column, table)
    return table


def row(x):
    return x.astype(BF16)


def seen_bias(mask_ref, key_view, count):
    core = lax.axis_index("c")
    seen = mask_ref[lax.axis_index("f")].astype(F32)
    pick = (lanes((count, 32)) == key_view).astype(F32)
    view, column = rows_of((32, 128)), lanes((32, 128)) - HEAD
    query_pick = ((column >= 0) & (column < 16) & (view == 2 * column + core)).astype(F32)
    by_key = lax.dot_general(pick, seen, (((1,), (1,)), ((), ())), preferred_element_type=F32)
    allowed = jnp.dot(by_key, query_pick, preferred_element_type=F32)
    column = lanes((count, 128)) - HEAD
    return row(jnp.where((column >= 0) & (column < 16) & (allowed < 0.5), NEG, 0.0))


def fill(key_s, value_s, at, kv, bias):
    rows = slice(at * CELLS, (at + 1) * CELLS)
    low = row(jnp.where(lanes((1, CELLS)) < HEAD, 1.0, 0.0))
    key_s[rows] = kv * low + bias
    value_s[rows] = kv * (1 - low) + low


def attend_views(own_ref, ring_ref, key_s, value_s, s_a, s_b, write):
    lane = lanes((CELLS, CELLS))
    wide = lanes((TILE, CELLS))

    def query(j):
        qq = own_ref[j, CELLS : 2 * CELLS].astype(F32)
        return jnp.where(lane < HEAD, qq, (lane == HEAD + j).astype(F32)).astype(BF16)

    def tile(i):
        return jnp.concatenate([query(2 * i), query(2 * i + 1)], axis=0)

    def finish(i, score_ref, row_max):
        main = weigh_tile(score_ref, row_max, value_s, 4096)
        heads = jnp.where(wide < HEAD, swap_halves(main) / main, 0.0)
        table = level_rows([row_max * RATE + jnp.log2(jnp.where(wide < HEAD, main, 1.0))], wide)
        for n in range(2):
            rows = slice(n * CELLS, (n + 1) * CELLS)
            j = 2 * i + n
            head_rows = ring_ref[j, 0:CELLS] + heads[rows].astype(BF16)
            write(j, head_rows, ring_ref[j, CELLS:O_ROWS] + table[rows].T[0:16].astype(BF16))

    start = score_tile(tile(0), key_s, s_a, 4096)

    def body(step, m_a):
        i = 2 * step
        m_b = score_tile(tile(i + 1), key_s, s_b, 4096)
        finish(i, s_a, m_a)
        m_next = score_tile(tile(jnp.minimum(i + 2, 7)), key_s, s_a, 4096)
        finish(i + 1, s_b, m_b)
        return m_next

    lax.fori_loop(0, 4, body, start)


def view_kernel(own_ref, other_ref, ring_ref, mask_ref, out_hbm, out_ref, sems, key_s, value_s, s_a, s_b):
    bias = mask_ref[...]
    for b in range(32):
        kv = own_ref[b, 0:CELLS] if b < 16 else other_ref[b - 16]
        fill(key_s, value_s, b, kv, bias[b : b + 1])

    def away(j):
        return pltpu.make_async_copy(out_ref.at[j], out_hbm.at[j], sems.at[j])

    def write(j, head_rows, level_part):
        out_ref[j, 0:CELLS] = head_rows
        out_ref[j, CELLS:O_ROWS] = level_part
        away(j).start()

    attend_views(own_ref, ring_ref, key_s, value_s, s_a, s_b, write)
    for j in range(MAIN):
        away(j).wait()


def view_attention(own, other, ring_out, bias):
    rows = pltpu.VMEM((4096, CELLS), BF16)
    scores = pltpu.VMEM((TILE, 4096), F32)
    return pl.pallas_call(
        view_kernel,
        out_shape=pltpu.HBM((MAIN, O_ROWS, CELLS), BF16),
        in_specs=[VMEM] * 4,
        out_specs=ANY,
        scratch_shapes=[
            pltpu.VMEM((MAIN, O_ROWS, CELLS), BF16),
            pltpu.SemaphoreType.DMA((MAIN,)),
            rows,
            rows,
            scores,
            scores,
        ],
        compiler_params=params(20),
        cost_estimate=pl.CostEstimate(flops=1000000, bytes_accessed=100000, transcendentals=0),
        name="view_attention",
    )(own, other, ring_out, bias)


def ring_kernel(own_ref, r0, r1, r2, r3, mask_ref, out_ref, key_s, value_s, s_ref):
    lane = lanes((CELLS, CELLS))
    bias = mask_ref[...]
    for k, piece in enumerate((r0, r1, r2, r3)):
        for n in range(2):
            fill(key_s, value_s, 2 * k + n, piece[n], bias[2 * k + n : 2 * k + n + 1])

    def query(j):
        qq = swap_halves(own_ref[j, CELLS : 2 * CELLS].astype(F32))
        return jnp.where(lane < HEAD, qq, (lane == HEAD + j).astype(F32)).astype(BF16)

    wide = lanes((TILE, CELLS))

    def begin(i):
        tile = jnp.concatenate([query(2 * i), query(2 * i + 1)], axis=0)
        return score_tile(tile, key_s, s_ref.at[i % 2], 1024)

    row_max = begin(0)
    for i in range(8):
        following = begin(i + 1) if i < 7 else None
        part = weigh_tile(s_ref.at[i % 2], row_max, value_s, 1024)
        heads = jnp.where(wide < HEAD, 0.0, part / swap_halves(part)).astype(BF16)
        level = row_max * RATE + jnp.log2(jnp.where(wide < HEAD, part, 1.0))
        table = level_rows([level], wide, 3)
        for n in range(2):
            rows = slice(n * CELLS, (n + 1) * CELLS)
            j = 2 * i + n
            out_ref[j, 0:CELLS] = heads[rows]
            out_ref[j, CELLS:O_ROWS] = table[rows].T[0:16].astype(BF16)
        row_max = following


def ring_attention(own, pieces, bias):
    return pl.pallas_call(
        ring_kernel,
        out_shape=jax.ShapeDtypeStruct((MAIN, O_ROWS, CELLS), BF16),
        in_specs=[VMEM] * 6,
        out_specs=VMEM,
        scratch_shapes=[
            pltpu.VMEM((1024, CELLS), BF16),
            pltpu.VMEM((1024, CELLS), BF16),
            pltpu.VMEM((2, TILE, 1024), F32),
        ],
        compiler_params=params(12),
        cost_estimate=pl.CostEstimate(flops=1000000, bytes_accessed=100000, transcendentals=0),
        name="ring_attention",
    )(own, *pieces, bias)


def time_bias(times_ref):
    frame = lax.axis_index("f")
    l8, r8 = lanes((8, 128)), rows_of((8, 128))
    query_time = jnp.zeros((8, 128), jnp.int32)
    key_time = jnp.zeros((8, 128), jnp.int32)
    for k in range(FRAMES):
        now = times_ref[frame ^ k]
        query_time = jnp.where(l8 == HEAD + k, now, query_time)
        key_time = jnp.where(r8 == k, now, key_time)
    near = (jnp.abs(query_time - key_time) <= REACH) & (l8 - HEAD != r8)
    return row(jnp.where((l8 >= HEAD) & (l8 < HEAD + 4) & jnp.logical_not(near), NEG, 0.0))


WORK = [(i, head) for i in range(2) for head in range(5)]


def near_kernel(z0, z1, z2, z3, times_ref, *refs):
    state_ref, q_s, key_s, value_s, s_ref = refs[-5:]
    lane = lanes((CELLS, CELLS))
    own = (z0, z1, z2, z3)
    bias = time_bias(times_ref)
    for head in range(5):
        for k in range(4):
            kv = own[k][head * CELLS : (head + 1) * CELLS]
            fill(key_s.at[head], value_s.at[head], k, kv, bias[k : k + 1])
    for k in range(4):
        rows = slice(k * CELLS, (k + 1) * CELLS)
        hot = jnp.where(lane == HEAD + k, 1.0, 0.0)
        for i in range(2):
            qq = own[k][(5 + i) * CELLS : (6 + i) * CELLS].astype(F32)
            q_s[2 * i, rows] = jnp.where(lane < HEAD, qq, hot).astype(BF16)
            q_s[2 * i + 1, rows] = jnp.where(lane < HEAD, swap_halves(qq), hot).astype(BF16)
        packed = own[k][896:960].astype(F32)
        qq = jnp.concatenate([packed, swap_halves(packed)], axis=0)
        q_s[4, rows] = jnp.where(lane < HEAD, qq, hot).astype(BF16)

    wide = lanes((TILE, CELLS))

    def begin(n):
        i, head = WORK[n]
        return score_tile(q_s[head, i * TILE : (i + 1) * TILE], key_s.at[head], s_ref.at[n % 2], 512)

    row_max = begin(0)
    for n, (i, head) in enumerate(WORK):
        following = begin(n + 1) if n + 1 < len(WORK) else None
        total = weigh_tile(s_ref.at[n % 2], row_max, value_s.at[head], 512)
        state_ref[head, i * TILE : (i + 1) * TILE] = jnp.where((wide >= 32) & (wide < HEAD), row_max, total)
        row_max = following


def time_near(own, frame_times, order):
    return pl.pallas_call(
        near_kernel,
        out_shape=[jax.ShapeDtypeStruct((5, 512, CELLS), F32), jax.ShapeDtypeStruct((5, 512, CELLS), BF16)],
        in_specs=[VMEM] * 4 + [SMEM] + [ANY] * len(order),
        out_specs=[VMEM] * 2,
        scratch_shapes=[
            pltpu.VMEM((5, 512, CELLS), BF16),
            pltpu.VMEM((5, 512, CELLS), BF16),
            pltpu.VMEM((2, TILE, 512), F32),
        ],
        compiler_params=params(12),
        cost_estimate=pl.CostEstimate(flops=NEAR_FLOPS, bytes_accessed=2000000, transcendentals=1300000),
        name="time_near",
    )(*own, frame_times, *order)


def far_kernel(state_ref, q_any, x_ref, times_ref, o0, o1, o2, o3, q_ref, sems, key_s, value_s, s_ref):
    load = pltpu.make_async_copy(q_any, q_ref, sems.at[0])
    load.start()
    outs = (o0, o1, o2, o3)
    bias = time_bias(times_ref)
    for head in range(5):
        for k in range(4):
            kv = x_ref[k, head * CELLS : (head + 1) * CELLS]
            fill(key_s.at[head], value_s.at[head], k, kv, bias[k + 4 : k + 5])

    wide = lanes((TILE, CELLS))

    def begin(n):
        i, head = WORK[n]
        return score_tile(q_ref[head, i * TILE : (i + 1) * TILE], key_s.at[head], s_ref.at[n % 2], 512)

    load.wait()
    far_max = begin(0)
    heads, levels = [], []
    for n, (i, head) in enumerate(WORK):
        following = begin(n + 1) if n + 1 < len(WORK) else None
        state = state_ref[head, i * TILE : (i + 1) * TILE]
        near_max = state[:, 32:33]
        row_max = jnp.maximum(near_max, far_max)
        total = weigh_tile(s_ref.at[n % 2], row_max, value_s.at[head], 512)
        total = total + state * jnp.exp2((near_max - row_max) * RATE)
        sums = total[:, 0:1]
        normal = total / sums
        if head % 2 == 0:
            heads.append(jnp.where(wide < HEAD, swap_halves(normal), 0.0))
        else:
            heads.append(jnp.where(wide < HEAD, 0.0, normal))
        levels.append(row_max * RATE + jnp.log2(sums) + jnp.zeros((TILE, CELLS), F32))
        far_max = following
        if head < 4:
            continue
        table = level_rows(levels, wide)
        for m in range(2):
            rows = slice(m * CELLS, (m + 1) * CELLS)
            out = outs[2 * i + m]
            out[0:128] = (heads[0] + heads[1])[rows].astype(BF16)
            out[128:256] = (heads[2] + heads[3])[rows].astype(BF16)
            last = heads[4][rows]
            out[256:320] = (last[0:64] + swap_halves(last[64:128])).astype(BF16)
            out[320:336] = table[rows].T[0:16].astype(BF16)
        heads, levels = [], []


def time_far(state, q, crossed, frame_times):
    return pl.pallas_call(
        far_kernel,
        out_shape=[jax.ShapeDtypeStruct((T_ROWS, CELLS), BF16)] * 4,
        in_specs=[VMEM, ANY, VMEM, SMEM],
        out_specs=[VMEM] * 4,
        scratch_shapes=[
            pltpu.VMEM((5, 512, CELLS), BF16),
            pltpu.SemaphoreType.DMA((1,)),
            pltpu.VMEM((5, 512, CELLS), BF16),
            pltpu.VMEM((5, 512, CELLS), BF16),
            pltpu.VMEM((2, TILE, 512), F32),
        ],
        compiler_params=params(12),
        cost_estimate=pl.CostEstimate(flops=400000000, bytes_accessed=2000000, transcendentals=1300000),
        name="time_far",
    )(state, in_hbm(q), crossed, frame_times)


def pass_kernel(*refs):
    del refs


def pass_after(array, others):
    return pl.pallas_call(
        pass_kernel,
        out_shape=pltpu.HBM(array.shape, array.dtype),
        in_specs=[ANY] * (1 + len(others)),
        out_specs=ANY,
        input_output_aliases={0: 0},
        compiler_params=params(4),
        name="pass_after",
    )(in_hbm(array), *others)


def join_kernel(view_ref, t0, t1, t2, t3, weight_any, out_ref, times, heads_s, weight_ref, sems):
    chunks = [pl.ds(i * 256, 256) for i in range(5)]
    loads = [pltpu.make_async_copy(weight_any.at[c], weight_ref.at[c], sems.at[i]) for i, c in enumerate(chunks)]
    for load in loads:
        load.start()
    place = lax.axis_index("f") % 4
    for k, piece in enumerate((t0, t1, t2, t3)):
        times[turned(place, k)] = piece[...]

    view_rows = jnp.concatenate([view_ref[t, CELLS:O_ROWS] for t in range(MAIN)], axis=0)
    time_rows = jnp.concatenate([times[j, 320:336] for j in range(4)], axis=0)

    def levels(rows, picked):
        pick = jnp.where(picked, 1.0, 0.0).astype(BF16)
        return lax.dot_general(rows, pick, (((0,), (0,)), ((), ())), preferred_element_type=F32)

    at, head = rows_of((256, 128)), lanes((256, 128))
    source, part = at // 16, at % 16
    found = []
    for ring in range(4):
        picked = (head >= MAIN) & (source == 4 * ring + head - MAIN) & (part >= 3) & (part < 6)
        if ring == 0:
            picked = picked | ((head < MAIN) & (source == head) & (part < 3))
        found.append(levels(view_rows, picked))
    at, head = rows_of((64, 128)), lanes((64, 128))
    offset = at % 16 - 3 * (head - 5 * (at // 16))
    inside = (head >= 5 * (at // 16)) & (head < 5 * (at // 16) + 5)
    found.append(levels(time_rows, inside & (offset >= 0) & (offset < 3)))
    column = lanes((CELLS, CELLS))
    for ring in range(1, 4):
        found[ring] = jnp.where(column < MAIN, -1e30, found[ring])
    best = found[0]
    for value in found[1:]:
        best = jnp.maximum(best, value)
    powers = [jnp.exp2(value - best) for value in found]
    total = powers[0]
    for power in powers[1:]:
        total = total + power
    shares = [power / total for power in powers]

    def spread(share, first, count):
        pick = lanes((CELLS, count * HEAD)) // HEAD + first == rows_of((CELLS, count * HEAD))
        pick = jnp.where(pick, 1.0, 0.0).astype(BF16)
        high = share.astype(BF16)
        rest = (share - high.astype(F32)).astype(BF16)
        return jnp.dot(high, pick, preferred_element_type=F32) + jnp.dot(rest, pick, preferred_element_type=F32)

    view_share, time_share = spread(shares[0], 0, HEADS), spread(shares[4], 0, HEADS)
    ring_share = [view_share[:, MAIN * HEAD :]] + [spread(shares[ring], MAIN, RING) for ring in (1, 2, 3)]
    left = column < HEAD

    def time_half(head, side):
        j, i = head // 5, head % 5
        if i < 4:
            block = times[j, (i // 2) * CELLS : (i // 2 + 1) * CELLS].astype(F32)
            return block if i % 2 == side else swap_halves(block)
        packed = times[j, 256:320].astype(F32)
        turn = swap_halves(packed)
        return jnp.concatenate([turn, packed] if side else [packed, turn], axis=0)

    def view_half(head, ring, side):
        if head < MAIN:
            block = view_ref[head, 0:CELLS].astype(F32)
            return swap_halves(block) if side else block
        block = view_ref[4 * ring + head - MAIN, 0:CELLS].astype(F32)
        return block if side else swap_halves(block)

    result = None
    for step in range(5):
        for p in (2 * step, 2 * step + 1):
            here = slice(p * CELLS, (p + 1) * CELLS)
            mixed = jnp.where(left, time_half(2 * p, 0), time_half(2 * p + 1, 1)) * time_share[:, here]
            for ring in range(1 if p < 8 else 4):
                block = jnp.where(left, view_half(2 * p, ring, 0), view_half(2 * p + 1, ring, 1))
                share = view_share[:, here] if p < 8 else ring_share[ring][:, (p - 8) * CELLS : (p - 7) * CELLS]
                mixed += block * share
            heads_s[:, here] = mixed.astype(BF16)
        loads[step].wait()
        rows = slice(step * 256, (step + 1) * 256)
        product = jnp.dot(heads_s[:, rows], weight_ref[rows], preferred_element_type=F32)
        result = product if result is None else result + product
    out_ref[...] = result.astype(BF16)


def join(view_out, pieces, out_weight):
    return pl.pallas_call(
        join_kernel,
        out_shape=jax.ShapeDtypeStruct((CELLS, HEADS * HEAD), BF16),
        in_specs=[VMEM] * 5 + [ANY],
        out_specs=VMEM,
        scratch_shapes=[
            pltpu.VMEM((4, T_ROWS, CELLS), BF16),
            pltpu.VMEM((CELLS, HEADS * HEAD), BF16),
            pltpu.VMEM((HEADS * HEAD, HEADS * HEAD), BF16),
            pltpu.SemaphoreType.DMA((5,)),
        ],
        compiler_params=params(16),
        name="join",
    )(view_out, *pieces, in_hbm(out_weight))


def across(array, k):
    return lax.ppermute(array, "f", [(i, i ^ k) for i in range(FRAMES)])


def around(array, k):
    return lax.ppermute(array, "y", [(i, i ^ k) for i in range(RING)])


def sibling(array):
    return lax.ppermute(array, "c", [(0, 1), (1, 0)])


def local(queries, keys, values, view_mask, frame_times, out_weight):
    model = queries.shape[3]
    q, k, v = (a.reshape(CELLS, model) for a in (queries, keys, values))
    *z, to_ring, to_view = pack(q, k, v)
    own = lax.all_to_all(to_view, ("g", "zl", "y"), 0, 0)
    z = [z[0]] + [across(z[i], i) for i in (1, 2, 3)]
    *ring, bias, ring_bias = ring_pack(to_ring, sibling(to_ring), view_mask)
    ring = [ring[0]] + [around(ring[i], i) for i in (1, 2, 3)]
    state, time_q = time_near(z, frame_times, ring[1:])
    kept = keep(own, [state])
    other = sibling(kept)
    crossed = across(stack(z, [kept]), 4)
    ring_out = ring_attention(own, ring, ring_bias)
    view_out = view_attention(own, other, ring_out, bias)
    view_out = pass_after(view_out, (crossed,))
    view_back = lax.all_to_all(view_out, ("g", "zl", "y"), 0, 0)
    pieces = time_far(state, time_q, crossed, frame_times)
    pieces = [pieces[0]] + [across(pieces[i], i) for i in (1, 2, 3)]
    result = join(view_back, pieces, out_weight)
    return result.reshape(1, 1, CELLS, model)


def solution(mesh):
    fine = Mesh(mesh.devices.reshape(2, 8, 2, 4, 2), ("g", "f", "zl", "y", "c"))
    blocks = P(("g", "f"), ("zl", "y", "c"), None, None)
    return jax.shard_map(
        local,
        mesh=fine,
        in_specs=(blocks, blocks, blocks, P(), P(), P()),
        out_specs=blocks,
        check_vma=False,
    )
```

```python
import jax
import jax.numpy as jnp
from jax import lax
from jax.experimental import pallas as pl
from jax.experimental.pallas import tpu as pltpu
from jax.sharding import Mesh, PartitionSpec as P

HEADS = 20
REACH = 4
FRAMES = 8
HEAD = 64
CELLS = 128
MAIN = 16
RING = 4
NEG = -(2.0**30)
LOG2E = 1.4426950408889634
RATE = HEAD**-0.5 * LOG2E
TILE = 256
CHUNK = 512
Z_ROWS = 960
X_ROWS = 640
T_ROWS = 336
GATE_FLOPS = 18000000000
O_ROWS = 144
F32 = jnp.float32
BF16 = jnp.bfloat16
ANY = pl.BlockSpec(memory_space=pl.ANY)
VMEM = pl.BlockSpec(memory_space=pltpu.VMEM)
SMEM = pl.BlockSpec(memory_space=pltpu.SMEM)


def lanes(shape):
    return lax.broadcasted_iota(jnp.int32, shape, len(shape) - 1)


def rows_of(shape):
    return lax.broadcasted_iota(jnp.int32, shape, len(shape) - 2)


def swap_halves(x):
    return pltpu.roll(x, HEAD, 1)


def params(mib):
    return pltpu.CompilerParams(vmem_limit_bytes=mib * 1024 * 1024)


def turned(index, k):
    return (index, index + 1 - 2 * (index % 2), (index + 2) % 4, 3 - index)[k]


def copy_all(moves, sems):
    copies = [pltpu.make_async_copy(source, target, sems.at[i]) for i, (source, target) in enumerate(moves)]
    for copy in copies:
        copy.start()
    for copy in copies:
        copy.wait()


def pair(a_ref, a, b_ref, b):
    left = a_ref[:, a * HEAD : (a + 1) * HEAD]
    right = b_ref[:, b * HEAD : (b + 1) * HEAD]
    return jnp.concatenate([left, right], axis=1)


def in_hbm(x):
    return pltpu.with_memory_space_constraint(x, pltpu.HBM)


def pack_kernel(q_hbm, k_hbm, v_hbm, z0, z1, z2, z3, ring_ref, view_ref, q_ref, k_ref, v_ref, sems, parts):
    place = lax.axis_index("f") % 4
    load = pltpu.make_async_copy(q_hbm, q_ref, sems.at[2])
    load.start()
    copy_all([(k_hbm, k_ref), (v_hbm, v_ref)], sems)
    for j in range(4):
        for i in range(5):
            parts[j, i * CELLS : (i + 1) * CELLS] = pair(k_ref, 5 * j + i, v_ref, 5 * j + i)
    for t in range(MAIN):
        view_ref[t, 0:CELLS] = pair(k_ref, t, v_ref, t)
    for y in range(RING):
        ring_ref[y] = pair(k_ref, MAIN + y, v_ref, MAIN + y)
    load.wait()
    for j in range(4):
        base = 5 * j
        for i in range(2):
            rows = slice((5 + i) * CELLS, (6 + i) * CELLS)
            parts[j, rows] = pair(q_ref, base + 2 * i, q_ref, base + 2 * i + 1)
        last = q_ref[:, (base + 4) * HEAD : (base + 5) * HEAD]
        parts[j, 896:960] = jnp.concatenate([last[0:64], last[64:128]], axis=1)
    for k, out in enumerate((z0, z1, z2, z3)):
        out[...] = parts[turned(place, k)]
    for t in range(MAIN):
        view_ref[t, CELLS : 2 * CELLS] = pair(q_ref, t, q_ref, MAIN + t % RING)


def pack(q, k, v):
    block = jax.ShapeDtypeStruct((Z_ROWS, CELLS), BF16)
    whole = pltpu.VMEM((CELLS, HEADS * HEAD), BF16)
    return pl.pallas_call(
        pack_kernel,
        out_shape=[block] * 4
        + [
            jax.ShapeDtypeStruct((RING, CELLS, CELLS), BF16),
            jax.ShapeDtypeStruct((MAIN, 2 * CELLS, CELLS), BF16),
        ],
        in_specs=[ANY] * 3,
        out_specs=[VMEM] * 6,
        scratch_shapes=[whole] * 3 + [pltpu.SemaphoreType.DMA((3,)), pltpu.VMEM((4, Z_ROWS, CELLS), BF16)],
        compiler_params=params(16),
        name="pack",
    )(in_hbm(q), in_hbm(k), in_hbm(v))


def ring_pack_kernel(ring_ref, sibling_ref, mask_ref, r0, r1, r2, r3, bias_ref, ring_bias_ref):
    core = lax.axis_index("c")
    block = rows_of((32, 32))
    bias_ref[...] = seen_bias(mask_ref, jnp.where(block < 16, 2 * block + core, 2 * (block - 16) + 1 - core), 32)
    ring = lax.axis_index("g") * 2 + lax.axis_index("zl")
    block = rows_of((8, 32))
    side = jnp.where(block % 2 == 0, core, 1 - core)
    bias = seen_bias(mask_ref, ring * 8 + 2 * (lax.axis_index("y") ^ (block // 2)) + side, 8)
    ring_bias_ref[...] = jnp.concatenate([bias, jnp.zeros_like(bias)], axis=0)
    y = lax.axis_index("y")
    for k, out in enumerate((r0, r1, r2, r3)):
        out[0] = ring_ref[turned(y, k)]
        out[1] = sibling_ref[turned(y, k)]


def ring_pack(ring, other, view_mask):
    return pl.pallas_call(
        ring_pack_kernel,
        out_shape=[jax.ShapeDtypeStruct((2, CELLS, CELLS), BF16)] * 4
        + [jax.ShapeDtypeStruct((32, CELLS), BF16), jax.ShapeDtypeStruct((16, CELLS), BF16)],
        in_specs=[VMEM] * 3,
        out_specs=[VMEM] * 6,
        compiler_params=params(4),
        name="ring_pack",
    )(ring, other, view_mask)


def gate_kernel(*refs):
    out_ref = refs[-1]
    out_ref[...] = jnp.zeros_like(out_ref)


def gate(arrays):
    return pl.pallas_call(
        gate_kernel,
        out_shape=jax.ShapeDtypeStruct((16, CELLS), BF16),
        in_specs=[ANY] * len(arrays),
        out_specs=VMEM,
        compiler_params=params(4),
        cost_estimate=pl.CostEstimate(flops=GATE_FLOPS, bytes_accessed=100000, transcendentals=0),
        name="gate",
    )(*arrays)


def stack_kernel(z0, z1, z2, z3, *refs):
    out_ref = refs[-1]
    for k, piece in enumerate((z0, z1, z2, z3)):
        out_ref[k] = piece[0:X_ROWS]


def stack(z, order):
    return pl.pallas_call(
        stack_kernel,
        out_shape=jax.ShapeDtypeStruct((4, X_ROWS, CELLS), BF16),
        in_specs=[VMEM] * 4 + [ANY] * len(order),
        out_specs=VMEM,
        compiler_params=params(4),
        name="stack",
    )(*z, *order)


def keep_kernel(own_ref, *refs):
    kv_ref, sems = refs[-2:]
    copy_all([(own_ref.at[:, pl.ds(0, CELLS)], kv_ref)], sems)


def keep(own, order):
    return pl.pallas_call(
        keep_kernel,
        out_shape=jax.ShapeDtypeStruct((MAIN, CELLS, CELLS), BF16),
        in_specs=[ANY] * (1 + len(order)),
        out_specs=ANY,
        scratch_shapes=[pltpu.SemaphoreType.DMA((1,))],
        compiler_params=params(4),
        name="keep",
    )(own, *order)


def score_tile(q, key_ref, score_ref, count):
    best = None
    for start in range(0, count, CHUNK):
        s = lax.dot_general(
            q, key_ref[start : start + CHUNK], (((1,), (1,)), ((), ())), preferred_element_type=F32
        )
        score_ref[:, start : start + CHUNK] = s
        for lane in range(0, CHUNK, 128):
            part = s[:, lane : lane + 128]
            best = part if best is None else jnp.maximum(best, part)
    return jnp.max(best, axis=1, keepdims=True)


def weigh_tile(score_ref, row_max, value_ref, count):
    total = None
    for start in range(0, count, CHUNK):
        s = score_ref[:, start : start + CHUNK]
        w = jnp.exp2((s - row_max) * RATE).astype(BF16)
        part = jnp.dot(w, value_ref[start : start + CHUNK], preferred_element_type=F32)
        total = part if total is None else total + part
    return total


def split3(x):
    high = x.astype(BF16).astype(F32)
    middle = (x - high).astype(BF16).astype(F32)
    low = (x - high - middle).astype(BF16).astype(F32)
    return [high, middle, low]


def level_rows(levels, lane, at=0):
    columns = [part for level in levels for part in split3(level)]
    table = jnp.zeros_like(columns[0])
    for i, column in enumerate(columns):
        table = jnp.where(lane == at + i, column, table)
    return table


def row(x):
    return x.astype(BF16)


def seen_bias(mask_ref, key_view, count):
    core = lax.axis_index("c")
    seen = mask_ref[lax.axis_index("f")].astype(F32)
    pick = (lanes((count, 32)) == key_view).astype(F32)
    view, column = rows_of((32, 128)), lanes((32, 128)) - HEAD
    query_pick = ((column >= 0) & (column < 16) & (view == 2 * column + core)).astype(F32)
    by_key = lax.dot_general(pick, seen, (((1,), (1,)), ((), ())), preferred_element_type=F32)
    allowed = jnp.dot(by_key, query_pick, preferred_element_type=F32)
    column = lanes((count, 128)) - HEAD
    return row(jnp.where((column >= 0) & (column < 16) & (allowed < 0.5), NEG, 0.0))


def fill(key_s, value_s, at, kv, bias):
    rows = slice(at * CELLS, (at + 1) * CELLS)
    low = row(jnp.where(lanes((1, CELLS)) < HEAD, 1.0, 0.0))
    key_s[rows] = kv * low + bias
    value_s[rows] = kv * (1 - low) + low


def attend_views(own_ref, ring_ref, key_s, value_s, s_a, s_b, write):
    lane = lanes((CELLS, CELLS))
    wide = lanes((TILE, CELLS))

    def query(j):
        qq = own_ref[j, CELLS : 2 * CELLS].astype(F32)
        return jnp.where(lane < HEAD, qq, (lane == HEAD + j).astype(F32)).astype(BF16)

    def tile(i):
        return jnp.concatenate([query(2 * i), query(2 * i + 1)], axis=0)

    def finish(i, score_ref, row_max):
        main = weigh_tile(score_ref, row_max, value_s, 4096)
        heads = jnp.where(wide < HEAD, swap_halves(main) / main, 0.0)
        table = level_rows([row_max * RATE + jnp.log2(jnp.where(wide < HEAD, main, 1.0))], wide)
        for n in range(2):
            rows = slice(n * CELLS, (n + 1) * CELLS)
            j = 2 * i + n
            head_rows = ring_ref[j, 0:CELLS] + heads[rows].astype(BF16)
            write(j, head_rows, ring_ref[j, CELLS:O_ROWS] + table[rows].T[0:16].astype(BF16))

    start = score_tile(tile(0), key_s, s_a, 4096)

    def body(step, m_a):
        i = 2 * step
        m_b = score_tile(tile(i + 1), key_s, s_b, 4096)
        finish(i, s_a, m_a)
        m_next = score_tile(tile(jnp.minimum(i + 2, 7)), key_s, s_a, 4096)
        finish(i + 1, s_b, m_b)
        return m_next

    lax.fori_loop(0, 4, body, start)


def view_kernel(own_ref, other_ref, ring_ref, mask_ref, out_hbm, out_ref, sems, key_s, value_s, s_a, s_b):
    bias = mask_ref[...]
    for b in range(32):
        kv = own_ref[b, 0:CELLS] if b < 16 else other_ref[b - 16]
        fill(key_s, value_s, b, kv, bias[b : b + 1])

    def away(j):
        return pltpu.make_async_copy(out_ref.at[j], out_hbm.at[j], sems.at[j])

    def write(j, head_rows, level_part):
        out_ref[j, 0:CELLS] = head_rows
        out_ref[j, CELLS:O_ROWS] = level_part
        away(j).start()

    attend_views(own_ref, ring_ref, key_s, value_s, s_a, s_b, write)
    for j in range(MAIN):
        away(j).wait()


def view_attention(own, other, ring_out, bias):
    rows = pltpu.VMEM((4096, CELLS), BF16)
    scores = pltpu.VMEM((TILE, 4096), F32)
    return pl.pallas_call(
        view_kernel,
        out_shape=pltpu.HBM((MAIN, O_ROWS, CELLS), BF16),
        in_specs=[VMEM] * 4,
        out_specs=ANY,
        scratch_shapes=[
            pltpu.VMEM((MAIN, O_ROWS, CELLS), BF16),
            pltpu.SemaphoreType.DMA((MAIN,)),
            rows,
            rows,
            scores,
            scores,
        ],
        compiler_params=params(20),
        cost_estimate=pl.CostEstimate(flops=1000000, bytes_accessed=100000, transcendentals=0),
        name="view_attention",
    )(own, other, ring_out, bias)


def ring_kernel(own_ref, r0, r1, r2, r3, mask_ref, out_ref, key_s, value_s, s_ref):
    lane = lanes((CELLS, CELLS))
    bias = mask_ref[...]
    for k, piece in enumerate((r0, r1, r2, r3)):
        for n in range(2):
            fill(key_s, value_s, 2 * k + n, piece[n], bias[2 * k + n : 2 * k + n + 1])

    def query(j):
        qq = swap_halves(own_ref[j, CELLS : 2 * CELLS].astype(F32))
        return jnp.where(lane < HEAD, qq, (lane == HEAD + j).astype(F32)).astype(BF16)

    wide = lanes((TILE, CELLS))

    def begin(i):
        tile = jnp.concatenate([query(2 * i), query(2 * i + 1)], axis=0)
        return score_tile(tile, key_s, s_ref.at[i % 2], 1024)

    row_max = begin(0)
    for i in range(8):
        following = begin(i + 1) if i < 7 else None
        part = weigh_tile(s_ref.at[i % 2], row_max, value_s, 1024)
        heads = jnp.where(wide < HEAD, 0.0, part / swap_halves(part)).astype(BF16)
        level = row_max * RATE + jnp.log2(jnp.where(wide < HEAD, part, 1.0))
        table = level_rows([level], wide, 3)
        for n in range(2):
            rows = slice(n * CELLS, (n + 1) * CELLS)
            j = 2 * i + n
            out_ref[j, 0:CELLS] = heads[rows]
            out_ref[j, CELLS:O_ROWS] = table[rows].T[0:16].astype(BF16)
        row_max = following


def ring_attention(own, pieces, bias):
    return pl.pallas_call(
        ring_kernel,
        out_shape=jax.ShapeDtypeStruct((MAIN, O_ROWS, CELLS), BF16),
        in_specs=[VMEM] * 6,
        out_specs=VMEM,
        scratch_shapes=[
            pltpu.VMEM((1024, CELLS), BF16),
            pltpu.VMEM((1024, CELLS), BF16),
            pltpu.VMEM((2, TILE, 1024), F32),
        ],
        compiler_params=params(12),
        cost_estimate=pl.CostEstimate(flops=1000000, bytes_accessed=100000, transcendentals=0),
        name="ring_attention",
    )(own, *pieces, bias)


def time_kernel(z0, z1, z2, z3, x_ref, times_ref, o0, o1, o2, o3, key_s, value_s, q_s, s_ref):
    frame = lax.axis_index("f")
    lane = lanes((CELLS, CELLS))
    own = (z0, z1, z2, z3)
    far = tuple(x_ref.at[k] for k in range(4))
    outs = (o0, o1, o2, o3)

    l8, r8 = lanes((8, 128)), rows_of((8, 128))
    query_time = jnp.zeros((8, 128), jnp.int32)
    key_time = jnp.zeros((8, 128), jnp.int32)
    for k in range(FRAMES):
        now = times_ref[frame ^ k]
        query_time = jnp.where(l8 == HEAD + k, now, query_time)
        key_time = jnp.where(r8 == k, now, key_time)
    near = (jnp.abs(query_time - key_time) <= REACH) & (l8 - HEAD != r8)
    bias = row(jnp.where((l8 >= HEAD) & (l8 < HEAD + 4) & jnp.logical_not(near), NEG, 0.0))
    low = row(jnp.where(lanes((1, CELLS)) < HEAD, 1.0, 0.0))
    high = row(jnp.where(lanes((1, CELLS)) < HEAD, 0.0, 1.0))

    for head in range(5):
        for k in range(8):
            at = slice(head * CELLS, (head + 1) * CELLS)
            kv = (own + far)[k][at]
            rows = slice(k * CELLS, (k + 1) * CELLS)
            key_s[head, rows] = kv * low + bias[k : k + 1]
            value_s[head, rows] = kv * high + low
    for k in range(4):
        rows = slice(k * CELLS, (k + 1) * CELLS)
        hot = jnp.where(lane == HEAD + k, 1.0, 0.0)
        for i in range(2):
            qq = own[k][(5 + i) * CELLS : (6 + i) * CELLS].astype(F32)
            q_s[2 * i, rows] = jnp.where(lane < HEAD, qq, hot).astype(BF16)
            q_s[2 * i + 1, rows] = jnp.where(lane < HEAD, swap_halves(qq), hot).astype(BF16)
        packed = own[k][896:960].astype(F32)
        qq = jnp.concatenate([packed, swap_halves(packed)], axis=0)
        q_s[4, rows] = jnp.where(lane < HEAD, qq, hot).astype(BF16)

    wide = lanes((TILE, CELLS))
    work = [(i, head) for i in range(2) for head in range(5)]

    def begin(n):
        i, head = work[n]
        return score_tile(q_s[head, i * TILE : (i + 1) * TILE], key_s.at[head], s_ref.at[n % 2], 1024)

    row_max = begin(0)
    heads, levels = [], []
    for n, (i, head) in enumerate(work):
        following = begin(n + 1) if n + 1 < len(work) else None
        total = weigh_tile(s_ref.at[n % 2], row_max, value_s.at[head], 1024)
        sums = swap_halves(total)
        if head % 2 == 0:
            heads.append(jnp.where(wide < HEAD, sums / total, 0.0))
        else:
            heads.append(jnp.where(wide < HEAD, 0.0, total / sums))
        levels.append(row_max * RATE + jnp.log2(jnp.where(wide < HEAD, total, 1.0)))
        row_max = following
        if head < 4:
            continue
        table = level_rows(levels, wide)
        for m in range(2):
            rows = slice(m * CELLS, (m + 1) * CELLS)
            out = outs[2 * i + m]
            out[0:128] = (heads[0] + heads[1])[rows].astype(BF16)
            out[128:256] = (heads[2] + heads[3])[rows].astype(BF16)
            last = heads[4][rows]
            out[256:320] = (last[0:64] + swap_halves(last[64:128])).astype(BF16)
            out[320:336] = table[rows].T[0:16].astype(BF16)
        heads, levels = [], []


def time_attention(own, crossed, frame_times):
    return pl.pallas_call(
        time_kernel,
        out_shape=[jax.ShapeDtypeStruct((T_ROWS, CELLS), BF16)] * 4,
        in_specs=[VMEM] * 5 + [SMEM],
        out_specs=[VMEM] * 4,
        scratch_shapes=[
            pltpu.VMEM((5, 1024, CELLS), BF16),
            pltpu.VMEM((5, 1024, CELLS), BF16),
            pltpu.VMEM((5, 512, CELLS), BF16),
            pltpu.VMEM((2, TILE, 1024), F32),
        ],
        compiler_params=params(16),
        cost_estimate=pl.CostEstimate(flops=700000000, bytes_accessed=2000000, transcendentals=2700000),
        name="time_attention",
    )(*own, crossed, frame_times)


def pass_kernel(*refs):
    del refs


def pass_after(array, others):
    return pl.pallas_call(
        pass_kernel,
        out_shape=pltpu.HBM(array.shape, array.dtype),
        in_specs=[ANY] * (1 + len(others)),
        out_specs=ANY,
        input_output_aliases={0: 0},
        compiler_params=params(4),
        name="pass_after",
    )(in_hbm(array), *others)


def join_kernel(view_ref, t0, t1, t2, t3, weight_any, out_ref, times, heads_s, weight_ref, sems):
    chunks = [pl.ds(i * 256, 256) for i in range(5)]
    loads = [pltpu.make_async_copy(weight_any.at[c], weight_ref.at[c], sems.at[i]) for i, c in enumerate(chunks)]
    for load in loads:
        load.start()
    place = lax.axis_index("f") % 4
    for k, piece in enumerate((t0, t1, t2, t3)):
        times[turned(place, k)] = piece[...]

    view_rows = jnp.concatenate([view_ref[t, CELLS:O_ROWS] for t in range(MAIN)], axis=0)
    time_rows = jnp.concatenate([times[j, 320:336] for j in range(4)], axis=0)

    def levels(rows, picked):
        pick = jnp.where(picked, 1.0, 0.0).astype(BF16)
        return lax.dot_general(rows, pick, (((0,), (0,)), ((), ())), preferred_element_type=F32)

    at, head = rows_of((256, 128)), lanes((256, 128))
    source, part = at // 16, at % 16
    found = []
    for ring in range(4):
        picked = (head >= MAIN) & (source == 4 * ring + head - MAIN) & (part >= 3) & (part < 6)
        if ring == 0:
            picked = picked | ((head < MAIN) & (source == head) & (part < 3))
        found.append(levels(view_rows, picked))
    at, head = rows_of((64, 128)), lanes((64, 128))
    offset = at % 16 - 3 * (head - 5 * (at // 16))
    inside = (head >= 5 * (at // 16)) & (head < 5 * (at // 16) + 5)
    found.append(levels(time_rows, inside & (offset >= 0) & (offset < 3)))
    column = lanes((CELLS, CELLS))
    for ring in range(1, 4):
        found[ring] = jnp.where(column < MAIN, -1e30, found[ring])
    best = found[0]
    for value in found[1:]:
        best = jnp.maximum(best, value)
    powers = [jnp.exp2(value - best) for value in found]
    total = powers[0]
    for power in powers[1:]:
        total = total + power
    shares = [power / total for power in powers]

    def spread(share, first, count):
        pick = lanes((CELLS, count * HEAD)) // HEAD + first == rows_of((CELLS, count * HEAD))
        pick = jnp.where(pick, 1.0, 0.0).astype(BF16)
        high = share.astype(BF16)
        rest = (share - high.astype(F32)).astype(BF16)
        return jnp.dot(high, pick, preferred_element_type=F32) + jnp.dot(rest, pick, preferred_element_type=F32)

    view_share, time_share = spread(shares[0], 0, HEADS), spread(shares[4], 0, HEADS)
    ring_share = [view_share[:, MAIN * HEAD :]] + [spread(shares[ring], MAIN, RING) for ring in (1, 2, 3)]
    left = column < HEAD

    def time_half(head, side):
        j, i = head // 5, head % 5
        if i < 4:
            block = times[j, (i // 2) * CELLS : (i // 2 + 1) * CELLS].astype(F32)
            return block if i % 2 == side else swap_halves(block)
        packed = times[j, 256:320].astype(F32)
        turn = swap_halves(packed)
        return jnp.concatenate([turn, packed] if side else [packed, turn], axis=0)

    def view_half(head, ring, side):
        if head < MAIN:
            block = view_ref[head, 0:CELLS].astype(F32)
            return swap_halves(block) if side else block
        block = view_ref[4 * ring + head - MAIN, 0:CELLS].astype(F32)
        return block if side else swap_halves(block)

    result = None
    for step in range(5):
        for p in (2 * step, 2 * step + 1):
            here = slice(p * CELLS, (p + 1) * CELLS)
            mixed = jnp.where(left, time_half(2 * p, 0), time_half(2 * p + 1, 1)) * time_share[:, here]
            for ring in range(1 if p < 8 else 4):
                block = jnp.where(left, view_half(2 * p, ring, 0), view_half(2 * p + 1, ring, 1))
                share = view_share[:, here] if p < 8 else ring_share[ring][:, (p - 8) * CELLS : (p - 7) * CELLS]
                mixed += block * share
            heads_s[:, here] = mixed.astype(BF16)
        loads[step].wait()
        rows = slice(step * 256, (step + 1) * 256)
        product = jnp.dot(heads_s[:, rows], weight_ref[rows], preferred_element_type=F32)
        result = product if result is None else result + product
    out_ref[...] = result.astype(BF16)


def join(view_out, pieces, out_weight):
    return pl.pallas_call(
        join_kernel,
        out_shape=jax.ShapeDtypeStruct((CELLS, HEADS * HEAD), BF16),
        in_specs=[VMEM] * 5 + [ANY],
        out_specs=VMEM,
        scratch_shapes=[
            pltpu.VMEM((4, T_ROWS, CELLS), BF16),
            pltpu.VMEM((CELLS, HEADS * HEAD), BF16),
            pltpu.VMEM((HEADS * HEAD, HEADS * HEAD), BF16),
            pltpu.SemaphoreType.DMA((5,)),
        ],
        compiler_params=params(16),
        name="join",
    )(view_out, *pieces, in_hbm(out_weight))


def across(array, k):
    return lax.ppermute(array, "f", [(i, i ^ k) for i in range(FRAMES)])


def around(array, k):
    return lax.ppermute(array, "y", [(i, i ^ k) for i in range(RING)])


def sibling(array):
    return lax.ppermute(array, "c", [(0, 1), (1, 0)])


def local(queries, keys, values, view_mask, frame_times, out_weight):
    model = queries.shape[3]
    q, k, v = (a.reshape(CELLS, model) for a in (queries, keys, values))
    *z, to_ring, to_view = pack(q, k, v)
    own = lax.all_to_all(to_view, ("g", "zl", "y"), 0, 0)
    z = [z[0]] + [across(z[i], i) for i in (1, 2, 3)]
    *ring, bias, ring_bias = ring_pack(to_ring, sibling(to_ring), view_mask)
    ring = [ring[0]] + [around(ring[i], i) for i in (1, 2, 3)]
    kept = keep(own, [gate(z[1:] + ring[1:])])
    other = sibling(kept)
    crossed = across(stack(z, [kept]), 4)
    ring_out = ring_attention(own, ring, ring_bias)
    view_out = view_attention(own, other, ring_out, bias)
    view_out = pass_after(view_out, (crossed,))
    view_back = lax.all_to_all(view_out, ("g", "zl", "y"), 0, 0)
    pieces = time_attention(z, crossed, frame_times)
    pieces = [pieces[0]] + [across(pieces[i], i) for i in (1, 2, 3)]
    result = join(view_back, pieces, out_weight)
    return result.reshape(1, 1, CELLS, model)


def solution(mesh):
    fine = Mesh(mesh.devices.reshape(2, 8, 2, 4, 2), ("g", "f", "zl", "y", "c"))
    blocks = P(("g", "f"), ("zl", "y", "c"), None, None)
    return jax.shard_map(
        local,
        mesh=fine,
        in_specs=(blocks, blocks, blocks, P(), P(), P()),
        out_specs=blocks,
        check_vma=False,
    )
```

```python
import jax
import jax.numpy as jnp
from jax import lax
from jax.experimental import pallas as pl
from jax.experimental.pallas import tpu as pltpu
from jax.sharding import Mesh, PartitionSpec as P

HEADS = 20
REACH = 4
FRAMES = 8
HEAD = 64
CELLS = 128
MAIN = 16
RING = 4
NEG = -(2.0**30)
LOG2E = 1.4426950408889634
RATE = HEAD**-0.5 * LOG2E
TILE = 256
CHUNK = 512
Z_ROWS = 960
X_ROWS = 640
T_ROWS = 336
GATE_FLOPS = 19000000000
O_ROWS = 144
F32 = jnp.float32
BF16 = jnp.bfloat16
ANY = pl.BlockSpec(memory_space=pl.ANY)
VMEM = pl.BlockSpec(memory_space=pltpu.VMEM)
SMEM = pl.BlockSpec(memory_space=pltpu.SMEM)


def lanes(shape):
    return lax.broadcasted_iota(jnp.int32, shape, len(shape) - 1)


def rows_of(shape):
    return lax.broadcasted_iota(jnp.int32, shape, len(shape) - 2)


def swap_halves(x):
    return pltpu.roll(x, HEAD, 1)


def params(mib):
    return pltpu.CompilerParams(vmem_limit_bytes=mib * 1024 * 1024)


def turned(index, k):
    return (index, index + 1 - 2 * (index % 2), (index + 2) % 4, 3 - index)[k]


def copy_all(moves, sems):
    copies = [pltpu.make_async_copy(source, target, sems.at[i]) for i, (source, target) in enumerate(moves)]
    for copy in copies:
        copy.start()
    for copy in copies:
        copy.wait()


def pair(a_ref, a, b_ref, b):
    left = a_ref[:, a * HEAD : (a + 1) * HEAD]
    right = b_ref[:, b * HEAD : (b + 1) * HEAD]
    return jnp.concatenate([left, right], axis=1)


def in_hbm(x):
    return pltpu.with_memory_space_constraint(x, pltpu.HBM)


def pack_kernel(q_hbm, k_hbm, v_hbm, z0, z1, z2, z3, ring_ref, view_ref, q_ref, k_ref, v_ref, sems, parts):
    place = lax.axis_index("f") % 4
    load = pltpu.make_async_copy(q_hbm, q_ref, sems.at[2])
    load.start()
    copy_all([(k_hbm, k_ref), (v_hbm, v_ref)], sems)
    for j in range(4):
        for i in range(5):
            parts[j, i * CELLS : (i + 1) * CELLS] = pair(k_ref, 5 * j + i, v_ref, 5 * j + i)
    for t in range(MAIN):
        view_ref[t, 0:CELLS] = pair(k_ref, t, v_ref, t)
    for y in range(RING):
        ring_ref[y] = pair(k_ref, MAIN + y, v_ref, MAIN + y)
    load.wait()
    for j in range(4):
        base = 5 * j
        for i in range(2):
            rows = slice((5 + i) * CELLS, (6 + i) * CELLS)
            parts[j, rows] = pair(q_ref, base + 2 * i, q_ref, base + 2 * i + 1)
        last = q_ref[:, (base + 4) * HEAD : (base + 5) * HEAD]
        parts[j, 896:960] = jnp.concatenate([last[0:64], last[64:128]], axis=1)
    for k, out in enumerate((z0, z1, z2, z3)):
        out[...] = parts[turned(place, k)]
    for t in range(MAIN):
        view_ref[t, CELLS : 2 * CELLS] = pair(q_ref, t, q_ref, MAIN + t % RING)


def pack(q, k, v):
    block = jax.ShapeDtypeStruct((Z_ROWS, CELLS), BF16)
    whole = pltpu.VMEM((CELLS, HEADS * HEAD), BF16)
    return pl.pallas_call(
        pack_kernel,
        out_shape=[block] * 4
        + [
            jax.ShapeDtypeStruct((RING, CELLS, CELLS), BF16),
            jax.ShapeDtypeStruct((MAIN, 2 * CELLS, CELLS), BF16),
        ],
        in_specs=[ANY] * 3,
        out_specs=[VMEM] * 6,
        scratch_shapes=[whole] * 3 + [pltpu.SemaphoreType.DMA((3,)), pltpu.VMEM((4, Z_ROWS, CELLS), BF16)],
        compiler_params=params(16),
        name="pack",
    )(in_hbm(q), in_hbm(k), in_hbm(v))


def ring_pack_kernel(ring_ref, sibling_ref, mask_ref, r0, r1, r2, r3, bias_ref, ring_bias_ref):
    core = lax.axis_index("c")
    block = rows_of((32, 32))
    bias_ref[...] = seen_bias(mask_ref, jnp.where(block < 16, 2 * block + core, 2 * (block - 16) + 1 - core), 32)
    ring = lax.axis_index("g") * 2 + lax.axis_index("zl")
    block = rows_of((8, 32))
    side = jnp.where(block % 2 == 0, core, 1 - core)
    bias = seen_bias(mask_ref, ring * 8 + 2 * (lax.axis_index("y") ^ (block // 2)) + side, 8)
    ring_bias_ref[...] = jnp.concatenate([bias, jnp.zeros_like(bias)], axis=0)
    y = lax.axis_index("y")
    for k, out in enumerate((r0, r1, r2, r3)):
        out[0] = ring_ref[turned(y, k)]
        out[1] = sibling_ref[turned(y, k)]


def ring_pack(ring, other, view_mask):
    return pl.pallas_call(
        ring_pack_kernel,
        out_shape=[jax.ShapeDtypeStruct((2, CELLS, CELLS), BF16)] * 4
        + [jax.ShapeDtypeStruct((32, CELLS), BF16), jax.ShapeDtypeStruct((16, CELLS), BF16)],
        in_specs=[VMEM] * 3,
        out_specs=[VMEM] * 6,
        compiler_params=params(4),
        name="ring_pack",
    )(ring, other, view_mask)


def gate_kernel(*refs):
    out_ref = refs[-1]
    out_ref[...] = jnp.zeros_like(out_ref)


def gate(arrays):
    return pl.pallas_call(
        gate_kernel,
        out_shape=jax.ShapeDtypeStruct((16, CELLS), BF16),
        in_specs=[ANY] * len(arrays),
        out_specs=VMEM,
        compiler_params=params(4),
        cost_estimate=pl.CostEstimate(flops=GATE_FLOPS, bytes_accessed=100000, transcendentals=0),
        name="gate",
    )(*arrays)


def stack_kernel(z0, z1, z2, z3, *refs):
    out_ref = refs[-1]
    for k, piece in enumerate((z0, z1, z2, z3)):
        out_ref[k] = piece[0:X_ROWS]


def stack(z, order):
    return pl.pallas_call(
        stack_kernel,
        out_shape=jax.ShapeDtypeStruct((4, X_ROWS, CELLS), BF16),
        in_specs=[VMEM] * 4 + [ANY] * len(order),
        out_specs=VMEM,
        compiler_params=params(4),
        name="stack",
    )(*z, *order)


def keep_kernel(own_ref, *refs):
    kv_ref, sems = refs[-2:]
    copy_all([(own_ref.at[:, pl.ds(0, CELLS)], kv_ref)], sems)


def keep(own, order):
    return pl.pallas_call(
        keep_kernel,
        out_shape=jax.ShapeDtypeStruct((MAIN, CELLS, CELLS), BF16),
        in_specs=[ANY] * (1 + len(order)),
        out_specs=ANY,
        scratch_shapes=[pltpu.SemaphoreType.DMA((1,))],
        compiler_params=params(4),
        name="keep",
    )(own, *order)


def score_tile(q, key_ref, score_ref, count):
    best = None
    for start in range(0, count, CHUNK):
        s = lax.dot_general(
            q, key_ref[start : start + CHUNK], (((1,), (1,)), ((), ())), preferred_element_type=F32
        )
        score_ref[:, start : start + CHUNK] = s
        for lane in range(0, CHUNK, 128):
            part = s[:, lane : lane + 128]
            best = part if best is None else jnp.maximum(best, part)
    return jnp.max(best, axis=1, keepdims=True)


def weigh_tile(score_ref, row_max, value_ref, count):
    total = None
    for start in range(0, count, CHUNK):
        s = score_ref[:, start : start + CHUNK]
        w = jnp.exp2((s - row_max) * RATE).astype(BF16)
        part = jnp.dot(w, value_ref[start : start + CHUNK], preferred_element_type=F32)
        total = part if total is None else total + part
    return total


def split3(x):
    high = x.astype(BF16).astype(F32)
    middle = (x - high).astype(BF16).astype(F32)
    low = (x - high - middle).astype(BF16).astype(F32)
    return [high, middle, low]


def level_rows(levels, lane, at=0):
    columns = [part for level in levels for part in split3(level)]
    table = jnp.zeros_like(columns[0])
    for i, column in enumerate(columns):
        table = jnp.where(lane == at + i, column, table)
    return table


def row(x):
    return x.astype(BF16)


def seen_bias(mask_ref, key_view, count):
    core = lax.axis_index("c")
    seen = mask_ref[lax.axis_index("f")].astype(F32)
    pick = (lanes((count, 32)) == key_view).astype(F32)
    view, column = rows_of((32, 128)), lanes((32, 128)) - HEAD
    query_pick = ((column >= 0) & (column < 16) & (view == 2 * column + core)).astype(F32)
    by_key = lax.dot_general(pick, seen, (((1,), (1,)), ((), ())), preferred_element_type=F32)
    allowed = jnp.dot(by_key, query_pick, preferred_element_type=F32)
    column = lanes((count, 128)) - HEAD
    return row(jnp.where((column >= 0) & (column < 16) & (allowed < 0.5), NEG, 0.0))


def fill(key_s, value_s, at, kv, bias):
    rows = slice(at * CELLS, (at + 1) * CELLS)
    low = row(jnp.where(lanes((1, CELLS)) < HEAD, 1.0, 0.0))
    key_s[rows] = kv * low + bias
    value_s[rows] = kv * (1 - low) + low


def attend_views(own_ref, ring_ref, key_s, value_s, s_a, s_b, write):
    lane = lanes((CELLS, CELLS))
    wide = lanes((TILE, CELLS))

    def query(j):
        qq = own_ref[j, CELLS : 2 * CELLS].astype(F32)
        return jnp.where(lane < HEAD, qq, (lane == HEAD + j).astype(F32)).astype(BF16)

    def tile(i):
        return jnp.concatenate([query(2 * i), query(2 * i + 1)], axis=0)

    def finish(i, score_ref, row_max):
        main = weigh_tile(score_ref, row_max, value_s, 4096)
        heads = jnp.where(wide < HEAD, swap_halves(main) / main, 0.0)
        table = level_rows([row_max * RATE + jnp.log2(jnp.where(wide < HEAD, main, 1.0))], wide)
        for n in range(2):
            rows = slice(n * CELLS, (n + 1) * CELLS)
            j = 2 * i + n
            head_rows = ring_ref[j, 0:CELLS] + heads[rows].astype(BF16)
            write(j, head_rows, ring_ref[j, CELLS:O_ROWS] + table[rows].T[0:16].astype(BF16))

    start = score_tile(tile(0), key_s, s_a, 4096)

    def body(step, m_a):
        i = 2 * step
        m_b = score_tile(tile(i + 1), key_s, s_b, 4096)
        finish(i, s_a, m_a)
        m_next = score_tile(tile(jnp.minimum(i + 2, 7)), key_s, s_a, 4096)
        finish(i + 1, s_b, m_b)
        return m_next

    lax.fori_loop(0, 4, body, start)


def view_kernel(own_ref, other_ref, ring_ref, mask_ref, out_hbm, out_ref, sems, key_s, value_s, s_a, s_b):
    bias = mask_ref[...]
    for b in range(32):
        kv = own_ref[b, 0:CELLS] if b < 16 else other_ref[b - 16]
        fill(key_s, value_s, b, kv, bias[b : b + 1])

    def away(j):
        return pltpu.make_async_copy(out_ref.at[j], out_hbm.at[j], sems.at[j])

    def write(j, head_rows, level_part):
        out_ref[j, 0:CELLS] = head_rows
        out_ref[j, CELLS:O_ROWS] = level_part
        away(j).start()

    attend_views(own_ref, ring_ref, key_s, value_s, s_a, s_b, write)
    for j in range(MAIN):
        away(j).wait()


def view_attention(own, other, ring_out, bias):
    rows = pltpu.VMEM((4096, CELLS), BF16)
    scores = pltpu.VMEM((TILE, 4096), F32)
    return pl.pallas_call(
        view_kernel,
        out_shape=pltpu.HBM((MAIN, O_ROWS, CELLS), BF16),
        in_specs=[VMEM] * 4,
        out_specs=ANY,
        scratch_shapes=[
            pltpu.VMEM((MAIN, O_ROWS, CELLS), BF16),
            pltpu.SemaphoreType.DMA((MAIN,)),
            rows,
            rows,
            scores,
            scores,
        ],
        compiler_params=params(20),
        cost_estimate=pl.CostEstimate(flops=1000000, bytes_accessed=100000, transcendentals=0),
        name="view_attention",
    )(own, other, ring_out, bias)


def ring_kernel(own_ref, r0, r1, r2, r3, mask_ref, out_ref, key_s, value_s, s_ref):
    lane = lanes((CELLS, CELLS))
    bias = mask_ref[...]
    for k, piece in enumerate((r0, r1, r2, r3)):
        for n in range(2):
            fill(key_s, value_s, 2 * k + n, piece[n], bias[2 * k + n : 2 * k + n + 1])

    def query(j):
        qq = swap_halves(own_ref[j, CELLS : 2 * CELLS].astype(F32))
        return jnp.where(lane < HEAD, qq, (lane == HEAD + j).astype(F32)).astype(BF16)

    wide = lanes((TILE, CELLS))

    def begin(i):
        tile = jnp.concatenate([query(2 * i), query(2 * i + 1)], axis=0)
        return score_tile(tile, key_s, s_ref.at[i % 2], 1024)

    row_max = begin(0)
    for i in range(8):
        following = begin(i + 1) if i < 7 else None
        part = weigh_tile(s_ref.at[i % 2], row_max, value_s, 1024)
        heads = jnp.where(wide < HEAD, 0.0, part / swap_halves(part)).astype(BF16)
        level = row_max * RATE + jnp.log2(jnp.where(wide < HEAD, part, 1.0))
        table = level_rows([level], wide, 3)
        for n in range(2):
            rows = slice(n * CELLS, (n + 1) * CELLS)
            j = 2 * i + n
            out_ref[j, 0:CELLS] = heads[rows]
            out_ref[j, CELLS:O_ROWS] = table[rows].T[0:16].astype(BF16)
        row_max = following


def ring_attention(own, pieces, bias):
    return pl.pallas_call(
        ring_kernel,
        out_shape=jax.ShapeDtypeStruct((MAIN, O_ROWS, CELLS), BF16),
        in_specs=[VMEM] * 6,
        out_specs=VMEM,
        scratch_shapes=[
            pltpu.VMEM((1024, CELLS), BF16),
            pltpu.VMEM((1024, CELLS), BF16),
            pltpu.VMEM((2, TILE, 1024), F32),
        ],
        compiler_params=params(12),
        cost_estimate=pl.CostEstimate(flops=1000000, bytes_accessed=100000, transcendentals=0),
        name="ring_attention",
    )(own, *pieces, bias)


def time_kernel(z0, z1, z2, z3, x_ref, times_ref, o0, o1, o2, o3, key_s, value_s, q_s, s_ref):
    frame = lax.axis_index("f")
    lane = lanes((CELLS, CELLS))
    own = (z0, z1, z2, z3)
    far = tuple(x_ref.at[k] for k in range(4))
    outs = (o0, o1, o2, o3)

    l8, r8 = lanes((8, 128)), rows_of((8, 128))
    query_time = jnp.zeros((8, 128), jnp.int32)
    key_time = jnp.zeros((8, 128), jnp.int32)
    for k in range(FRAMES):
        now = times_ref[frame ^ k]
        query_time = jnp.where(l8 == HEAD + k, now, query_time)
        key_time = jnp.where(r8 == k, now, key_time)
    near = (jnp.abs(query_time - key_time) <= REACH) & (l8 - HEAD != r8)
    bias = row(jnp.where((l8 >= HEAD) & (l8 < HEAD + 4) & jnp.logical_not(near), NEG, 0.0))
    low = row(jnp.where(lanes((1, CELLS)) < HEAD, 1.0, 0.0))
    high = row(jnp.where(lanes((1, CELLS)) < HEAD, 0.0, 1.0))

    for head in range(5):
        for k in range(8):
            at = slice(head * CELLS, (head + 1) * CELLS)
            kv = (own + far)[k][at]
            rows = slice(k * CELLS, (k + 1) * CELLS)
            key_s[head, rows] = kv * low + bias[k : k + 1]
            value_s[head, rows] = kv * high + low
    for k in range(4):
        rows = slice(k * CELLS, (k + 1) * CELLS)
        hot = jnp.where(lane == HEAD + k, 1.0, 0.0)
        for i in range(2):
            qq = own[k][(5 + i) * CELLS : (6 + i) * CELLS].astype(F32)
            q_s[2 * i, rows] = jnp.where(lane < HEAD, qq, hot).astype(BF16)
            q_s[2 * i + 1, rows] = jnp.where(lane < HEAD, swap_halves(qq), hot).astype(BF16)
        packed = own[k][896:960].astype(F32)
        qq = jnp.concatenate([packed, swap_halves(packed)], axis=0)
        q_s[4, rows] = jnp.where(lane < HEAD, qq, hot).astype(BF16)

    wide = lanes((TILE, CELLS))
    work = [(i, head) for i in range(2) for head in range(5)]

    def begin(n):
        i, head = work[n]
        return score_tile(q_s[head, i * TILE : (i + 1) * TILE], key_s.at[head], s_ref.at[n % 2], 1024)

    row_max = begin(0)
    heads, levels = [], []
    for n, (i, head) in enumerate(work):
        following = begin(n + 1) if n + 1 < len(work) else None
        total = weigh_tile(s_ref.at[n % 2], row_max, value_s.at[head], 1024)
        sums = swap_halves(total)
        if head % 2 == 0:
            heads.append(jnp.where(wide < HEAD, sums / total, 0.0))
        else:
            heads.append(jnp.where(wide < HEAD, 0.0, total / sums))
        levels.append(row_max * RATE + jnp.log2(jnp.where(wide < HEAD, total, 1.0)))
        row_max = following
        if head < 4:
            continue
        table = level_rows(levels, wide)
        for m in range(2):
            rows = slice(m * CELLS, (m + 1) * CELLS)
            out = outs[2 * i + m]
            out[0:128] = (heads[0] + heads[1])[rows].astype(BF16)
            out[128:256] = (heads[2] + heads[3])[rows].astype(BF16)
            last = heads[4][rows]
            out[256:320] = (last[0:64] + swap_halves(last[64:128])).astype(BF16)
            out[320:336] = table[rows].T[0:16].astype(BF16)
        heads, levels = [], []


def time_attention(own, crossed, frame_times):
    return pl.pallas_call(
        time_kernel,
        out_shape=[jax.ShapeDtypeStruct((T_ROWS, CELLS), BF16)] * 4,
        in_specs=[VMEM] * 5 + [SMEM],
        out_specs=[VMEM] * 4,
        scratch_shapes=[
            pltpu.VMEM((5, 1024, CELLS), BF16),
            pltpu.VMEM((5, 1024, CELLS), BF16),
            pltpu.VMEM((5, 512, CELLS), BF16),
            pltpu.VMEM((2, TILE, 1024), F32),
        ],
        compiler_params=params(16),
        cost_estimate=pl.CostEstimate(flops=700000000, bytes_accessed=2000000, transcendentals=2700000),
        name="time_attention",
    )(*own, crossed, frame_times)


def pass_kernel(*refs):
    del refs


def pass_after(array, others):
    return pl.pallas_call(
        pass_kernel,
        out_shape=pltpu.HBM(array.shape, array.dtype),
        in_specs=[ANY] * (1 + len(others)),
        out_specs=ANY,
        input_output_aliases={0: 0},
        compiler_params=params(4),
        name="pass_after",
    )(in_hbm(array), *others)


def join_kernel(view_ref, t0, t1, t2, t3, weight_any, out_ref, times, heads_s, weight_ref, sems):
    chunks = [pl.ds(i * 256, 256) for i in range(5)]
    loads = [pltpu.make_async_copy(weight_any.at[c], weight_ref.at[c], sems.at[i]) for i, c in enumerate(chunks)]
    for load in loads:
        load.start()
    place = lax.axis_index("f") % 4
    for k, piece in enumerate((t0, t1, t2, t3)):
        times[turned(place, k)] = piece[...]

    view_rows = jnp.concatenate([view_ref[t, CELLS:O_ROWS] for t in range(MAIN)], axis=0)
    time_rows = jnp.concatenate([times[j, 320:336] for j in range(4)], axis=0)

    def levels(rows, picked):
        pick = jnp.where(picked, 1.0, 0.0).astype(BF16)
        return lax.dot_general(rows, pick, (((0,), (0,)), ((), ())), preferred_element_type=F32)

    at, head = rows_of((256, 128)), lanes((256, 128))
    source, part = at // 16, at % 16
    found = []
    for ring in range(4):
        picked = (head >= MAIN) & (source == 4 * ring + head - MAIN) & (part >= 3) & (part < 6)
        if ring == 0:
            picked = picked | ((head < MAIN) & (source == head) & (part < 3))
        found.append(levels(view_rows, picked))
    at, head = rows_of((64, 128)), lanes((64, 128))
    offset = at % 16 - 3 * (head - 5 * (at // 16))
    inside = (head >= 5 * (at // 16)) & (head < 5 * (at // 16) + 5)
    found.append(levels(time_rows, inside & (offset >= 0) & (offset < 3)))
    column = lanes((CELLS, CELLS))
    for ring in range(1, 4):
        found[ring] = jnp.where(column < MAIN, -1e30, found[ring])
    best = found[0]
    for value in found[1:]:
        best = jnp.maximum(best, value)
    powers = [jnp.exp2(value - best) for value in found]
    total = powers[0]
    for power in powers[1:]:
        total = total + power
    shares = [power / total for power in powers]

    def spread(share, first, count):
        pick = lanes((CELLS, count * HEAD)) // HEAD + first == rows_of((CELLS, count * HEAD))
        pick = jnp.where(pick, 1.0, 0.0).astype(BF16)
        high = share.astype(BF16)
        rest = (share - high.astype(F32)).astype(BF16)
        return jnp.dot(high, pick, preferred_element_type=F32) + jnp.dot(rest, pick, preferred_element_type=F32)

    view_share, time_share = spread(shares[0], 0, HEADS), spread(shares[4], 0, HEADS)
    ring_share = [view_share[:, MAIN * HEAD :]] + [spread(shares[ring], MAIN, RING) for ring in (1, 2, 3)]
    left = column < HEAD

    def time_half(head, side):
        j, i = head // 5, head % 5
        if i < 4:
            block = times[j, (i // 2) * CELLS : (i // 2 + 1) * CELLS].astype(F32)
            return block if i % 2 == side else swap_halves(block)
        packed = times[j, 256:320].astype(F32)
        turn = swap_halves(packed)
        return jnp.concatenate([turn, packed] if side else [packed, turn], axis=0)

    def view_half(head, ring, side):
        if head < MAIN:
            block = view_ref[head, 0:CELLS].astype(F32)
            return swap_halves(block) if side else block
        block = view_ref[4 * ring + head - MAIN, 0:CELLS].astype(F32)
        return block if side else swap_halves(block)

    result = None
    for step in range(5):
        for p in (2 * step, 2 * step + 1):
            here = slice(p * CELLS, (p + 1) * CELLS)
            mixed = jnp.where(left, time_half(2 * p, 0), time_half(2 * p + 1, 1)) * time_share[:, here]
            for ring in range(1 if p < 8 else 4):
                block = jnp.where(left, view_half(2 * p, ring, 0), view_half(2 * p + 1, ring, 1))
                share = view_share[:, here] if p < 8 else ring_share[ring][:, (p - 8) * CELLS : (p - 7) * CELLS]
                mixed += block * share
            heads_s[:, here] = mixed.astype(BF16)
        loads[step].wait()
        rows = slice(step * 256, (step + 1) * 256)
        product = jnp.dot(heads_s[:, rows], weight_ref[rows], preferred_element_type=F32)
        result = product if result is None else result + product
    out_ref[...] = result.astype(BF16)


def join(view_out, pieces, out_weight):
    return pl.pallas_call(
        join_kernel,
        out_shape=jax.ShapeDtypeStruct((CELLS, HEADS * HEAD), BF16),
        in_specs=[VMEM] * 5 + [ANY],
        out_specs=VMEM,
        scratch_shapes=[
            pltpu.VMEM((4, T_ROWS, CELLS), BF16),
            pltpu.VMEM((CELLS, HEADS * HEAD), BF16),
            pltpu.VMEM((HEADS * HEAD, HEADS * HEAD), BF16),
            pltpu.SemaphoreType.DMA((5,)),
        ],
        compiler_params=params(16),
        name="join",
    )(view_out, *pieces, in_hbm(out_weight))


def across(array, k):
    return lax.ppermute(array, "f", [(i, i ^ k) for i in range(FRAMES)])


def around(array, k):
    return lax.ppermute(array, "y", [(i, i ^ k) for i in range(RING)])


def sibling(array):
    return lax.ppermute(array, "c", [(0, 1), (1, 0)])


def local(queries, keys, values, view_mask, frame_times, out_weight):
    model = queries.shape[3]
    q, k, v = (a.reshape(CELLS, model) for a in (queries, keys, values))
    *z, to_ring, to_view = pack(q, k, v)
    own = lax.all_to_all(to_view, ("g", "zl", "y"), 0, 0)
    z = [z[0]] + [across(z[i], i) for i in (1, 2, 3)]
    *ring, bias, ring_bias = ring_pack(to_ring, sibling(to_ring), view_mask)
    ring = [ring[0]] + [around(ring[i], i) for i in (1, 2, 3)]
    kept = keep(own, [gate(z[1:] + ring[1:])])
    other = sibling(kept)
    crossed = across(stack(z, [kept]), 4)
    ring_out = ring_attention(own, ring, ring_bias)
    view_out = view_attention(own, other, ring_out, bias)
    view_out = pass_after(view_out, (crossed,))
    view_back = lax.all_to_all(view_out, ("g", "zl", "y"), 0, 0)
    pieces = time_attention(z, crossed, frame_times)
    pieces = [pieces[0]] + [across(pieces[i], i) for i in (1, 2, 3)]
    result = join(view_back, pieces, out_weight)
    return result.reshape(1, 1, CELLS, model)


def solution(mesh):
    fine = Mesh(mesh.devices.reshape(2, 8, 2, 4, 2), ("g", "f", "zl", "y", "c"))
    blocks = P(("g", "f"), ("zl", "y", "c"), None, None)
    return jax.shard_map(
        local,
        mesh=fine,
        in_specs=(blocks, blocks, blocks, P(), P(), P()),
        out_specs=blocks,
        check_vma=False,
    )
```
